32 devices in a mesh: dp: 8 (over y, x, core), head: 4 (over z).
Axes of the slice: x: 2, y: 2, z: 4, core: 2. Of those that a mesh axis runs over, the one named last changes fastest.
Arguments:
- images: bfloat16 [24, 96, 96, 180], P('dp', 'head'), may hold values from -6 to 6
- cotangent: bfloat16 [24, 96, 96, 180], P('dp', 'head'), may hold values from -6 to 6
- valid_size: int32 [24], P('dp'), may hold values from 48 to 96, as said below
- vectors: float32 [11, 180], replicated, may hold values from -0.8 to 1.4, as said below
- vectors_first: float32 [11, 180], replicated, may hold values from -0.0034179688 to 0.0034179688
- vectors_second: float32 [11, 180], replicated, may hold values from 2.887409e-08 to 1.1549636e-07
- qkv_weight: float32 [180, 540], replicated, may hold values from -0.4375 to 0.4375
- qkv_first: float32 [180, 540], replicated, may hold values from -0.0008544922 to 0.0008544922
- qkv_second: float32 [180, 540], replicated, may hold values from 1.8046307e-09 to 7.2185227e-09
- proj_weight: float32 [180, 180], replicated, may hold values from -1.25 to 1.25
- proj_first: float32 [180, 180], replicated, may hold values from -0.0008544922 to 0.0008544922
- proj_second: float32 [180, 180], replicated, may hold values from 1.8046307e-09 to 7.2185227e-09
- rel_table: float32 [225, 6], replicated, may hold values from -2 to 2
- rel_first: float32 [225, 6], replicated, may hold values from -0.0034179688 to 0.0034179688
- rel_second: float32 [225, 6], replicated, may hold values from 3.6092615e-10 to 1.4437046e-09
- fc1_weight: float32 [180, 360], replicated, may hold values from -0.4375 to 0.4375
- fc1_first: float32 [180, 360], replicated, may hold values from -0.0008544922 to 0.0008544922
- fc1_second: float32 [180, 360], replicated, may hold values from 1.8046307e-09 to 7.2185227e-09
- fc2_weight: float32 [360, 180], replicated, may hold values from -0.3125 to 0.3125
- fc2_first: float32 [360, 180], replicated, may hold values from -0.0008544922 to 0.0008544922
- fc2_second: float32 [360, 180], replicated, may hold values from 1.8046307e-09 to 7.2185227e-09
- conv_weight: float32 [3, 3, 180, 180], replicated, may hold values from -0.15625 to 0.15625
- conv_first: float32 [3, 3, 180, 180], replicated, may hold values from -0.0008544922 to 0.0008544922
- conv_second: float32 [3, 3, 180, 180], replicated, may hold values from 1.8046307e-09 to 7.2185227e-09
- step: int32 [1], replicated, may hold values from 2 to 20
- sr_crops: float32 [64, 3, 96, 96], P(('dp', 'head')), may hold values from 0 to 1, as said below
- hr_crops: float32 [64, 3, 96, 96], P(('dp', 'head')), may hold values from 0 to 1, as said below
- psnr_running: float32 [1], replicated, may hold values from 0 to 1000
Outputs:
- output: bfloat16 [24, 96, 96, 180], P('dp', 'head')
- image_grad: float32 [24, 96, 96, 180], P('dp', 'head')
- grad_norm: float32 [1], replicated
- psnr_total: float32 [1], replicated
- new_vectors: float32 [11, 180], replicated
- new_vectors_first: float32 [11, 180], replicated
- new_vectors_second: float32 [11, 180], replicated
- new_qkv_weight: float32 [180, 540], replicated
- new_qkv_first: float32 [180, 540], replicated
- new_qkv_second: float32 [180, 540], replicated
- new_proj_weight: float32 [180, 180], replicated
- new_proj_first: float32 [180, 180], replicated
- new_proj_second: float32 [180, 180], replicated
- new_rel_table: float32 [225, 6], replicated
- new_rel_first: float32 [225, 6], replicated
- new_rel_second: float32 [225, 6], replicated
- new_fc1_weight: float32 [180, 360], replicated
- new_fc1_first: float32 [180, 360], replicated
- new_fc1_second: float32 [180, 360], replicated
- new_fc2_weight: float32 [360, 180], replicated
- new_fc2_first: float32 [360, 180], replicated
- new_fc2_second: float32 [360, 180], replicated
- new_conv_weight: float32 [3, 3, 180, 180], replicated
- new_conv_first: float32 [3, 3, 180, 180], replicated
- new_conv_second: float32 [3, 3, 180, 180], replicated
The draws below stay inside these ranges and needn't reach their ends.
Inputs may be any that keep to these rules, and one draw needn't show every extreme that they name: `valid_size`: each image's valid side is one of 48, 64 and 96. `vectors`: rows 0 and 5 are gains near 1, the other rows biases near 0. `sr_crops`: intensities. `hr_crops`: intensities.
All inputs are finite; a program needn't handle non-finite values.
Results may differ from the reference program's by a relative error of at most 0.008.
The reference program's roundings to bfloat16 on the way count: a program that leaves them out, or rounds other values in their place, can miss the bound.
Values may be sent and summed in bfloat16 or wider, within the bound.
A program may use at most 384 MiB of HBM per device.

```python
import math
import jax
import jax.numpy as jnp
from jax import lax

C = 180
HEADS = 6
HID = 360
WIN = 8
NREL = 225
NVEC = 11
IMG = 96
NIMG = 24
CROP = 96
NCROP = 64
NPARAM = 554130


def draw_valid_size(key, part):
    picks = jax.random.randint(key, (NIMG,), 0, 3)
    chosen = jnp.where(picks == 0, IMG // 2, jnp.where(picks == 1, 2 * IMG // 3, IMG))
    return chosen.at[0].set(IMG).astype(jnp.int32)


def draw_vectors(key, part):
    noise = jnp.clip(jax.random.normal(key, (NVEC, C), jnp.float32), -4.0, 4.0)
    row_ids = jnp.arange(NVEC)[:, None]
    gain_rows = (row_ids == 0) | (row_ids == 5)
    return jnp.where(gain_rows, 1.0 + 0.1 * noise, 0.2 * noise).astype(jnp.float32)


def crop_pair(key):
    base = jax.random.fold_in(key, 71)
    shape_all = (NCROP, 3, CROP, CROP)
    reference_crop = jax.random.uniform(jax.random.fold_in(base, 1), shape_all, jnp.float32, 0.0, 1.0)
    log_spread = jax.random.uniform(jax.random.fold_in(base, 2), (NCROP, 1, 1, 1), jnp.float32, -5.8, -1.2)
    noise = jnp.clip(jax.random.normal(jax.random.fold_in(base, 3), shape_all, jnp.float32), -4.0, 4.0)
    restored = jnp.clip(reference_crop + jnp.exp(log_spread) * noise, 0.0, 1.0)
    return (restored, reference_crop)


def draw_sr_crops(key, part):
    return crop_pair(key)[0].astype(jnp.float32)


def draw_hr_crops(key, part):
    return crop_pair(key)[1].astype(jnp.float32)


def steps_of(rng, extent, cuts, least, high):
    factor_of = 1.0
    for dim, shards_of in cuts:
        draws = jax.random.uniform(jax.random.fold_in(jax.random.fold_in(rng, 6), dim), (shards_of,), jnp.float32, least / len(cuts), high / len(cuts))
        factor_of = factor_of * jnp.repeat(jnp.exp(draws), extent[dim] // shards_of).reshape((-1,) + (1,) * (len(extent) - 1 - dim))
    return factor_of


def normal_values(key, shape, spread, most, shards=(), kind=jnp.bfloat16):
    drawn = jax.random.normal(key, shape, jnp.float32) * spread
    if len(shards) > 0:
        drawn = steps_of(key, shape, shards, -0.22, 0.18) * drawn
    return jnp.clip(drawn, min=-most, max=most).astype(kind)


def setup_inputs(seed: int = 0) -> dict:
    splits = jax.random.split(jax.random.key(seed), 29)
    return {
        "images": normal_values(splits[0], (NIMG, IMG, IMG, C), 1.0, 6.0, ((0, 8), (1, 4))),
        "cotangent": normal_values(splits[1], (NIMG, IMG, IMG, C), 1.0, 6.0, ((0, 8), (1, 4))),
        "valid_size": draw_valid_size(jax.random.fold_in(splits[28], 71), 0),
        "vectors": draw_vectors(jax.random.fold_in(splits[28], 71), 0),
        "vectors_first": normal_values(splits[4], (NVEC, C), (0.44 / NPARAM ** 0.5), 0.0034179688, (), jnp.float32),
        "vectors_second": jnp.clip(jnp.exp(jax.random.uniform(splits[5], (NVEC, C), jnp.float32, math.log(2.887409067398039e-08), math.log(1.1549636269592156e-07))), 2.887409067398039e-08, 1.1549636269592156e-07),
        "qkv_weight": normal_values(splits[6], (C, 3 * C), C ** -0.5, 0.4375, (), jnp.float32),
        "qkv_first": normal_values(splits[7], (C, 3 * C), (0.11 / NPARAM ** 0.5), 0.0008544922, (), jnp.float32),
        "qkv_second": jnp.clip(jnp.exp(jax.random.uniform(splits[8], (C, 3 * C), jnp.float32, math.log(1.8046306671237744e-09), math.log(7.218522668495098e-09))), 1.8046306671237744e-09, 7.218522668495098e-09),
        "proj_weight": normal_values(splits[9], (C, C), (C // 8) ** -0.5, 1.25, (), jnp.float32),
        "proj_first": normal_values(splits[10], (C, C), (0.11 / NPARAM ** 0.5), 0.0008544922, (), jnp.float32),
        "proj_second": jnp.clip(jnp.exp(jax.random.uniform(splits[11], (C, C), jnp.float32, math.log(1.8046306671237744e-09), math.log(7.218522668495098e-09))), 1.8046306671237744e-09, 7.218522668495098e-09),
        "rel_table": normal_values(splits[12], (NREL, HEADS), 0.5, 2.0, (), jnp.float32),
        "rel_first": normal_values(splits[13], (NREL, HEADS), (0.44 / NPARAM ** 0.5), 0.0034179688, (), jnp.float32),
        "rel_second": jnp.clip(jnp.exp(jax.random.uniform(splits[14], (NREL, HEADS), jnp.float32, math.log(3.6092615007810025e-10), math.log(1.443704600312401e-09))), 3.6092615007810025e-10, 1.443704600312401e-09),
        "fc1_weight": normal_values(splits[15], (C, HID), C ** -0.5, 0.4375, (), jnp.float32),
        "fc1_first": normal_values(splits[16], (C, HID), (0.11 / NPARAM ** 0.5), 0.0008544922, (), jnp.float32),
        "fc1_second": jnp.clip(jnp.exp(jax.random.uniform(splits[17], (C, HID), jnp.float32, math.log(1.8046306671237744e-09), math.log(7.218522668495098e-09))), 1.8046306671237744e-09, 7.218522668495098e-09),
        "fc2_weight": normal_values(splits[18], (HID, C), HID ** -0.5, 0.3125, (), jnp.float32),
        "fc2_first": normal_values(splits[19], (HID, C), (0.11 / NPARAM ** 0.5), 0.0008544922, (), jnp.float32),
        "fc2_second": jnp.clip(jnp.exp(jax.random.uniform(splits[20], (HID, C), jnp.float32, math.log(1.8046306671237744e-09), math.log(7.218522668495098e-09))), 1.8046306671237744e-09, 7.218522668495098e-09),
        "conv_weight": normal_values(splits[21], (3, 3, C, C), (9 * C) ** -0.5, 0.15625, (), jnp.float32),
        "conv_first": normal_values(splits[22], (3, 3, C, C), (0.11 / NPARAM ** 0.5), 0.0008544922, (), jnp.float32),
        "conv_second": jnp.clip(jnp.exp(jax.random.uniform(splits[23], (3, 3, C, C), jnp.float32, math.log(1.8046306671237744e-09), math.log(7.218522668495098e-09))), 1.8046306671237744e-09, 7.218522668495098e-09),
        "step": jax.random.randint(splits[24], (1,), 2, 21).astype(jnp.int32),
        "sr_crops": draw_sr_crops(jax.random.fold_in(splits[28], 71), 0),
        "hr_crops": draw_hr_crops(jax.random.fold_in(splits[28], 71), 0),
        "psnr_running": jnp.clip(jax.random.uniform(splits[27], (1,), jnp.float32, 0.0, 1000.0), 0.0, 1000.0),
    }


eps_norm = 1e-05
neg_mask = -100.0
max_norm = 1.0
learn_rate = 0.03
vector_rate = 0.2
beta_one = 0.9
beta_two = 0.999
adam_eps = 1e-08
decay_rate = 0.01
highest = lax.Precision.HIGHEST

@jax.custom_vjp
def low(v):
    return lax.optimization_barrier(v.astype(jnp.bfloat16)).astype(jnp.float32)

@jax.custom_vjp
def low_back(v):
    return v

def low_keep(v):
    return (low(v), None)

def low_pass(kept, grad):
    return (grad,)

def back_keep(v):
    return (v, None)

def back_low(kept, grad):
    return (low(grad),)
low.defvjp(low_keep, low_pass)
low_back.defvjp(back_keep, back_low)

def to_windows(image, window):
    per_side = image.shape[0] // window
    channels = image.shape[-1]
    tiled = image.reshape(per_side, window, per_side, window, channels)
    return tiled.transpose(0, 2, 1, 3, 4).reshape(per_side * per_side, window * window, channels)

def from_windows(blocks, image_side, window):
    per_side = image_side // window
    channels = blocks.shape[-1]
    tiled = blocks.reshape(per_side, per_side, window, window, channels)
    return tiled.transpose(0, 2, 1, 3, 4).reshape(image_side, image_side, channels)

def region_mask(valid_len, image_side, window):
    shift_by = window // 2
    coords = jnp.arange(image_side)
    band_id = jnp.where(coords < image_side - window, 0, jnp.where(coords < image_side - shift_by, 1, 2))
    region = band_id[:, None] * 3 + band_id[None, :]
    anchor = (coords + shift_by) % image_side
    outside = anchor >= valid_len
    masked_key = outside[:, None] | outside[None, :]
    region_win = to_windows(region[:, :, None], window)[:, :, 0]
    masked_win = to_windows(masked_key[:, :, None], window)[:, :, 0]
    apart = region_win[:, :, None] != region_win[:, None, :]
    additive = jnp.where(apart, neg_mask, 0.0) + jnp.where(masked_win[:, None, :], neg_mask, 0.0)
    return additive.astype(jnp.float32)

def relative_onehot(window):
    position = jnp.arange(window * window)
    pos_row = position // window
    pos_col = position % window
    span_rel = 2 * window - 1
    rel_index = (pos_row[:, None] - pos_row[None, :] + window - 1) * span_rel + (pos_col[:, None] - pos_col[None, :] + window - 1)
    return (rel_index.reshape(-1)[:, None] == jnp.arange(span_rel * span_rel)[None, :]).astype(jnp.float32)

def layer_norm(values_in, gain, shift_vec):
    average = lax.optimization_barrier(jnp.mean(values_in, axis=-1, keepdims=True))
    centered = values_in - average
    variance = lax.optimization_barrier(jnp.mean(centered * centered, axis=-1, keepdims=True))
    return centered * lax.rsqrt(variance + eps_norm) * gain + shift_vec

def image_forward(image, valid_len, vectors, qkv_weight, proj_weight, rel_table, fc1_weight, fc2_weight, conv_weight):
    image_side = image.shape[0]
    channels = image.shape[-1]
    head_count = rel_table.shape[1]
    head_dim = channels // head_count
    shift_by = WIN // 2
    win_tokens = WIN * WIN
    normed = low(layer_norm(image, vectors[0], vectors[1]))
    rolled = jnp.roll(normed, (-shift_by, -shift_by), (0, 1))
    blocks = to_windows(rolled, WIN)
    win_count = blocks.shape[0]
    packed = jnp.einsum('wtc,cf->wtf', blocks, qkv_weight, precision=highest)
    queries = (packed[:, :, :channels] + vectors[2]) * head_dim ** (-0.5)
    key_rows = packed[:, :, channels:2 * channels]
    value_rows = packed[:, :, 2 * channels:] + vectors[3]
    shape_heads = (win_count, win_tokens, head_count, head_dim)
    queries = low(low_back(queries)).reshape(shape_heads)
    key_rows = low(low_back(key_rows)).reshape(shape_heads)
    value_rows = low(low_back(value_rows)).reshape(shape_heads)
    table_bias = jnp.dot(relative_onehot(WIN), rel_table, precision=highest)
    table_bias = table_bias.reshape(win_tokens, win_tokens, head_count).transpose(2, 0, 1)
    scores = jnp.einsum('wqhd,wkhd->whqk', queries, key_rows, precision=highest)
    scores = low_back(scores + table_bias[None] + region_mask(valid_len, image_side, WIN)[:, None])
    attn_probs = jax.nn.softmax(scores, axis=-1)
    mixed_rows = jnp.einsum('whqk,wkhd->wqhd', low(attn_probs), value_rows, precision=highest)
    mixed_rows = low(low_back(mixed_rows)).reshape(win_count, win_tokens, channels)
    projected = jnp.einsum('wtc,cf->wtf', mixed_rows, proj_weight, precision=highest) + vectors[4]
    attn_out = jnp.roll(from_windows(low_back(projected), image_side, WIN), (shift_by, shift_by), (0, 1))
    resid_one = image + attn_out
    normed_two = low(layer_norm(resid_one, vectors[5], vectors[6]))
    hidden_bias = jnp.concatenate([vectors[7], vectors[8]])
    hidden = low_back(jnp.einsum('ijc,cf->ijf', normed_two, fc1_weight, precision=highest) + hidden_bias)
    active = low(jax.nn.gelu(hidden, approximate=False))
    branch = low_back(jnp.einsum('ijf,fc->ijc', active, fc2_weight, precision=highest) + vectors[9])
    resid_two = resid_one + branch
    conv_in = low(resid_two)
    conv_out = lax.conv_general_dilated(conv_in[None], conv_weight, (1, 1), 'SAME', dimension_numbers=('NHWC', 'HWIO', 'NHWC'), precision=highest)[0]
    return conv_out + vectors[10] + image

def adam_update(weight, moment_one, moment_two, grad_item, clip_factor, first_fix, second_fix, step_rate):
    clipped = grad_item * clip_factor
    moment_one = beta_one * moment_one + (1.0 - beta_one) * clipped
    moment_two = beta_two * moment_two + (1.0 - beta_two) * clipped * clipped
    update = moment_one / first_fix / (jnp.sqrt(moment_two / second_fix) + adam_eps)
    return (weight - step_rate * (update + decay_rate * weight), moment_one, moment_two)

def reference(images, cotangent, valid_size, vectors, vectors_first, vectors_second, qkv_weight, qkv_first, qkv_second, proj_weight, proj_first, proj_second, rel_table, rel_first, rel_second, fc1_weight, fc1_first, fc1_second, fc2_weight, fc2_first, fc2_second, conv_weight, conv_first, conv_second, step, sr_crops, hr_crops, psnr_running):

    def forward(image_all, vec_all, qkv_all, proj_all, rel_all, fc1_all, fc2_all, conv_all):
        qkv_low = low(qkv_all)
        proj_low = low(proj_all)
        fc1_low = low(fc1_all)
        fc2_low = low(fc2_all)
        conv_low = low(conv_all)

        def per_image(item_pair):
            return jax.checkpoint(image_forward)(item_pair[0], item_pair[1], vec_all, qkv_low, proj_low, rel_all, fc1_low, fc2_low, conv_low)
        return lax.map(per_image, (image_all, valid_size))
    weights = (vectors, qkv_weight, proj_weight, rel_table, fc1_weight, fc2_weight, conv_weight)
    result, pullback = jax.vjp(forward, images.astype(jnp.float32), *weights)
    grads = pullback(cotangent.astype(jnp.float32))
    image_grad = grads[0]
    weight_grads = grads[1:]
    total_sq = jnp.zeros((), jnp.float32)
    for grad_item in weight_grads:
        total_sq = total_sq + jnp.sum(grad_item * grad_item)
    grad_norm = jnp.sqrt(total_sq)
    clip_factor = jnp.minimum(1.0, max_norm / (grad_norm + 1e-06))
    step_count = step[0].astype(jnp.float32)
    first_fix = 1.0 - beta_one ** step_count
    second_fix = 1.0 - beta_two ** step_count
    firsts = (vectors_first, qkv_first, proj_first, rel_first, fc1_first, fc2_first, conv_first)
    seconds = (vectors_second, qkv_second, proj_second, rel_second, fc1_second, fc2_second, conv_second)
    rate_list = (vector_rate, learn_rate, learn_rate, learn_rate, learn_rate, learn_rate, learn_rate)
    updated = []
    for weight, moment_one, moment_two, grad_item, step_rate in zip(weights, firsts, seconds, weight_grads, rate_list):
        updated.extend(adam_update(weight, moment_one, moment_two, grad_item, clip_factor, first_fix, second_fix, step_rate))
    difference = sr_crops - hr_crops
    luma_diff = (65.481 * difference[:, 0] + 128.553 * difference[:, 1] + 24.966 * difference[:, 2]) / 255.0
    mean_error = lax.optimization_barrier(jnp.mean(luma_diff * luma_diff, axis=(1, 2)))
    psnr_total = psnr_running + jnp.sum(-10.0 * jnp.log10(mean_error + 1e-06))
    return (result.astype(jnp.bfloat16), image_grad, grad_norm.reshape(1), psnr_total, updated[0], updated[1], updated[2], updated[3], updated[4], updated[5], updated[6], updated[7], updated[8], updated[9], updated[10], updated[11], updated[12], updated[13], updated[14], updated[15], updated[16], updated[17], updated[18], updated[19], updated[20])
```

```python
import functools

import jax
import jax.numpy as jnp
import numpy as np
from jax import lax
from jax.experimental import pallas as pl
from jax.experimental.pallas import tpu as pltpu
from jax.sharding import PartitionSpec as P

WIN = 8
TOK = WIN * WIN
SHIFT = WIN // 2
LANE = 128
TAP = 256

eps_norm = 1e-05
neg_mask = -100.0
max_norm = 1.0
learn_rate = 0.03
vector_rate = 0.2
beta_one = 0.9
beta_two = 0.999
adam_eps = 1e-08
decay_rate = 0.01
highest = lax.Precision.HIGHEST
f32 = jnp.float32
bf16 = jnp.bfloat16


def nn(a, b):
    return lax.dot_general(a, b, (((1,), (0,)), ((), ())), preferred_element_type=f32)


def nt(a, b):
    return lax.dot_general(a, b, (((1,), (1,)), ((), ())), preferred_element_type=f32)


def head_of(index):
    total = jnp.zeros(index.shape, jnp.int32)
    for k in range(1, 6):
        total = total + (index >= 30 * k).astype(jnp.int32)
    return total


def to_tokens(rows):
    side = rows.shape[1]
    return jnp.concatenate(
        [rows[:, w * WIN : (w + 1) * WIN, :].reshape(TOK, rows.shape[2]) for w in range(side // WIN)],
        axis=0,
    )


def from_tokens(tokens):
    count = tokens.shape[0] // TOK
    return jnp.concatenate(
        [tokens[w * TOK : (w + 1) * TOK].reshape(WIN, WIN, tokens.shape[1]) for w in range(count)],
        axis=1,
    )


def roll_cols(rows, by):
    side = rows.shape[1]
    by = by % side
    return jnp.concatenate([rows[:, by:, :], rows[:, :by, :]], axis=1)


def block_step(x_rows, gy_rows, first_step, edge, base_row, valid, image_side, wts, prep, acc, tmp, c_out, ig_out):
    (vec_ref, qkv_ref, proj_ref, fc1_ref, fc2_ref, conv_ref, bias_ref) = wts
    (vecT, wqT, wkT, wvT, wpT, w1T, w2T, wq, wk, wv, wp, w1, w2, wc, masks, pmask, colmask, rowmask, eye, b1T) = prep
    (acc_conv, acc_qkv, acc_proj, acc_fc1, acc_fc2, acc_ln, acc_rel) = acc
    (g9, a_aug, o_aug, m_aug, g_aug, c_aug, qeo_s, p_s, pb_s, kv_s, first_s, dat_s, dq_s, dkv_s, u2_s, xT_s, slope_s, vt_s, qt_s, kt_s) = tmp
    ch = x_rows.shape[2]
    hid = fc1_ref.shape[1]
    px = x_rows.shape[1] * WIN
    pairs = px // LANE

    @pl.when(first_step)
    def _():
        def split(ref, lo, hi):
            return ref[:, lo:hi]

        vecT[...] = jnp.transpose(vec_ref[...])
        b1T[...] = jnp.concatenate([vecT[:, 7:8], vecT[:, 8:9]], axis=0)
        for dst, dst_t, lo in ((wq, wqT, 0), (wk, wkT, ch), (wv, wvT, 2 * ch)):
            part = split(qkv_ref, lo, lo + ch)
            dst[...] = part.astype(bf16)
            dst_t[...] = jnp.transpose(part).astype(bf16)
        wp[...] = proj_ref[...].astype(bf16)
        wpT[...] = jnp.transpose(proj_ref[...]).astype(bf16)
        w1[...] = fc1_ref[...].astype(bf16)
        w1T[...] = jnp.transpose(fc1_ref[...]).astype(bf16)
        w2[...] = fc2_ref[...].astype(bf16)
        w2T[...] = jnp.transpose(fc2_ref[...]).astype(bf16)
        wc[...] = jnp.zeros_like(wc)
        g9[...] = jnp.zeros_like(g9)
        for tap in range(9):
            wc[:, tap * TAP : tap * TAP + ch] = conv_ref[tap // 3, tap % 3].astype(bf16)
        row = lax.broadcasted_iota(jnp.int32, (ch, LANE), 0)
        lane = lax.broadcasted_iota(jnp.int32, (ch, LANE), 1)
        head = head_of(row)
        low_half = lane < TOK
        odd = (head & 1) == 1
        pair = head >> 1
        one = lambda m: m.astype(f32)
        masks[0] = one(low_half & jnp.logical_not(odd))
        masks[1] = one(jnp.logical_not(low_half) & odd)
        masks[2] = one(low_half & (pair == 0))
        masks[3] = one(jnp.logical_not(low_half) & (pair == 1))
        masks[4] = one(pair == 2)
        lane_pair = head_of(lax.broadcasted_iota(jnp.int32, (TOK, ch), 1)) >> 1
        for p in range(3):
            pmask[p] = one(lane_pair == p)
        key = lax.broadcasted_iota(jnp.int32, (TOK, LANE), 0)
        query = lax.broadcasted_iota(jnp.int32, (TOK, LANE), 1) & (TOK - 1)
        colmask[...] = one(((key & 7) < SHIFT) != ((query & 7) < SHIFT))
        rowmask[...] = one(((key >> 3) < SHIFT) != ((query >> 3) < SHIFT))
        er = lax.broadcasted_iota(jnp.int32, (ch, ch), 0)
        ec = lax.broadcasted_iota(jnp.int32, (ch, ch), 1)
        eye[...] = (er == ec).astype(f32).astype(bf16)
        for ref in (a_aug, o_aug, m_aug, c_aug):
            pad = ref.shape[0] - ch
            ref[ch:, :] = (lax.broadcasted_iota(jnp.int32, (pad, px), 0) == 0).astype(f32).astype(bf16)
        pad = g_aug.shape[0] - hid
        g_aug[hid:, :] = (lax.broadcasted_iota(jnp.int32, (pad, px), 0) == 0).astype(f32).astype(bf16)

    def column(k):
        return vecT[:, k : k + 1]

    def natural(matrix_t):
        return jnp.transpose(matrix_t.astype(f32))

    def stats(v):
        mean = jnp.sum(v, axis=0, keepdims=True) * (1.0 / ch)
        cen = v - mean
        var = jnp.sum(cen * cen, axis=0, keepdims=True) * (1.0 / ch)
        inv = lax.rsqrt(var + eps_norm)
        return cen * inv, inv

    def ln_back(grad, u, inv, gain):
        t = grad * gain
        mean_t = jnp.sum(t, axis=0, keepdims=True) * (1.0 / ch)
        mean_tu = jnp.sum(t * u, axis=0, keepdims=True) * (1.0 / ch)
        return inv * (t - mean_t - u * mean_tu)

    def lane_fold(v):
        out = v[:, :LANE]
        for k in range(1, v.shape[1] // LANE):
            out = out + v[:, k * LANE : (k + 1) * LANE]
        return out

    gyf = gy_rows.astype(f32)
    keep = jnp.where(edge, 0.0, 1.0).astype(f32)
    col = lax.broadcasted_iota(jnp.int32, (1, image_side, ch), 1)
    for j in range(3):
        shifted = roll_cols(gyf, SHIFT + 1 - j)
        if j == 0:
            shifted = jnp.where(col == image_side - SHIFT - 1, 0.0, shifted)
        if j == 2:
            shifted = jnp.where(col == image_side - SHIFT, 0.0, shifted)
        for i in range(3):
            rows = [shifted[r + 2 - i : r + 3 - i] for r in range(WIN)]
            if i == 0:
                rows[SHIFT - 1] = rows[SHIFT - 1] * keep
            if i == 2:
                rows[SHIFT] = rows[SHIFT] * keep
            tap = 3 * i + j
            g9[:, tap * TAP : tap * TAP + ch] = to_tokens(jnp.concatenate(rows, axis=0)).astype(bf16)

    x_tok = to_tokens(roll_cols(x_rows.astype(f32), SHIFT)).astype(bf16)
    xT = nt(eye[...], x_tok)
    xT_s[...] = xT
    u1, inv1 = stats(xT)
    aT = (u1 * column(0) + column(1)).astype(bf16)
    a_aug[:ch, :] = aT
    scale = (ch // 6) ** (-0.5)
    qt_s[...] = ((nn(wqT[...], aT) + column(2)) * scale).astype(bf16).astype(f32)
    kT = nn(wkT[...], aT).astype(bf16).astype(f32)
    vT = (nn(wvT[...], aT) + column(3)).astype(bf16).astype(f32)
    kt_s[...] = kT
    vt_s[...] = vT
    kv_s[0] = jnp.transpose(kT).astype(bf16)
    kv_s[1] = jnp.transpose(vT).astype(bf16)

    def dup(slab):
        other = pltpu.roll(slab, TOK, 1)
        return (
            (slab * masks[0] + other * masks[1]).astype(bf16),
            (other * masks[0] + slab * masks[1]).astype(bf16),
        )

    def spread(slab):
        other = pltpu.roll(slab, TOK, 1)
        first = jnp.concatenate(
            [slab * masks[2] + other * masks[3], (slab * masks[4])[:, :TOK]], axis=1
        ).astype(bf16)
        second = jnp.concatenate(
            [other * masks[2] + slab * masks[3], (other * masks[4])[:, :TOK]], axis=1
        ).astype(bf16)
        return first, second

    def merge(one, two):
        lane = lax.broadcasted_iota(jnp.int32, (ch, LANE), 1)
        crossed = pltpu.roll(jnp.where(lane < TOK, two, one), TOK, 1)
        return jnp.where(masks[0] > 0.5, one, jnp.where(masks[1] > 0.5, two, crossed))

    def by_pair(rows):
        return jnp.concatenate([rows * pmask[p].astype(bf16) for p in range(3)], axis=0)

    def pick_pair(stacked):
        return (
            stacked[:TOK] * pmask[0] + stacked[TOK : 2 * TOK] * pmask[1] + stacked[2 * TOK :] * pmask[2]
        )

    key = lax.broadcasted_iota(jnp.int32, (TOK, LANE), 0)
    key_row = base_row + (key >> 3)
    key_row = jnp.where(key_row >= image_side, key_row - image_side, key_row)
    out_row = key_row >= valid
    edge_f = jnp.where(edge, neg_mask, 0.0).astype(f32)
    for pp in range(pairs):
        cols = slice(pp * LANE, (pp + 1) * LANE)
        q_pair = dup(qt_s[:, cols])
        v_pair = spread(vt_s[:, cols])
        mixed = []
        for half in range(2):
            w = 2 * pp + half
            qeo_s[w] = q_pair[half]
            s = nn(by_pair(kv_s[0, w * TOK : (w + 1) * TOK, :]), q_pair[half])
            key_col = (key & 7) + (w * WIN + SHIFT)
            if w == 2 * pairs - 1:
                key_col = jnp.where(key_col >= image_side, key_col - image_side, key_col)
                apart = rowmask[...] * edge_f
                apart = jnp.where(colmask[...] > 0.5, neg_mask, apart)
            else:
                apart = rowmask[...] * edge_f
            extra = apart + jnp.where(out_row | (key_col >= valid), neg_mask, 0.0)
            s = s.reshape(3, TOK, LANE) + bias_ref[...] + extra[None]
            top = jnp.max(s, axis=1, keepdims=True)
            e = jnp.exp(s - top)
            p = e / jnp.sum(e, axis=1, keepdims=True)
            p = p.reshape(3 * TOK, LANE)
            p_s[w] = p
            pb = p.astype(bf16)
            pb_s[w] = pb
            mixed.append(nn(v_pair[half], pb))
        o_aug[:ch, cols] = merge(*mixed).astype(bf16)

    first = xT_s[...] + (nn(wpT[...], o_aug[:ch, :]) + column(4))
    u2, inv2 = stats(first)
    u2_s[...] = u2
    mT = (u2 * column(5) + column(6)).astype(bf16)
    m_aug[:ch, :] = mT
    hidden = nn(w1T[...], mT) + b1T[...]
    cdf = 0.5 * (1.0 + lax.erf(hidden * 0.7071067811865476))
    g_aug[:hid, :] = (hidden * cdf).astype(bf16)
    slope_s[...] = cdf + hidden * jnp.exp(-0.5 * hidden * hidden) * 0.3989422804014327
    second = first + (nn(w2T[...], g_aug[:hid, :]) + column(9))
    cT = second.astype(bf16)
    c_aug[:ch, :] = cT
    c_out[0] = roll_cols(from_tokens(natural(cT)), -SHIFT).astype(bf16)

    dsecond = nt(wc[...], g9[...])
    acc_conv[...] += nn(c_aug[...], g9[...])
    dbT = dsecond.astype(bf16)
    acc_fc2[...] += nt(g_aug[...], dbT)
    dhT = (nn(w2[...], dbT) * slope_s[...]).astype(bf16)
    acc_fc1[...] += nt(m_aug[...], dhT)
    dm = nn(w1[...], dhT)
    u2 = u2_s[...]
    acc_ln[2] += lane_fold(dm * u2)
    acc_ln[3] += lane_fold(dm)
    dfirst = dsecond + ln_back(dm, u2, inv2, column(5))
    first_s[...] = dfirst
    datT = dfirst.astype(bf16)
    acc_proj[...] += nt(o_aug[...], datT)
    dat_s[...] = nn(wp[...], datT).astype(bf16).astype(f32)

    rel_sum = jnp.zeros((3 * TOK, LANE), f32)
    for pp in range(pairs):
        cols = slice(pp * LANE, (pp + 1) * LANE)
        do_pair = dup(dat_s[:, cols])
        k_pair = spread(kt_s[:, cols])
        dq = []
        for half in range(2):
            w = 2 * pp + half
            toks = slice(w * TOK, (w + 1) * TOK)
            dv = pick_pair(nt(pb_s[w], do_pair[half]))
            dp = nn(by_pair(kv_s[1, toks, :]), do_pair[half])
            p = p_s[w].reshape(3, TOK, LANE)
            dp = dp.reshape(3, TOK, LANE)
            ds = p * (dp - jnp.sum(p * dp, axis=1, keepdims=True))
            ds = ds.reshape(3 * TOK, LANE).astype(bf16)
            rel_sum = rel_sum + ds.astype(f32)
            dk = pick_pair(nt(ds, qeo_s[w]))
            dq.append(nn(k_pair[half], ds))
            dkv_s[0, toks, :] = dk.astype(bf16)
            dkv_s[1, toks, :] = dv.astype(bf16)
        dq_s[:, cols] = merge(*dq).astype(bf16)
    acc_rel[...] += rel_sum

    dqT = dq_s[...]
    acc_qkv[0] += nt(a_aug[...], dqT) * scale
    acc_qkv[1] += nn(a_aug[...], dkv_s[0])
    acc_qkv[2] += nn(a_aug[...], dkv_s[1])
    da = nn(wq[...], dqT) * scale + (nt(wk[...], dkv_s[0]) + nt(wv[...], dkv_s[1]))
    u1, inv1 = stats(xT_s[...])
    acc_ln[0] += lane_fold(da * u1)
    acc_ln[1] += lane_fold(da)
    ig = first_s[...] + ln_back(da, u1, inv1, column(0))
    ig_out[0] = roll_cols(from_tokens(jnp.transpose(ig)), -SHIFT) + gyf[1 : 1 + WIN]


N_ACC = 7
N_WTS = 7


def inner_kernel(image_side, own_rows, info, x_ref, gy_ref, *refs):
    wts, refs = refs[:N_WTS], refs[N_WTS:]
    c_out, ig_out, refs = refs[0], refs[1], refs[2:]
    acc, refs = refs[:N_ACC], refs[N_ACC:]
    prep, tmp = refs[:20], refs[20:]
    image, row_block = pl.program_id(0), pl.program_id(1)
    first_step = (image == 0) & (row_block == 0)

    @pl.when(first_step)
    def _():
        for ref in acc:
            ref[...] = jnp.zeros_like(ref)

    start = row_block * WIN + SHIFT
    x_rows = x_ref[0, pl.ds(start, WIN)]
    gy_rows = gy_ref[0, pl.ds(start - 1, WIN + 2)]
    base_row = info[0] * own_rows + start
    block_step(
        x_rows, gy_rows, first_step, False, base_row, info[2 + image], image_side, wts, prep, acc, tmp, c_out, ig_out
    )


def last_kernel(image_side, own_rows, info, x_ref, gy_ref, xh_ref, gyh_ref, *refs):
    wts, refs = refs[:N_WTS], refs[N_WTS:]
    acc_in, refs = refs[:N_ACC], refs[N_ACC:]
    c_out, ig_out, refs = refs[0], refs[1], refs[2:]
    acc, refs = refs[:N_ACC], refs[N_ACC:]
    prep, tmp = refs[:20], refs[20:]
    image = pl.program_id(0)
    first_step = image == 0

    @pl.when(first_step)
    def _():
        for ref, given in zip(acc, acc_in):
            ref[...] = given[...]

    x_rows = jnp.concatenate([x_ref[0, SHIFT:], xh_ref[0]], axis=0)
    gy_rows = jnp.concatenate([gy_ref[0, SHIFT - 1 :], gyh_ref[0]], axis=0)
    base_row = info[0] * own_rows + own_rows - SHIFT
    block_step(
        x_rows, gy_rows, first_step, info[1] == 1, base_row, info[2 + image], image_side, wts, prep, acc, tmp, c_out, ig_out
    )


def whole(shape):
    return pl.BlockSpec(shape, lambda *_: (0,) * len(shape))


def acc_shapes(ch, hid):
    up = lambda n: -(-(n + 1) // 16) * 16
    return [
        (up(ch), 9 * TAP),
        (3, up(ch), ch),
        (up(ch), ch),
        (up(ch), hid),
        (up(hid), ch),
        (4, ch, LANE),
        (3 * TOK, LANE),
    ]


def scratches(ch, hid, px, vec_rows):
    up = lambda n: -(-(n + 1) // 16) * 16
    v = pltpu.VMEM
    prep = [
        v((ch, vec_rows), f32),
        v((ch, ch), bf16), v((ch, ch), bf16), v((ch, ch), bf16), v((ch, ch), bf16),
        v((hid, ch), bf16), v((ch, hid), bf16),
        v((ch, ch), bf16), v((ch, ch), bf16), v((ch, ch), bf16), v((ch, ch), bf16),
        v((ch, hid), bf16), v((hid, ch), bf16),
        v((ch, 9 * TAP), bf16),
        v((5, ch, LANE), f32),
        v((3, TOK, ch), f32),
        v((TOK, LANE), f32),
        v((TOK, LANE), f32),
        v((ch, ch), bf16),
        v((hid, 1), f32),
    ]
    wins = px // TOK
    tmp = [
        v((px, 9 * TAP), bf16),
        v((up(ch), px), bf16), v((up(ch), px), bf16), v((up(ch), px), bf16), v((up(hid), px), bf16), v((up(ch), px), bf16),
        v((wins, ch, LANE), bf16),
        v((wins, 3 * TOK, LANE), f32),
        v((wins, 3 * TOK, LANE), bf16),
        v((2, px, ch), bf16),
        v((ch, px), f32),
        v((ch, px), f32),
        v((ch, px), bf16),
        v((2, px, ch), bf16),
        v((ch, px), f32),
        v((ch, px), f32),
        v((hid, px), f32),
        v((ch, px), f32),
        v((ch, px), f32),
        v((ch, px), f32),
    ]
    return prep + tmp


def conv_kernel(image_side, own_rows, info, hc_ref, c1_ref, c2_ref, hg_ref, g1_ref, g2_ref, x_ref, vec_ref, conv_ref, out_ref, ig_ref, cs, wc):
    ch = x_ref.shape[3]

    @pl.when(pl.program_id(0) == 0)
    def _():
        wc[...] = jnp.zeros_like(wc)
        cs[...] = jnp.zeros_like(cs)
        for tap in range(9):
            wc[tap * TAP : tap * TAP + ch, :] = conv_ref[tap // 3, tap % 3].astype(bf16)

    first = jnp.where(info[0] == 0, 0.0, 1.0).astype(f32)
    last = jnp.where(info[1] == 1, 0.0, 1.0).astype(f32)
    need = own_rows + 2
    col = lax.broadcasted_iota(jnp.int32, (1, image_side, ch), 1)
    halo = hc_ref.shape[1]
    for r in range(need):
        if r < halo:
            row = hc_ref[0, r : r + 1]
        elif r - halo < c1_ref.shape[1]:
            row = c1_ref[0, r - halo : r - halo + 1]
        else:
            at = r - halo - c1_ref.shape[1]
            row = c2_ref[0, at : at + 1]
        row = row.astype(f32)
        if r == 0:
            row = row * first
        if r == need - 1:
            row = row * last
        left = jnp.where(col == 0, 0.0, roll_cols(row, -1))
        right = jnp.where(col == image_side - 1, 0.0, roll_cols(row, 1))
        at = slice(r * image_side, (r + 1) * image_side)
        cs[at, 0:ch] = left[0].astype(bf16)
        cs[at, TAP : TAP + ch] = row[0].astype(bf16)
        cs[at, 2 * TAP : 2 * TAP + ch] = right[0].astype(bf16)
    group = 4
    bias = vec_ref[10:11, :]
    for r in range(0, own_rows, group):
        total = None
        for i in range(3):
            at = slice((r + i) * image_side, (r + i + group) * image_side)
            term = nn(cs[at, :], wc[i * 3 * TAP : (i + 1) * 3 * TAP, :])
            total = term if total is None else total + term
        total = total + bias
        total = total.reshape(group, image_side, ch) + x_ref[0, r : r + group].astype(f32)
        out_ref[0, r : r + group] = total.astype(bf16)
    head = hg_ref.shape[1]
    mid = g1_ref.shape[1]
    ig_ref[0, :head] = hg_ref[0]
    ig_ref[0, head : head + mid] = g1_ref[0]
    ig_ref[0, head + mid :] = g2_ref[0, : own_rows - head - mid]


def adam_kernel(scal, a_conv, a_qkv, a_proj, a_fc1, a_fc2, a_ln, a_rel, *refs):
    weights, firsts, seconds = refs[0:7], refs[7:14], refs[14:21]
    norm_ref, outs = refs[21], refs[22:43]
    ch = weights[2].shape[0]
    hid = weights[5].shape[0]
    g_vec = [
        a_ln[0:1, :],
        a_ln[1:2, :],
        a_qkv[0, ch : ch + 1, :],
        a_qkv[2, ch : ch + 1, :],
        a_proj[ch : ch + 1, :],
        a_ln[2:3, :],
        a_ln[3:4, :],
        a_fc1[ch : ch + 1, :ch],
        a_fc1[ch : ch + 1, ch:],
        a_fc2[hid : hid + 1, :],
        a_conv[ch : ch + 1, 4 * TAP : 4 * TAP + ch],
    ]
    vec = jnp.concatenate(g_vec, axis=0)
    qkv = jnp.concatenate([a_qkv[k, :ch, :] for k in range(3)], axis=1)
    small = [vec, qkv, a_proj[:ch, :], a_rel[...], a_fc1[:ch, :], a_fc2[:hid, :]]
    taps = [a_conv[:ch, t * TAP : t * TAP + ch] for t in range(9)]
    total = jnp.zeros((1, 1), f32)
    for g in small + taps:
        total = total + jnp.sum(jnp.sum(g * g, axis=0, keepdims=True), axis=1, keepdims=True)
    norm = jnp.sqrt(total)
    norm_ref[...] = norm
    clip = jnp.minimum(1.0, max_norm / (norm + 1e-06))
    fix_one, fix_two = scal[0], scal[1]

    def update(w, m1, m2, g, rate):
        g = g * clip
        m1 = beta_one * m1 + (1.0 - beta_one) * g
        m2 = beta_two * m2 + (1.0 - beta_two) * g * g
        step = (m1 / fix_one) / (jnp.sqrt(m2 / fix_two) + adam_eps)
        return w - rate * (step + decay_rate * w), m1, m2

    for k, g in enumerate(small):
        new = update(weights[k][...], firsts[k][...], seconds[k][...], g, vector_rate if k == 0 else learn_rate)
        for ref, value in zip(outs[3 * k : 3 * k + 3], new):
            ref[...] = value
    for t, g in enumerate(taps):
        at = (t // 3, t % 3)
        new = update(weights[6][at], firsts[6][at], seconds[6][at], g, learn_rate)
        for ref, value in zip(outs[18:21], new):
            ref[at] = value


def relative_onehot_keys_first():
    position = np.arange(TOK)
    pos_row, pos_col = position // WIN, position % WIN
    span = 2 * WIN - 1
    index = (pos_row[None, :] - pos_row[:, None] + WIN - 1) * span + (
        pos_col[None, :] - pos_col[:, None] + WIN - 1
    )
    return index.reshape(-1), span * span


def on_device(
    images, cotangent, valid_size,
    vectors, vectors_first, vectors_second,
    qkv_weight, qkv_first, qkv_second,
    proj_weight, proj_first, proj_second,
    rel_table, rel_first, rel_second,
    fc1_weight, fc1_first, fc1_second,
    fc2_weight, fc2_first, fc2_second,
    conv_weight, conv_first, conv_second,
    step, sr_crops, hr_crops, psnr_running,
):
    count, own_rows, image_side, ch = images.shape
    hid = fc1_weight.shape[1]
    px = image_side * WIN
    blocks = own_rows // WIN
    heads = lax.axis_size("head")
    place = lax.axis_index("head")
    to_lower = [((i + 1) % heads, i) for i in range(heads)]
    to_upper = [(i, (i + 1) % heads) for i in range(heads)]
    info = jnp.concatenate(
        [
            jnp.stack([place, (place == heads - 1).astype(jnp.int32)]).astype(jnp.int32),
            valid_size.astype(jnp.int32),
        ]
    )
    halo = lax.ppermute(
        jnp.concatenate([images[:, :SHIFT], cotangent[:, : SHIFT + 1]], axis=1), "head", to_lower
    )
    x_halo, gy_halo = halo[:, :SHIFT], halo[:, SHIFT:]

    index, span = relative_onehot_keys_first()
    onehot = (jnp.asarray(index)[:, None] == jnp.arange(span)[None, :]).astype(f32)
    bias = jnp.dot(onehot, rel_table, precision=highest)
    bias = bias.reshape(TOK, TOK, 3, 2).transpose(2, 0, 3, 1).reshape(3, TOK, LANE)

    wts = (vectors, qkv_weight, proj_weight, fc1_weight, fc2_weight, conv_weight, bias)
    wts_specs = [whole(w.shape) for w in wts]
    acc_dims = acc_shapes(ch, hid)
    acc_types = [jax.ShapeDtypeStruct(s, f32) for s in acc_dims]
    smem = pl.BlockSpec(memory_space=pltpu.SMEM)
    params = pltpu.CompilerParams(
        dimension_semantics=("arbitrary", "arbitrary"), vmem_limit_bytes=60 * 1024 * 1024
    )
    c1, ig1, *acc = pl.pallas_call(
        functools.partial(inner_kernel, image_side, own_rows),
        grid=(count, blocks - 1),
        in_specs=[
            smem,
            pl.BlockSpec((1, own_rows, image_side, ch), lambda n, r: (n, 0, 0, 0)),
            pl.BlockSpec((1, own_rows, image_side, ch), lambda n, r: (n, 0, 0, 0)),
            *wts_specs,
        ],
        out_specs=[
            pl.BlockSpec((1, WIN, image_side, ch), lambda n, r: (n, r, 0, 0)),
            pl.BlockSpec((1, WIN, image_side, ch), lambda n, r: (n, r, 0, 0)),
            *[whole(s) for s in acc_dims],
        ],
        out_shape=[
            jax.ShapeDtypeStruct((count, own_rows - WIN, image_side, ch), bf16),
            jax.ShapeDtypeStruct((count, own_rows - WIN, image_side, ch), f32),
            *acc_types,
        ],
        scratch_shapes=scratches(ch, hid, px, vectors.shape[0]),
        compiler_params=params,
        name="inner_windows",
    )(info, images, cotangent, *wts)
    c2, ig2, *acc = pl.pallas_call(
        functools.partial(last_kernel, image_side, own_rows),
        grid=(count,),
        in_specs=[
            smem,
            pl.BlockSpec((1, WIN, image_side, ch), lambda n: (n, blocks - 1, 0, 0)),
            pl.BlockSpec((1, WIN, image_side, ch), lambda n: (n, blocks - 1, 0, 0)),
            pl.BlockSpec((1, SHIFT, image_side, ch), lambda n: (n, 0, 0, 0)),
            pl.BlockSpec((1, SHIFT + 1, image_side, ch), lambda n: (n, 0, 0, 0)),
            *wts_specs,
            *[whole(s) for s in acc_dims],
        ],
        out_specs=[
            pl.BlockSpec((1, WIN, image_side, ch), lambda n: (n, 0, 0, 0)),
            pl.BlockSpec((1, WIN, image_side, ch), lambda n: (n, 0, 0, 0)),
            *[whole(s) for s in acc_dims],
        ],
        out_shape=[
            jax.ShapeDtypeStruct((count, WIN, image_side, ch), bf16),
            jax.ShapeDtypeStruct((count, WIN, image_side, ch), f32),
            *acc_types,
        ],
        scratch_shapes=scratches(ch, hid, px, vectors.shape[0]),
        compiler_params=pltpu.CompilerParams(
            dimension_semantics=("arbitrary",), vmem_limit_bytes=60 * 1024 * 1024
        ),
        name="last_windows",
    )(info, images, cotangent, x_halo, gy_halo, *wts, *acc)

    c_halo = lax.ppermute(c2[:, WIN - SHIFT - 1 :], "head", to_upper)
    ig_halo = lax.ppermute(ig2[:, WIN - SHIFT :], "head", to_upper)

    a_conv, a_qkv, a_proj, a_fc1, a_fc2, a_ln, a_rel = acc
    rel = a_rel.reshape(3, TOK, 2, TOK).transpose(0, 2, 1, 3).reshape(6, TOK * TOK)
    rel = jnp.dot(rel, onehot, precision=highest).T
    ln = jnp.sum(a_ln, axis=2)

    difference = sr_crops - hr_crops
    luma = (65.481 * difference[:, 0] + 128.553 * difference[:, 1] + 24.966 * difference[:, 2]) / 255.0
    mean_error = jnp.mean(luma * luma, axis=(1, 2))
    local_psnr = jnp.sum(-10.0 * jnp.log10(mean_error + 1e-06))
    a_conv, a_qkv, a_proj, a_fc1, a_fc2, ln, rel, psnr = lax.psum(
        (a_conv, a_qkv, a_proj, a_fc1, a_fc2, ln, rel, local_psnr), ("dp", "head")
    )
    psnr_total = psnr_running + psnr

    image_block = lambda rows: pl.BlockSpec((1, rows, image_side, ch), lambda n: (n, 0, 0, 0))
    output, image_grad = pl.pallas_call(
        functools.partial(conv_kernel, image_side, own_rows),
        grid=(count,),
        in_specs=[
            smem,
            image_block(SHIFT + 1), image_block(own_rows - WIN), image_block(WIN),
            image_block(SHIFT), image_block(own_rows - WIN), image_block(WIN),
            image_block(own_rows),
            whole(vectors.shape), whole(conv_weight.shape),
        ],
        out_specs=[image_block(own_rows), image_block(own_rows)],
        out_shape=[
            jax.ShapeDtypeStruct(images.shape, bf16),
            jax.ShapeDtypeStruct(images.shape, f32),
        ],
        scratch_shapes=[
            pltpu.VMEM(((own_rows + 2) * image_side, 3 * TAP), bf16),
            pltpu.VMEM((9 * TAP, ch), bf16),
        ],
        compiler_params=pltpu.CompilerParams(
            dimension_semantics=("arbitrary",), vmem_limit_bytes=60 * 1024 * 1024
        ),
        name="conv_output",
    )(info, c_halo, c1, c2, ig_halo, ig1, ig2, images, vectors, conv_weight)

    step_count = step[0].astype(f32)
    scal = jnp.stack([1.0 - beta_one**step_count, 1.0 - beta_two**step_count])
    weights = (vectors, qkv_weight, proj_weight, rel_table, fc1_weight, fc2_weight, conv_weight)
    firsts = (vectors_first, qkv_first, proj_first, rel_first, fc1_first, fc2_first, conv_first)
    seconds = (vectors_second, qkv_second, proj_second, rel_second, fc1_second, fc2_second, conv_second)
    vmem = pl.BlockSpec(memory_space=pltpu.VMEM)
    grad_norm, *updated = pl.pallas_call(
        adam_kernel,
        in_specs=[smem] + [vmem] * 28,
        out_specs=[vmem] * 22,
        out_shape=[jax.ShapeDtypeStruct((1, 1), f32)]
        + [jax.ShapeDtypeStruct(w.shape, f32) for w in weights for _ in range(3)],
        compiler_params=pltpu.CompilerParams(vmem_limit_bytes=60 * 1024 * 1024),
        name="adam",
    )(scal, a_conv, a_qkv, a_proj, a_fc1, a_fc2, ln, rel, *weights, *firsts, *seconds)
    return (output, image_grad, grad_norm.reshape(1), psnr_total, *updated)


def solution(mesh):
    pixels = P("dp", "head", None, None)
    crops = P(("dp", "head"), None, None, None)
    placed = (pixels, pixels, P("dp")) + (P(),) * 22 + (crops, crops, P())
    return jax.shard_map(
        on_device,
        mesh=mesh,
        in_specs=placed,
        out_specs=(pixels, pixels) + (P(),) * 23,
        check_vma=False,
    )
```

```python
import functools

import jax
import jax.numpy as jnp
import numpy as np
from jax import lax
from jax.experimental import pallas as pl
from jax.experimental.pallas import tpu as pltpu
from jax.sharding import PartitionSpec as P

WIN = 8
TOK = WIN * WIN
SHIFT = WIN // 2
LANE = 128
TAP = 256

eps_norm = 1e-05
neg_mask = -100.0
max_norm = 1.0
learn_rate = 0.03
vector_rate = 0.2
beta_one = 0.9
beta_two = 0.999
adam_eps = 1e-08
decay_rate = 0.01
highest = lax.Precision.HIGHEST
f32 = jnp.float32
bf16 = jnp.bfloat16


def nn(a, b):
    return lax.dot_general(a, b, (((1,), (0,)), ((), ())), preferred_element_type=f32)


def nt(a, b):
    return lax.dot_general(a, b, (((1,), (1,)), ((), ())), preferred_element_type=f32)


def head_of(index):
    total = jnp.zeros(index.shape, jnp.int32)
    for k in range(1, 6):
        total = total + (index >= 30 * k).astype(jnp.int32)
    return total


def to_tokens(rows):
    side = rows.shape[1]
    return jnp.concatenate(
        [rows[:, w * WIN : (w + 1) * WIN, :].reshape(TOK, rows.shape[2]) for w in range(side // WIN)],
        axis=0,
    )


def from_tokens(tokens):
    count = tokens.shape[0] // TOK
    return jnp.concatenate(
        [tokens[w * TOK : (w + 1) * TOK].reshape(WIN, WIN, tokens.shape[1]) for w in range(count)],
        axis=1,
    )


def roll_cols(rows, by):
    side = rows.shape[1]
    by = by % side
    return jnp.concatenate([rows[:, by:, :], rows[:, :by, :]], axis=1)


def block_step(x_rows, gy_rows, first_step, edge, base_row, valid, image_side, wts, prep, acc, tmp, c_out, ig_out):
    (vec_ref, qkv_ref, proj_ref, fc1_ref, fc2_ref, conv_ref, bias_ref) = wts
    (vecT, wqT, wkT, wvT, wpT, w1T, w2T, wq, wk, wv, wp, w1, w2, wc, masks, pmask, colmask, rowmask, eye, b1T) = prep
    (acc_conv, acc_qkv, acc_proj, acc_fc1, acc_fc2, acc_ln, acc_rel) = acc
    (g9, a_aug, o_aug, m_aug, g_aug, c_aug, qeo_s, p_s, pb_s, kv_s, first_s, dat_s, dq_s, dkv_s, u2_s, xT_s, slope_s, vt_s, qt_s, kt_s) = tmp
    ch = x_rows.shape[2]
    hid = fc1_ref.shape[1]
    px = x_rows.shape[1] * WIN
    pairs = px // LANE

    @pl.when(first_step)
    def _():
        def split(ref, lo, hi):
            return ref[:, lo:hi]

        vecT[...] = jnp.transpose(vec_ref[...])
        b1T[...] = jnp.concatenate([vecT[:, 7:8], vecT[:, 8:9]], axis=0)
        for dst, dst_t, lo in ((wq, wqT, 0), (wk, wkT, ch), (wv, wvT, 2 * ch)):
            part = split(qkv_ref, lo, lo + ch)
            dst[...] = part.astype(bf16)
            dst_t[...] = jnp.transpose(part).astype(bf16)
        wp[...] = proj_ref[...].astype(bf16)
        wpT[...] = jnp.transpose(proj_ref[...]).astype(bf16)
        w1[...] = fc1_ref[...].astype(bf16)
        w1T[...] = jnp.transpose(fc1_ref[...]).astype(bf16)
        w2T[...] = fc2_ref[...].astype(bf16)
        w2[...] = jnp.transpose(fc2_ref[...]).astype(bf16)
        wc[...] = jnp.zeros_like(wc)
        g9[...] = jnp.zeros_like(g9)
        for tap in range(9):
            wc[:, tap * TAP : tap * TAP + ch] = conv_ref[tap // 3, tap % 3].astype(bf16)
        row = lax.broadcasted_iota(jnp.int32, (ch, LANE), 0)
        lane = lax.broadcasted_iota(jnp.int32, (ch, LANE), 1)
        head = head_of(row)
        low_half = lane < TOK
        odd = (head & 1) == 1
        pair = head >> 1
        one = lambda m: m.astype(f32)
        masks[0] = one(low_half & jnp.logical_not(odd))
        masks[1] = one(jnp.logical_not(low_half) & odd)
        masks[2] = one(low_half & (pair == 0))
        masks[3] = one(jnp.logical_not(low_half) & (pair == 1))
        masks[4] = one(pair == 2)
        lane_pair = head_of(lax.broadcasted_iota(jnp.int32, (TOK, ch), 1)) >> 1
        for p in range(3):
            pmask[p] = one(lane_pair == p)
        key = lax.broadcasted_iota(jnp.int32, (TOK, LANE), 0)
        query = lax.broadcasted_iota(jnp.int32, (TOK, LANE), 1) & (TOK - 1)
        colmask[...] = one(((key & 7) < SHIFT) != ((query & 7) < SHIFT))
        rowmask[...] = one(((key >> 3) < SHIFT) != ((query >> 3) < SHIFT))
        er = lax.broadcasted_iota(jnp.int32, (ch, ch), 0)
        ec = lax.broadcasted_iota(jnp.int32, (ch, ch), 1)
        eye[...] = (er == ec).astype(f32).astype(bf16)
        for ref in (a_aug, o_aug, m_aug, c_aug):
            pad = ref.shape[0] - ch
            ref[ch:, :] = (lax.broadcasted_iota(jnp.int32, (pad, px), 0) == 0).astype(f32).astype(bf16)

    def column(k):
        return vecT[:, k : k + 1]

    def natural(matrix_t):
        return jnp.transpose(matrix_t.astype(f32))

    def stats(v):
        mean = jnp.sum(v, axis=0, keepdims=True) * (1.0 / ch)
        cen = v - mean
        var = jnp.sum(cen * cen, axis=0, keepdims=True) * (1.0 / ch)
        inv = lax.rsqrt(var + eps_norm)
        return cen * inv, inv

    def ln_back(grad, u, inv, gain):
        t = grad * gain
        mean_t = jnp.sum(t, axis=0, keepdims=True) * (1.0 / ch)
        mean_tu = jnp.sum(t * u, axis=0, keepdims=True) * (1.0 / ch)
        return inv * (t - mean_t - u * mean_tu)

    def lane_fold(v):
        out = v[:, :LANE]
        for k in range(1, v.shape[1] // LANE):
            out = out + v[:, k * LANE : (k + 1) * LANE]
        return out

    gyf = gy_rows.astype(f32)
    keep = jnp.where(edge, 0.0, 1.0).astype(f32)
    col = lax.broadcasted_iota(jnp.int32, (1, image_side, ch), 1)
    for j in range(3):
        shifted = roll_cols(gyf, SHIFT + 1 - j)
        if j == 0:
            shifted = jnp.where(col == image_side - SHIFT - 1, 0.0, shifted)
        if j == 2:
            shifted = jnp.where(col == image_side - SHIFT, 0.0, shifted)
        for i in range(3):
            rows = [shifted[r + 2 - i : r + 3 - i] for r in range(WIN)]
            if i == 0:
                rows[SHIFT - 1] = rows[SHIFT - 1] * keep
            if i == 2:
                rows[SHIFT] = rows[SHIFT] * keep
            tap = 3 * i + j
            g9[:, tap * TAP : tap * TAP + ch] = to_tokens(jnp.concatenate(rows, axis=0)).astype(bf16)

    x_tok = to_tokens(roll_cols(x_rows.astype(f32), SHIFT)).astype(bf16)
    xT = nt(eye[...], x_tok)
    xT_s[...] = xT
    u1, inv1 = stats(xT)
    aT = (u1 * column(0) + column(1)).astype(bf16)
    a_aug[:ch, :] = aT
    scale = (ch // 6) ** (-0.5)
    qt_s[...] = ((nn(wqT[...], aT) + column(2)) * scale).astype(bf16).astype(f32)
    kT = nn(wkT[...], aT).astype(bf16).astype(f32)
    vT = (nn(wvT[...], aT) + column(3)).astype(bf16).astype(f32)
    kt_s[...] = kT
    vt_s[...] = vT
    kv_s[0] = jnp.transpose(kT).astype(bf16)
    kv_s[1] = jnp.transpose(vT).astype(bf16)

    def dup(slab):
        other = pltpu.roll(slab, TOK, 1)
        return (
            (slab * masks[0] + other * masks[1]).astype(bf16),
            (other * masks[0] + slab * masks[1]).astype(bf16),
        )

    def spread(slab):
        other = pltpu.roll(slab, TOK, 1)
        first = jnp.concatenate(
            [slab * masks[2] + other * masks[3], (slab * masks[4])[:, :TOK]], axis=1
        ).astype(bf16)
        second = jnp.concatenate(
            [other * masks[2] + slab * masks[3], (other * masks[4])[:, :TOK]], axis=1
        ).astype(bf16)
        return first, second

    def merge(one, two):
        lane = lax.broadcasted_iota(jnp.int32, (ch, LANE), 1)
        crossed = pltpu.roll(jnp.where(lane < TOK, two, one), TOK, 1)
        return jnp.where(masks[0] > 0.5, one, jnp.where(masks[1] > 0.5, two, crossed))

    def by_pair(rows):
        return jnp.concatenate([rows * pmask[p].astype(bf16) for p in range(3)], axis=0)

    def pick_pair(stacked):
        return (
            stacked[:TOK] * pmask[0] + stacked[TOK : 2 * TOK] * pmask[1] + stacked[2 * TOK :] * pmask[2]
        )

    key = lax.broadcasted_iota(jnp.int32, (TOK, LANE), 0)
    key_row = base_row + (key >> 3)
    key_row = jnp.where(key_row >= image_side, key_row - image_side, key_row)
    out_row = key_row >= valid
    edge_f = jnp.where(edge, neg_mask, 0.0).astype(f32)
    for pp in range(pairs):
        cols = slice(pp * LANE, (pp + 1) * LANE)
        q_pair = dup(qt_s[:, cols])
        v_pair = spread(vt_s[:, cols])
        mixed = []
        for half in range(2):
            w = 2 * pp + half
            qeo_s[w] = q_pair[half]
            s = nn(by_pair(kv_s[0, w * TOK : (w + 1) * TOK, :]), q_pair[half])
            key_col = (key & 7) + (w * WIN + SHIFT)
            if w == 2 * pairs - 1:
                key_col = jnp.where(key_col >= image_side, key_col - image_side, key_col)
                apart = rowmask[...] * edge_f
                apart = jnp.where(colmask[...] > 0.5, neg_mask, apart)
            else:
                apart = rowmask[...] * edge_f
            extra = apart + jnp.where(out_row | (key_col >= valid), neg_mask, 0.0)
            s = s.reshape(3, TOK, LANE) + bias_ref[...] + extra[None]
            top = jnp.max(s, axis=1, keepdims=True)
            e = jnp.exp(s - top)
            p = e / jnp.sum(e, axis=1, keepdims=True)
            p = p.reshape(3 * TOK, LANE)
            p_s[w] = p
            pb = p.astype(bf16)
            pb_s[w] = pb
            mixed.append(nn(v_pair[half], pb))
        o_aug[:ch, cols] = merge(*mixed).astype(bf16)

    first = xT_s[...] + (nn(wpT[...], o_aug[:ch, :]) + column(4))
    u2, inv2 = stats(first)
    u2_s[...] = u2
    mT = (u2 * column(5) + column(6)).astype(bf16)
    m_aug[:ch, :] = mT
    hidden = nn(w1T[...], mT) + b1T[...]
    cdf = 0.5 * (1.0 + lax.erf(hidden * 0.7071067811865476))
    g_aug[...] = (hidden * cdf).astype(bf16)
    slope_s[...] = cdf + hidden * jnp.exp(-0.5 * hidden * hidden) * 0.3989422804014327
    second = first + (nn(w2T[...], g_aug[...]) + column(9))
    cT = second.astype(bf16)
    c_aug[:ch, :] = cT
    c_out[0] = roll_cols(from_tokens(natural(cT)), -SHIFT).astype(bf16)

    dsecond = nt(wc[...], g9[...])
    acc_conv[...] += nn(c_aug[...], g9[...])
    dbT = dsecond.astype(bf16)
    acc_fc2[...] += nt(dbT, g_aug[...])
    acc_ln[4] += lane_fold(dbT.astype(f32))
    dhT = (nn(w2[...], dbT) * slope_s[...]).astype(bf16)
    acc_fc1[...] += nt(m_aug[...], dhT)
    dm = nn(w1[...], dhT)
    u2 = u2_s[...]
    acc_ln[2] += lane_fold(dm * u2)
    acc_ln[3] += lane_fold(dm)
    dfirst = dsecond + ln_back(dm, u2, inv2, column(5))
    first_s[...] = dfirst
    datT = dfirst.astype(bf16)
    acc_proj[...] += nt(o_aug[...], datT)
    dat_s[...] = nn(wp[...], datT).astype(bf16).astype(f32)

    rel_sum = jnp.zeros((3 * TOK, LANE), f32)
    for pp in range(pairs):
        cols = slice(pp * LANE, (pp + 1) * LANE)
        do_pair = dup(dat_s[:, cols])
        k_pair = spread(kt_s[:, cols])
        dq = []
        for half in range(2):
            w = 2 * pp + half
            toks = slice(w * TOK, (w + 1) * TOK)
            dv = pick_pair(nt(pb_s[w], do_pair[half]))
            dp = nn(by_pair(kv_s[1, toks, :]), do_pair[half])
            p = p_s[w].reshape(3, TOK, LANE)
            dp = dp.reshape(3, TOK, LANE)
            ds = p * (dp - jnp.sum(p * dp, axis=1, keepdims=True))
            ds = ds.reshape(3 * TOK, LANE).astype(bf16)
            rel_sum = rel_sum + ds.astype(f32)
            dk = pick_pair(nt(ds, qeo_s[w]))
            dq.append(nn(k_pair[half], ds))
            dkv_s[0, toks, :] = dk.astype(bf16)
            dkv_s[1, toks, :] = dv.astype(bf16)
        dq_s[:, cols] = merge(*dq).astype(bf16)
    acc_rel[...] += rel_sum

    dqT = dq_s[...]
    acc_qkv[0] += nt(a_aug[...], dqT) * scale
    acc_qkv[1] += nn(a_aug[...], dkv_s[0])
    acc_qkv[2] += nn(a_aug[...], dkv_s[1])
    da = nn(wq[...], dqT) * scale + (nt(wk[...], dkv_s[0]) + nt(wv[...], dkv_s[1]))
    u1, inv1 = stats(xT_s[...])
    acc_ln[0] += lane_fold(da * u1)
    acc_ln[1] += lane_fold(da)
    ig = first_s[...] + ln_back(da, u1, inv1, column(0))
    ig_out[0] = roll_cols(from_tokens(jnp.transpose(ig)), -SHIFT) + gyf[1 : 1 + WIN]


N_ACC = 7
N_WTS = 7


def inner_kernel(image_side, own_rows, info, x_ref, gy_ref, *refs):
    wts, refs = refs[:N_WTS], refs[N_WTS:]
    c_out, ig_out, refs = refs[0], refs[1], refs[2:]
    acc, refs = refs[:N_ACC], refs[N_ACC:]
    prep, tmp = refs[:20], refs[20:]
    image, row_block = pl.program_id(0), pl.program_id(1)
    first_step = (image == 0) & (row_block == 0)

    @pl.when(first_step)
    def _():
        for ref in acc:
            ref[...] = jnp.zeros_like(ref)

    start = row_block * WIN + SHIFT
    x_rows = x_ref[0, pl.ds(start, WIN)]
    gy_rows = gy_ref[0, pl.ds(start - 1, WIN + 2)]
    base_row = info[0] * own_rows + start
    block_step(
        x_rows, gy_rows, first_step, False, base_row, info[2 + image], image_side, wts, prep, acc, tmp, c_out, ig_out
    )


def last_kernel(image_side, own_rows, info, x_ref, gy_ref, xh_ref, gyh_ref, *refs):
    wts, refs = refs[:N_WTS], refs[N_WTS:]
    acc_in, refs = refs[:N_ACC], refs[N_ACC:]
    sr_ref, hr_ref, c_out, ig_out, pack_out, refs = *refs[:5], refs[5:]
    acc, refs = refs[:N_ACC], refs[N_ACC:]
    prep, tmp = refs[:20], refs[20:]
    image = pl.program_id(0)
    first_step = image == 0

    @pl.when(first_step)
    def _():
        for ref, given in zip(acc, acc_in):
            ref[...] = given[...]

    x_rows = jnp.concatenate([x_ref[0, SHIFT:], xh_ref[0]], axis=0)
    gy_rows = jnp.concatenate([gy_ref[0, SHIFT - 1 :], gyh_ref[0]], axis=0)
    base_row = info[0] * own_rows + own_rows - SHIFT
    block_step(
        x_rows, gy_rows, first_step, info[1] == 1, base_row, info[2 + image], image_side, wts, prep, acc, tmp, c_out, ig_out
    )

    @pl.when(image == pl.num_programs(0) - 1)
    def _():
        pack_gradients(info[2 + pl.num_programs(0)], acc, sr_ref, hr_ref, pack_out)


def pack_rows(ch):
    up = -(-ch // 8) * 8
    blocks = 17
    vec_at = (blocks + (blocks + 1) // 2) * up
    return up, blocks, vec_at, vec_at + 32, vec_at + 32 + 3 * TOK


def pack_gradients(device, acc, sr_ref, hr_ref, out):
    (acc_conv, acc_qkv, acc_proj, acc_fc1, acc_fc2, acc_ln, acc_rel) = acc
    ch = acc_fc2.shape[0]
    up, count, vec_at, rel_at, used = pack_rows(ch)
    rest = ch - LANE
    out[used:, :] = jnp.zeros((out.shape[0] - used, LANE), f32)
    out[rel_at:used, :] = acc_rel[...]
    blocks = [acc_conv[:ch, t * TAP : t * TAP + ch] for t in range(9)]
    blocks += [acc_qkv[k, :ch, :] for k in range(3)]
    blocks += [acc_proj[:ch, :]]
    blocks += [acc_fc1[:ch, :ch], acc_fc1[:ch, ch:]]
    blocks += [acc_fc2[:, :ch], acc_fc2[:, ch:]]
    out[:vec_at, :] = jnp.zeros((vec_at, LANE), f32)
    for k, block in enumerate(blocks):
        out[k * up : k * up + ch, :] = block[:, :LANE]
        at = (count + k // 2) * up
        half = (k % 2) * TOK
        out[at : at + ch, half : half + rest] = block[:, LANE:]
    ln = [jnp.sum(jnp.transpose(acc_ln[k]), axis=0, keepdims=True) for k in range(5)]
    vec = [
        ln[0],
        ln[1],
        acc_qkv[0, ch : ch + 1, :],
        acc_qkv[2, ch : ch + 1, :],
        acc_proj[ch : ch + 1, :],
        ln[2],
        ln[3],
        acc_fc1[ch : ch + 1, :ch],
        acc_fc1[ch : ch + 1, ch:],
        ln[4],
        acc_conv[ch : ch + 1, 4 * TAP : 4 * TAP + ch],
    ]
    vec = jnp.concatenate(vec, axis=0)
    diff = sr_ref[...] - hr_ref[...]
    luma = (65.481 * diff[:, 0] + 128.553 * diff[:, 1] + 24.966 * diff[:, 2]) / 255.0
    square = jnp.sum(luma * luma, axis=1, keepdims=True)
    mse = jnp.sum(square, axis=2, keepdims=True) * (1.0 / (luma.shape[1] * luma.shape[2]))
    psnr = jnp.sum(jnp.log(mse + 1e-06) * (-10.0 / 2.302585092994046), axis=0)
    out[vec_at : vec_at + 32, :] = jnp.zeros((32, LANE), f32)
    out[vec_at : vec_at + 11, :] = vec[:, :LANE]
    lane = lax.broadcasted_iota(jnp.int32, (1, LANE), 1)
    for k in range(3):
        piece = psnr.astype(bf16).astype(f32)
        out[vec_at + 11 + k : vec_at + 12 + k, :] = jnp.where(lane == device, piece, 0.0)
        psnr = psnr - piece
    out[vec_at + 16 : vec_at + 27, :rest] = vec[:, LANE:]


def whole(shape):
    return pl.BlockSpec(shape, lambda *_: (0,) * len(shape))


def acc_shapes(ch, hid):
    up = lambda n: -(-(n + 1) // 16) * 16
    return [
        (up(ch), 9 * TAP),
        (3, up(ch), ch),
        (up(ch), ch),
        (up(ch), hid),
        (ch, hid),
        (5, ch, LANE),
        (3 * TOK, LANE),
    ]


def scratches(ch, hid, px, vec_rows):
    up = lambda n: -(-(n + 1) // 16) * 16
    v = pltpu.VMEM
    prep = [
        v((ch, vec_rows), f32),
        v((ch, ch), bf16), v((ch, ch), bf16), v((ch, ch), bf16), v((ch, ch), bf16),
        v((hid, ch), bf16), v((ch, hid), bf16),
        v((ch, ch), bf16), v((ch, ch), bf16), v((ch, ch), bf16), v((ch, ch), bf16),
        v((ch, hid), bf16), v((hid, ch), bf16),
        v((ch, 9 * TAP), bf16),
        v((5, ch, LANE), f32),
        v((3, TOK, ch), f32),
        v((TOK, LANE), f32),
        v((TOK, LANE), f32),
        v((ch, ch), bf16),
        v((hid, 1), f32),
    ]
    wins = px // TOK
    tmp = [
        v((px, 9 * TAP), bf16),
        v((up(ch), px), bf16), v((up(ch), px), bf16), v((up(ch), px), bf16), v((hid, px), bf16), v((up(ch), px), bf16),
        v((wins, ch, LANE), bf16),
        v((wins, 3 * TOK, LANE), f32),
        v((wins, 3 * TOK, LANE), bf16),
        v((2, px, ch), bf16),
        v((ch, px), f32),
        v((ch, px), f32),
        v((ch, px), bf16),
        v((2, px, ch), bf16),
        v((ch, px), f32),
        v((ch, px), f32),
        v((hid, px), f32),
        v((ch, px), f32),
        v((ch, px), f32),
        v((ch, px), f32),
    ]
    return prep + tmp


def conv_kernel(image_side, own_rows, info, hc_ref, c1_ref, c2_ref, hg_ref, g1_ref, g2_ref, x_ref, vec_ref, conv_ref, out_ref, ig_ref, cs, wc):
    ch = x_ref.shape[3]

    @pl.when(pl.program_id(0) == 0)
    def _():
        wc[...] = jnp.zeros_like(wc)
        cs[...] = jnp.zeros_like(cs)
        for tap in range(9):
            wc[tap * TAP : tap * TAP + ch, :] = conv_ref[tap // 3, tap % 3].astype(bf16)

    first = jnp.where(info[0] == 0, 0.0, 1.0).astype(f32)
    last = jnp.where(info[1] == 1, 0.0, 1.0).astype(f32)
    need = own_rows + 2
    col = lax.broadcasted_iota(jnp.int32, (1, image_side, ch), 1)
    halo = hc_ref.shape[1]
    for r in range(need):
        if r < halo:
            row = hc_ref[0, r : r + 1]
        elif r - halo < c1_ref.shape[1]:
            row = c1_ref[0, r - halo : r - halo + 1]
        else:
            at = r - halo - c1_ref.shape[1]
            row = c2_ref[0, at : at + 1]
        row = row.astype(f32)
        if r == 0:
            row = row * first
        if r == need - 1:
            row = row * last
        left = jnp.where(col == 0, 0.0, roll_cols(row, -1))
        right = jnp.where(col == image_side - 1, 0.0, roll_cols(row, 1))
        at = slice(r * image_side, (r + 1) * image_side)
        cs[at, 0:ch] = left[0].astype(bf16)
        cs[at, TAP : TAP + ch] = row[0].astype(bf16)
        cs[at, 2 * TAP : 2 * TAP + ch] = right[0].astype(bf16)
    group = 4
    bias = vec_ref[10:11, :]
    for r in range(0, own_rows, group):
        total = None
        for i in range(3):
            at = slice((r + i) * image_side, (r + i + group) * image_side)
            term = nn(cs[at, :], wc[i * 3 * TAP : (i + 1) * 3 * TAP, :])
            total = term if total is None else total + term
        total = total + bias
        total = total.reshape(group, image_side, ch) + x_ref[0, r : r + group].astype(f32)
        out_ref[0, r : r + group] = total.astype(bf16)
    head = hg_ref.shape[1]
    mid = g1_ref.shape[1]
    ig_ref[0, :head] = hg_ref[0]
    ig_ref[0, head : head + mid] = g1_ref[0]
    ig_ref[0, head + mid :] = g2_ref[0, : own_rows - head - mid]


def split_bits(size):
    return [b for b in range(size.bit_length() - 1)]


def exchange_kernel(stages, g_ref, out_ref, work, given, low, send_sem, recv_sem):
    rows = g_ref.shape[0]

    def meet(stage):
        axis, b = stage
        me = lax.axis_index(axis)
        step = 2**b
        bit = (me // step) % 2
        return {axis: me + (1 - 2 * bit) * step}, bit

    barrier = pltpu.get_barrier_semaphore()
    for stage in stages:
        other, _ = meet(stage)
        pl.semaphore_signal(barrier, inc=1, device_id=other, device_id_type=pl.DeviceIdType.MESH)
    pl.semaphore_wait(barrier, len(stages))

    def span(start, size):
        return pl.ds(pl.multiple_of(start, 16), size)

    start = 0
    size = rows
    starts = []
    taken = 0
    for s, stage in enumerate(stages):
        other, bit = meet(stage)
        size = size // 2
        starts.append(start)
        keep = start + bit * size
        give = start + (1 - bit) * size
        source = g_ref if s == 0 else work
        copy = pltpu.make_async_remote_copy(
            src_ref=source.at[span(give, size)],
            dst_ref=given.at[pl.ds(taken, size)],
            send_sem=send_sem.at[s],
            recv_sem=recv_sem.at[s],
            device_id=other,
            device_id_type=pl.DeviceIdType.MESH,
        )
        copy.start()
        copy.wait()
        total = source[span(keep, size), :] + given[taken : taken + size, :]
        if s < len(stages) - 1:
            work[span(keep, size), :] = total
        else:
            low[span(keep, size), :] = total.astype(bf16)
        taken += size
        start = keep
    for s in reversed(range(len(stages))):
        other, bit = meet(stages[s])
        n = len(stages) + s
        copy = pltpu.make_async_remote_copy(
            src_ref=low.at[span(start, size)],
            dst_ref=low.at[span(start, size)],
            send_sem=send_sem.at[n],
            recv_sem=recv_sem.at[n],
            device_id=other,
            device_id_type=pl.DeviceIdType.MESH,
        )
        copy.start()
        copy.wait()
        start = starts[s]
        size = size * 2
    out_ref[...] = low[...]


def reduce_all(packed, sizes):
    stages = [(axis, b) for axis, size in sizes for b in split_bits(size)]
    rows = packed.shape[0]
    vmem = pl.BlockSpec(memory_space=pltpu.VMEM)
    return pl.pallas_call(
        functools.partial(exchange_kernel, stages),
        in_specs=[vmem],
        out_specs=vmem,
        out_shape=jax.ShapeDtypeStruct(packed.shape, bf16),
        scratch_shapes=[
            pltpu.VMEM(packed.shape, f32),
            pltpu.VMEM(packed.shape, f32),
            pltpu.VMEM(packed.shape, bf16),
            pltpu.SemaphoreType.DMA((2 * len(stages),)),
            pltpu.SemaphoreType.DMA((2 * len(stages),)),
        ],
        compiler_params=pltpu.CompilerParams(
            collective_id=0, has_side_effects=True, vmem_limit_bytes=40 * 1024 * 1024
        ),
        name="sum_gradients",
    )(packed)


def adam_kernel(scal, g_ref, *refs):
    weights, firsts, seconds = refs[0:7], refs[7:14], refs[14:21]
    norm_ref, psnr_ref, outs = refs[21], refs[22], refs[23:44]
    ch = weights[2].shape[0]
    up, count, vec_at, rel_at, used = pack_rows(ch)
    rest = ch - LANE

    def block(k):
        left = g_ref[k * up : (k + 1) * up, :].astype(f32)
        at = (count + k // 2) * up
        right = g_ref[at : at + up, :].astype(f32)
        if k % 2:
            right = pltpu.roll(right, TOK, 1)
        return jnp.concatenate([left, right[:, :rest]], axis=1)[:ch]

    vec_rows = g_ref[vec_at : vec_at + 32, :].astype(f32)
    vec = jnp.concatenate([vec_rows[:11], vec_rows[16:27, :rest]], axis=1)
    psnr = vec_rows[11:12] + vec_rows[12:13] + vec_rows[13:14]
    psnr_ref[...] = jnp.sum(psnr, axis=1, keepdims=True)

    span = 2 * WIN
    wide = span * span
    at = lax.broadcasted_iota(jnp.int32, (TOK, wide), 0)
    to = lax.broadcasted_iota(jnp.int32, (TOK, wide), 1)
    place = ((at >> 3) + (WIN - 1)) * span + (at & 7) + (WIN - 1)
    expand = (to == place).astype(f32).astype(bf16)
    pairs = g_ref[rel_at:used, :]
    rel_rows = []
    for p in range(3):
        for parity in range(2):
            part = pairs[p * TOK : (p + 1) * TOK, :].astype(f32)
            if parity:
                part = pltpu.roll(part, TOK, 1)
            spread = nn(part[:, :TOK].astype(bf16), expand)
            total = jnp.zeros((WIN, wide), f32)
            for row in range(WIN):
                piece = spread[row * WIN : (row + 1) * WIN]
                piece = pltpu.roll(piece, (wide - span * row) % wide, 1)
                total = total + piece
            line = total[0:1]
            for c in range(1, WIN):
                line = line + pltpu.roll(total, wide - c, 1)[c : c + 1]
            rel_rows.append(line)
    rel = jnp.concatenate(rel_rows, axis=0)
    rel = jnp.concatenate(
        [rel[:, k * span : k * span + span - 1] for k in range(span - 1)], axis=1
    )
    qkv = jnp.concatenate([block(9), block(10), block(11)], axis=1)
    fc1 = jnp.concatenate([block(13), block(14)], axis=1)
    fc2 = jnp.concatenate([block(15), block(16)], axis=1)
    small = [vec, qkv, block(12), rel, fc1, fc2]
    taps = [block(t) for t in range(9)]
    total = jnp.zeros((1, 1), f32)
    for g in small + taps:
        total = total + jnp.sum(jnp.sum(g * g, axis=0, keepdims=True), axis=1, keepdims=True)
    norm = jnp.sqrt(total)
    norm_ref[...] = norm
    clip = jnp.minimum(1.0, max_norm / (norm + 1e-06))
    fix_one, fix_two = scal[0], scal[1]

    def update(w, m1, m2, g, rate):
        g = g * clip
        m1 = beta_one * m1 + (1.0 - beta_one) * g
        m2 = beta_two * m2 + (1.0 - beta_two) * g * g
        step = (m1 / fix_one) / (jnp.sqrt(m2 / fix_two) + adam_eps)
        return w - rate * (step + decay_rate * w), m1, m2

    for k, g in enumerate(small):
        new = update(weights[k][...], firsts[k][...], seconds[k][...], g, vector_rate if k == 0 else learn_rate)
        for ref, value in zip(outs[3 * k : 3 * k + 3], new):
            ref[...] = value
    for t, g in enumerate(taps):
        at = (t // 3, t % 3)
        new = update(weights[6][at], firsts[6][at], seconds[6][at], g, learn_rate)
        for ref, value in zip(outs[18:21], new):
            ref[at] = value


def relative_onehot_keys_first():
    position = np.arange(TOK)
    pos_row, pos_col = position // WIN, position % WIN
    span = 2 * WIN - 1
    index = (pos_row[None, :] - pos_row[:, None] + WIN - 1) * span + (
        pos_col[None, :] - pos_col[:, None] + WIN - 1
    )
    return index.reshape(-1), span * span


def on_device(
    images, cotangent, valid_size,
    vectors, vectors_first, vectors_second,
    qkv_weight, qkv_first, qkv_second,
    proj_weight, proj_first, proj_second,
    rel_table, rel_first, rel_second,
    fc1_weight, fc1_first, fc1_second,
    fc2_weight, fc2_first, fc2_second,
    conv_weight, conv_first, conv_second,
    step, sr_crops, hr_crops, psnr_running,
):
    count, own_rows, image_side, ch = images.shape
    hid = fc1_weight.shape[1]
    px = image_side * WIN
    blocks = own_rows // WIN
    heads = lax.axis_size("head")
    place = lax.axis_index("head")
    to_lower = [((i + 1) % heads, i) for i in range(heads)]
    to_upper = [(i, (i + 1) % heads) for i in range(heads)]
    info = jnp.concatenate(
        [
            jnp.stack([place, (place == heads - 1).astype(jnp.int32)]).astype(jnp.int32),
            valid_size.astype(jnp.int32),
            ((lax.axis_index("dp") * heads + place) % LANE)[None].astype(jnp.int32),
        ]
    )
    halo = lax.ppermute(
        jnp.concatenate([images[:, :SHIFT], cotangent[:, : SHIFT + 1]], axis=1), "head", to_lower
    )
    x_halo, gy_halo = halo[:, :SHIFT], halo[:, SHIFT:]

    index, span = relative_onehot_keys_first()
    onehot = (jnp.asarray(index)[:, None] == jnp.arange(span)[None, :]).astype(f32)
    bias = jnp.dot(onehot, rel_table, precision=highest)
    bias = bias.reshape(TOK, TOK, 3, 2).transpose(2, 0, 3, 1).reshape(3, TOK, LANE)

    wts = (vectors, qkv_weight, proj_weight, fc1_weight, fc2_weight.T, conv_weight, bias)
    wts_specs = [whole(w.shape) for w in wts]
    acc_dims = acc_shapes(ch, hid)
    acc_types = [jax.ShapeDtypeStruct(s, f32) for s in acc_dims]
    smem = pl.BlockSpec(memory_space=pltpu.SMEM)
    params = pltpu.CompilerParams(
        dimension_semantics=("arbitrary", "arbitrary"), vmem_limit_bytes=60 * 1024 * 1024
    )
    c1, ig1, *acc = pl.pallas_call(
        functools.partial(inner_kernel, image_side, own_rows),
        grid=(count, blocks - 1),
        in_specs=[
            smem,
            pl.BlockSpec((1, own_rows, image_side, ch), lambda n, r: (n, 0, 0, 0)),
            pl.BlockSpec((1, own_rows, image_side, ch), lambda n, r: (n, 0, 0, 0)),
            *wts_specs,
        ],
        out_specs=[
            pl.BlockSpec((1, WIN, image_side, ch), lambda n, r: (n, r, 0, 0)),
            pl.BlockSpec((1, WIN, image_side, ch), lambda n, r: (n, r, 0, 0)),
            *[whole(s) for s in acc_dims],
        ],
        out_shape=[
            jax.ShapeDtypeStruct((count, own_rows - WIN, image_side, ch), bf16),
            jax.ShapeDtypeStruct((count, own_rows - WIN, image_side, ch), f32),
            *acc_types,
        ],
        scratch_shapes=scratches(ch, hid, px, vectors.shape[0]),
        compiler_params=params,
        name="inner_windows",
    )(info, images, cotangent, *wts)
    device_count = lax.axis_size("dp") * heads
    unit = 16 * device_count
    rows = -(-pack_rows(ch)[-1] // unit) * unit
    c2, ig2, packed = pl.pallas_call(
        functools.partial(last_kernel, image_side, own_rows),
        grid=(count,),
        in_specs=[
            smem,
            pl.BlockSpec((1, WIN, image_side, ch), lambda n: (n, blocks - 1, 0, 0)),
            pl.BlockSpec((1, WIN, image_side, ch), lambda n: (n, blocks - 1, 0, 0)),
            pl.BlockSpec((1, SHIFT, image_side, ch), lambda n: (n, 0, 0, 0)),
            pl.BlockSpec((1, SHIFT + 1, image_side, ch), lambda n: (n, 0, 0, 0)),
            *wts_specs,
            *[whole(s) for s in acc_dims],
            whole(sr_crops.shape),
            whole(hr_crops.shape),
        ],
        out_specs=[
            pl.BlockSpec((1, WIN, image_side, ch), lambda n: (n, 0, 0, 0)),
            pl.BlockSpec((1, WIN, image_side, ch), lambda n: (n, 0, 0, 0)),
            whole((rows, LANE)),
        ],
        out_shape=[
            jax.ShapeDtypeStruct((count, WIN, image_side, ch), bf16),
            jax.ShapeDtypeStruct((count, WIN, image_side, ch), f32),
            jax.ShapeDtypeStruct((rows, LANE), f32),
        ],
        scratch_shapes=[pltpu.VMEM(s, f32) for s in acc_dims] + scratches(ch, hid, px, vectors.shape[0]),
        compiler_params=pltpu.CompilerParams(
            dimension_semantics=("arbitrary",), vmem_limit_bytes=60 * 1024 * 1024
        ),
        name="last_windows",
    )(info, images, cotangent, x_halo, gy_halo, *wts, *acc, sr_crops, hr_crops)

    c_halo = lax.ppermute(c2[:, WIN - SHIFT - 1 :], "head", to_upper)
    ig_halo = lax.ppermute(ig2[:, WIN - SHIFT :], "head", to_upper)

    summed = reduce_all(packed, (("dp", lax.axis_size("dp")), ("head", heads)))

    image_block = lambda size: pl.BlockSpec((1, size, image_side, ch), lambda n: (n, 0, 0, 0))
    output, image_grad = pl.pallas_call(
        functools.partial(conv_kernel, image_side, own_rows),
        grid=(count,),
        in_specs=[
            smem,
            image_block(SHIFT + 1), image_block(own_rows - WIN), image_block(WIN),
            image_block(SHIFT), image_block(own_rows - WIN), image_block(WIN),
            image_block(own_rows),
            whole(vectors.shape), whole(conv_weight.shape),
        ],
        out_specs=[image_block(own_rows), image_block(own_rows)],
        out_shape=[
            jax.ShapeDtypeStruct(images.shape, bf16),
            jax.ShapeDtypeStruct(images.shape, f32),
        ],
        scratch_shapes=[
            pltpu.VMEM(((own_rows + 2) * image_side, 3 * TAP), bf16),
            pltpu.VMEM((9 * TAP, ch), bf16),
        ],
        compiler_params=pltpu.CompilerParams(
            dimension_semantics=("arbitrary",), vmem_limit_bytes=60 * 1024 * 1024
        ),
        name="conv_output",
    )(info, c_halo, c1, c2, ig_halo, ig1, ig2, images, vectors, conv_weight)

    step_count = step[0].astype(f32)
    scal = jnp.stack([1.0 - beta_one**step_count, 1.0 - beta_two**step_count])
    weights = (vectors, qkv_weight, proj_weight, rel_table.T, fc1_weight, fc2_weight.T, conv_weight)
    firsts = (vectors_first, qkv_first, proj_first, rel_first.T, fc1_first, fc2_first.T, conv_first)
    seconds = (vectors_second, qkv_second, proj_second, rel_second.T, fc1_second, fc2_second.T, conv_second)
    vmem = pl.BlockSpec(memory_space=pltpu.VMEM)
    grad_norm, psnr, *updated = pl.pallas_call(
        adam_kernel,
        in_specs=[smem] + [vmem] * 22,
        out_specs=[vmem] * 23,
        out_shape=[jax.ShapeDtypeStruct((1, 1), f32)] * 2
        + [jax.ShapeDtypeStruct(w.shape, f32) for w in weights for _ in range(3)],
        compiler_params=pltpu.CompilerParams(vmem_limit_bytes=60 * 1024 * 1024),
        name="adam",
    )(scal, summed, *weights, *firsts, *seconds)
    for k in (9, 10, 11, 15, 16, 17):
        updated[k] = updated[k].T
    psnr_total = psnr_running + psnr.reshape(1)
    return (output, image_grad, grad_norm.reshape(1), psnr_total, *updated)


def solution(mesh):
    pixels = P("dp", "head", None, None)
    crops = P(("dp", "head"), None, None, None)
    placed = (pixels, pixels, P("dp")) + (P(),) * 22 + (crops, crops, P())
    return jax.shard_map(
        on_device,
        mesh=mesh,
        in_specs=placed,
        out_specs=(pixels, pixels) + (P(),) * 23,
        check_vma=False,
    )
```

```python
import functools

import jax
import jax.numpy as jnp
import numpy as np
from jax import lax
from jax.experimental import pallas as pl
from jax.experimental.pallas import tpu as pltpu
from jax.sharding import PartitionSpec as P

WIN = 8
TOK = WIN * WIN
SHIFT = WIN // 2
LANE = 128
TAP = 256
HPAD = 32
HEADS = 6
CPAD = HEADS * HPAD

eps_norm = 1e-05
neg_mask = -100.0
max_norm = 1.0
learn_rate = 0.03
vector_rate = 0.2
beta_one = 0.9
beta_two = 0.999
adam_eps = 1e-08
decay_rate = 0.01
highest = lax.Precision.HIGHEST
f32 = jnp.float32
bf16 = jnp.bfloat16


def nn(a, b):
    return lax.dot_general(a, b, (((1,), (0,)), ((), ())), preferred_element_type=f32)


def nt(a, b):
    return lax.dot_general(a, b, (((1,), (1,)), ((), ())), preferred_element_type=f32)


def pad_heads(rows, heads):
    dim = rows.shape[0] // heads
    gap = jnp.zeros((HPAD - dim, rows.shape[1]), rows.dtype)
    parts = []
    for h in range(heads):
        parts += [rows[h * dim : (h + 1) * dim], gap]
    return jnp.concatenate(parts, axis=0)


def drop_rows(rows, heads, dim):
    return jnp.concatenate([rows[h * HPAD : h * HPAD + dim] for h in range(heads)], axis=0)


def drop_lanes(rows, heads, dim):
    return jnp.concatenate([rows[:, h * HPAD : h * HPAD + dim] for h in range(heads)], axis=1)


def to_tokens(rows):
    side = rows.shape[1]
    return jnp.concatenate(
        [rows[:, w * WIN : (w + 1) * WIN, :].reshape(TOK, rows.shape[2]) for w in range(side // WIN)],
        axis=0,
    )


def from_tokens(tokens):
    count = tokens.shape[0] // TOK
    return jnp.concatenate(
        [tokens[w * TOK : (w + 1) * TOK].reshape(WIN, WIN, tokens.shape[1]) for w in range(count)],
        axis=1,
    )


def roll_cols(rows, by):
    side = rows.shape[1]
    by = by % side
    return jnp.concatenate([rows[:, by:, :], rows[:, :by, :]], axis=1)


def block_step(x_rows, gy_rows, first_step, edge, base_row, valid, image_side, wts, prep, acc, tmp, c_out):
    (vec_ref, qkv_ref, proj_ref, fc1_ref, fc2_ref, conv_ref, bias_ref) = wts
    (vecT, wqkvT, wpT, w1T, w2T, wq, wk, wv, wp, w1, w2, wcT, colmask, rowmask, b1T, wide_vec, head_vec) = prep
    (acc_conv, acc_qkv, acc_proj, acc_fc1, acc_fc2, acc_ln, acc_rel) = acc
    (g9, a_aug, o_aug, m_aug, g_aug, c_aug, qeo_s, p_s, pb_s, kv_s, first_s, do_s, dq_s, dkv_s, u2_s, xT_s, slope_s, vt_s, qt_s, kt_s, inv_s, db_s, dh_s, ds_s) = tmp
    ch = x_rows.shape[2]
    dim = ch // HEADS
    hid = fc1_ref.shape[1]
    px = x_rows.shape[1] * WIN
    pairs = px // LANE
    ones_row = dim

    @pl.when(first_step)
    def _():
        vecT[...] = jnp.transpose(vec_ref[...])
        for k in range(10):
            wide_vec[k] = jnp.broadcast_to(vecT[:, k : k + 1], (ch, LANE))
        for k in range(2):
            head_vec[k] = pad_heads(wide_vec[2 + k], HEADS)
        b1T[:ch, :] = wide_vec[7]
        b1T[ch:, :] = wide_vec[8]
        for k, dst in enumerate((wq, wk, wv)):
            part = pad_heads(jnp.transpose(qkv_ref[:, k * ch : (k + 1) * ch]), HEADS)
            wqkvT[k * CPAD : (k + 1) * CPAD, :] = part.astype(bf16)
            dst[...] = jnp.transpose(part).astype(bf16)
        padded = pad_heads(proj_ref[...], HEADS)
        wp[...] = padded.astype(bf16)
        wpT[...] = jnp.transpose(padded).astype(bf16)
        w1[...] = fc1_ref[...].astype(bf16)
        w1T[...] = jnp.transpose(fc1_ref[...]).astype(bf16)
        w2T[...] = fc2_ref[...].astype(bf16)
        w2[...] = jnp.transpose(fc2_ref[...]).astype(bf16)
        wcT[...] = jnp.zeros_like(wcT)
        g9[...] = jnp.zeros_like(g9)
        for tap in range(9):
            wcT[tap * CPAD : tap * CPAD + ch, :] = jnp.transpose(conv_ref[tap // 3, tap % 3]).astype(bf16)
        key = lax.broadcasted_iota(jnp.int32, (TOK, LANE), 0)
        query = lax.broadcasted_iota(jnp.int32, (TOK, LANE), 1) & (TOK - 1)
        one = lambda m: m.astype(f32)
        colmask[...] = one(((key & 7) < SHIFT) != ((query & 7) < SHIFT))
        rowmask[...] = one(((key >> 3) < SHIFT) != ((query >> 3) < SHIFT))
        for ref in (a_aug, m_aug, c_aug):
            pad = ref.shape[0] - ch
            ref[ch:, :] = (lax.broadcasted_iota(jnp.int32, (pad, px), 0) == 0).astype(f32).astype(bf16)

    def column(k):
        return wide_vec[k]

    def stats(v):
        mean = jnp.sum(v, axis=0, keepdims=True) * (1.0 / ch)
        cen = v - mean
        var = jnp.sum(cen * cen, axis=0, keepdims=True) * (1.0 / ch)
        inv = lax.rsqrt(var + eps_norm)
        return cen * inv, inv

    def ln_back(grad, u, inv, gain):
        t = grad * gain
        mean_t = jnp.sum(t, axis=0, keepdims=True) * (1.0 / ch)
        mean_tu = jnp.sum(t * u, axis=0, keepdims=True) * (1.0 / ch)
        return inv * (t - mean_t - u * mean_tu)

    chunks = [slice(k * LANE, (k + 1) * LANE) for k in range(px // LANE)]
    third = hid // 3
    bands = [slice(k * third, (k + 1) * third) for k in range(3)]

    keep = jnp.where(edge, 0.0, 1.0).astype(f32)
    col = lax.broadcasted_iota(jnp.int32, (1, image_side, ch), 1)
    moved = {}

    def build_tap(tap):
        i, j = tap % 3, tap // 3
        if i == 0:
            shifted = roll_cols(gy_rows, SHIFT + 1 - j)
            if j == 0:
                shifted = jnp.where(col == image_side - SHIFT - 1, 0.0, shifted)
            if j == 2:
                shifted = jnp.where(col == image_side - SHIFT, 0.0, shifted)
            moved[j] = shifted
        rows = [moved[j][r + 2 - i : r + 3 - i] for r in range(WIN)]
        if i == 0:
            rows[SHIFT - 1] = rows[SHIFT - 1] * keep
        if i == 2:
            rows[SHIFT] = rows[SHIFT] * keep
        at = (3 * i + j) * CPAD
        g9[:, at : at + ch] = to_tokens(jnp.concatenate(rows, axis=0)).astype(bf16)

    x_tok = to_tokens(roll_cols(x_rows, SHIFT))
    for at in chunks:
        xT = jnp.transpose(x_tok[at])
        xT_s[:, at] = xT
        u1, _ = stats(xT)
        a_aug[:ch, at] = (u1 * column(0) + column(1)).astype(bf16)
    scale = dim ** (-0.5)
    qkv_all = nn(wqkvT[...], a_aug[:ch, :])
    for at in chunks:
        qt_s[:, at] = ((qkv_all[:CPAD, at] + head_vec[0]) * scale).astype(bf16)
        kT = qkv_all[CPAD : 2 * CPAD, at].astype(bf16)
        vT = (qkv_all[2 * CPAD :, at] + head_vec[1]).astype(bf16)
        kt_s[:, at] = kT
        vt_s[:, at] = vT
        kv_s[0, at, :] = jnp.transpose(kT.astype(f32)).astype(bf16)
        kv_s[1, at, :] = jnp.transpose(vT.astype(f32)).astype(bf16)

    def low_lanes(rows):
        return lax.broadcasted_iota(jnp.int32, (rows, LANE), 1) < TOK

    def swap(slab):
        return pltpu.roll(slab, TOK, 1)

    def only_low(v):
        return jnp.where(low_lanes(v.shape[0]), v, jnp.zeros_like(v))

    def only_high(v):
        return jnp.where(low_lanes(v.shape[0]), jnp.zeros_like(v), v)

    def head_rows(v, h):
        return v[h * HPAD : (h + 1) * HPAD]

    def dup(slab):
        slab = slab.astype(f32)
        other = swap(slab)
        out = []
        for low, high in ((slab, other), (other, slab)):
            rows = [
                only_high(head_rows(high, h)) if h % 2 else only_low(head_rows(low, h)) for h in range(HEADS)
            ]
            out.append(jnp.concatenate(rows, axis=0).astype(bf16))
        return out

    def spread(slab):
        slab = slab.astype(f32)
        other = swap(slab)
        two = 2 * HPAD
        gap = jnp.zeros((two, TOK), f32)
        wide = jnp.zeros((two, LANE), f32)
        out = []
        for low, high in ((slab, other), (other, slab)):
            rows = [
                jnp.concatenate([only_low(low[:two]), gap], axis=1),
                jnp.concatenate([only_high(high[two : 2 * two]), gap], axis=1),
                jnp.concatenate([wide, low[2 * two :, :TOK]], axis=1),
            ]
            out.append(jnp.concatenate(rows, axis=0).astype(bf16))
        return out

    def merge(one, two):
        rows = []
        for h in range(HEADS):
            first, second = head_rows(one, h), head_rows(two, h)
            if h % 2:
                rows.append(jnp.where(low_lanes(HPAD), swap(first), second))
            else:
                rows.append(jnp.where(low_lanes(HPAD), first, swap(second)))
        return jnp.concatenate(rows, axis=0)

    def by_pair(rows):
        front, back = rows[:, :LANE], rows[:, LANE:]
        zero_back = jnp.zeros_like(back)
        return jnp.concatenate(
            [
                jnp.concatenate([only_low(front), zero_back], axis=1),
                jnp.concatenate([only_high(front), zero_back], axis=1),
                jnp.concatenate([jnp.zeros_like(front), back], axis=1),
            ],
            axis=0,
        )

    def pick_pair(stacked):
        front = jnp.where(low_lanes(TOK), stacked[:TOK, :LANE], stacked[TOK : 2 * TOK, :LANE])
        return jnp.concatenate([front, stacked[2 * TOK :, LANE:]], axis=1)

    key = lax.broadcasted_iota(jnp.int32, (TOK, LANE), 0)
    key_row = base_row + (key >> 3)
    key_row = jnp.where(key_row >= image_side, key_row - image_side, key_row)
    out_row = key_row >= valid
    edge_f = jnp.where(edge, neg_mask, 0.0).astype(f32)

    def scores_of(pp):
        q_pair = dup(qt_s[:, chunks[pp]])
        raw = []
        for half in range(2):
            w = 2 * pp + half
            qeo_s[w] = q_pair[half]
            raw.append(nn(by_pair(kv_s[0, w * TOK : (w + 1) * TOK, :]), q_pair[half]))
        return raw

    def soften(pp, raw):
        for half in range(2):
            w = 2 * pp + half
            key_col = (key & 7) + (w * WIN + SHIFT)
            apart = rowmask[...] * edge_f
            if w == 2 * pairs - 1:
                key_col = jnp.where(key_col >= image_side, key_col - image_side, key_col)
                apart = jnp.where(colmask[...] > 0.5, neg_mask, apart)
            extra = apart + jnp.where(out_row | (key_col >= valid), neg_mask, 0.0)
            s = raw[half].reshape(3, TOK, LANE) + bias_ref[...] + extra[None]
            top = jnp.max(s, axis=1, keepdims=True)
            e = jnp.exp(s - top)
            p = e / jnp.sum(e, axis=1, keepdims=True)
            p = p.reshape(3 * TOK, LANE)
            p_s[w] = p
            pb_s[w] = p.astype(bf16)

    def mix(pp):
        v_pair = spread(vt_s[:, chunks[pp]])
        return [nn(v_pair[half], pb_s[2 * pp + half]) for half in range(2)]

    def place(pp, mixed):
        o_aug[:, chunks[pp]] = merge(*mixed).astype(bf16)

    raws, mixes = {}, {}
    for t in range(pairs + 3):
        if 0 <= t - 2 < pairs:
            mixes[t - 2] = mix(t - 2)
        if t < pairs:
            raws[t] = scores_of(t)
        if 0 <= t - 1 < pairs:
            soften(t - 1, raws.pop(t - 1))
        if 0 <= t - 3 < pairs:
            place(t - 3, mixes.pop(t - 3))
        if t < 9:
            build_tap(t)
    o_aug[ones_row : ones_row + 1, :] = jnp.ones((1, px), bf16)

    attn = nn(wpT[...], o_aug[...])
    part = px // 3
    conv_back = [nn(g9[:part, :], wcT[...])]
    for at in chunks:
        first = xT_s[:, at] + (attn[:, at] + column(4))
        first_s[:, at] = first
        u2, inv2 = stats(first)
        u2_s[:, at] = u2
        inv_s[0:1, at] = inv2
        m_aug[:ch, at] = (u2 * column(5) + column(6)).astype(bf16)
    hidden_all = nn(w1T[...], m_aug[:ch, :])
    conv_back.append(nn(g9[part : 2 * part, :], wcT[...]))
    for at in chunks:
        for band in bands:
            hidden = hidden_all[band, at] + b1T[band, :]
            cdf = 0.5 * (1.0 + lax.erf(hidden * 0.7071067811865476))
            g_aug[band, at] = (hidden * cdf).astype(bf16)
            slope_s[band, at] = cdf + hidden * jnp.exp(-0.5 * hidden * hidden) * 0.3989422804014327
    branch = nn(w2T[...], g_aug[...])
    conv_back.append(nn(g9[2 * part :, :], wcT[...]))
    c_rows = []
    for at in chunks:
        cT = (first_s[:, at] + (branch[:, at] + column(9))).astype(bf16)
        c_aug[:ch, at] = cT
        c_rows.append(jnp.transpose(cT.astype(f32)))
    c_out[0] = roll_cols(from_tokens(jnp.concatenate(c_rows, axis=0)), -SHIFT).astype(bf16)

    dsecond = jnp.concatenate(conv_back, axis=0)
    for at in chunks:
        ds_chunk = jnp.transpose(dsecond[at])
        ds_s[:, at] = ds_chunk
        dbT = ds_chunk.astype(bf16)
        db_s[:, at] = dbT
        acc_ln[4] += dbT.astype(f32)
    dg = nn(w2[...], db_s[...])
    acc_fc2[...] += nt(g_aug[...], db_s[...])
    for at in chunks:
        for band in bands:
            dh_s[band, at] = (dg[band, at] * slope_s[band, at]).astype(bf16)
    dm_all = nn(w1[...], dh_s[...])
    acc_fc1[...] += nt(dh_s[...], m_aug[...])
    for at in chunks:
        u2 = u2_s[:, at]
        dm = dm_all[:, at]
        acc_ln[2] += dm * u2
        acc_ln[3] += dm
        dfirst = ds_s[:, at] + ln_back(dm, u2, inv_s[0:1, at], column(5))
        first_s[:, at] = dfirst
        db_s[:, at] = dfirst.astype(bf16)
    do_all = nn(wp[...], db_s[...])
    acc_proj[...] += nt(o_aug[...], db_s[...])
    for at in chunks:
        do_s[:, at] = do_all[:, at].astype(bf16)

    rel_sum = jnp.zeros((3 * TOK, LANE), f32)

    def probs_grad(pp):
        do_pair = dup(do_s[:, chunks[pp]])
        dps, dvs = [], []
        for half in range(2):
            w = 2 * pp + half
            dps.append(nn(by_pair(kv_s[1, w * TOK : (w + 1) * TOK, :]), do_pair[half]))
            dvs.append(nt(pb_s[w], do_pair[half]))
        return dps, dvs

    def scores_grad(pp, dps, dvs, rel_sum):
        out = []
        for half in range(2):
            w = 2 * pp + half
            p = p_s[w].reshape(3, TOK, LANE)
            dp = dps[half].reshape(3, TOK, LANE)
            ds = p * (dp - jnp.sum(p * dp, axis=1, keepdims=True))
            ds = ds.reshape(3 * TOK, LANE).astype(bf16)
            rel_sum = rel_sum + ds.astype(f32)
            out.append(ds)
            dkv_s[1, w * TOK : (w + 1) * TOK, :] = pick_pair(dvs[half]).astype(bf16)
        return out, rel_sum

    def inner_grads(pp, ds):
        k_pair = spread(kt_s[:, chunks[pp]])
        dks = [nt(ds[half], qeo_s[2 * pp + half]) for half in range(2)]
        dqs = [nn(k_pair[half], ds[half]) for half in range(2)]
        return dks, dqs

    def place_grads(pp, dks, dqs):
        for half in range(2):
            w = 2 * pp + half
            dkv_s[0, w * TOK : (w + 1) * TOK, :] = pick_pair(dks[half]).astype(bf16)
        dq_s[:, chunks[pp]] = merge(*dqs).astype(bf16)

    first_part, second_part, third_part = {}, {}, {}
    for t in range(pairs + 3):
        if 0 <= t - 2 < pairs:
            third_part[t - 2] = inner_grads(t - 2, second_part.pop(t - 2))
        if t < pairs:
            first_part[t] = probs_grad(t)
        if 0 <= t - 1 < pairs:
            second_part[t - 1], rel_sum = scores_grad(t - 1, *first_part.pop(t - 1), rel_sum)
        if 0 <= t - 3 < pairs:
            place_grads(t - 3, *third_part.pop(t - 3))
        at = slice(t * TAP, min((t + 1) * TAP, 9 * CPAD))
        if at.start < at.stop:
            acc_conv[:, at] += nn(c_aug[...], g9[:, at])
    acc_rel[...] += rel_sum

    dqT = dq_s[...]
    da_q = nn(wq[...], dqT)
    da_kv = nt(wk[...], dkv_s[0]) + nt(wv[...], dkv_s[1])
    acc_qkv[0] += nt(a_aug[...], dqT) * scale
    acc_qkv[1] += nn(a_aug[...], dkv_s[0])
    acc_qkv[2] += nn(a_aug[...], dkv_s[1])
    ig_rows = []
    for at in chunks:
        da = da_q[:, at] * scale + da_kv[:, at]
        u1, inv1 = stats(xT_s[:, at])
        acc_ln[0] += da * u1
        acc_ln[1] += da
        ig_rows.append(jnp.transpose(first_s[:, at] + ln_back(da, u1, inv1, column(0))))
    return roll_cols(from_tokens(jnp.concatenate(ig_rows, axis=0)), -SHIFT) + gy_rows[1 : 1 + WIN]


N_ACC = 7
N_PREP = 17
N_WTS = 7


def natural_rows(ref, start, count):
    return jnp.concatenate([jnp.transpose(ref[start + r])[None] for r in range(count)], axis=0)


def inner_kernel(image_side, own_rows, info, x_ref, gy_ref, *refs):
    wts, refs = refs[:N_WTS], refs[N_WTS:]
    c_out, ig_out, refs = refs[0], refs[1], refs[2:]
    acc, refs = refs[:N_ACC], refs[N_ACC:]
    x_s, gy_s, ig_s, refs = *refs[:3], refs[3:]
    prep, tmp = refs[:N_PREP], refs[N_PREP:]
    image, row_block = pl.program_id(0), pl.program_id(1)
    first_step = (image == 0) & (row_block == 0)

    @pl.when(first_step)
    def _():
        for ref in acc:
            ref[...] = jnp.zeros_like(ref)
        ig_s[...] = jnp.zeros_like(ig_s)

    @pl.when(row_block == 0)
    def _():
        x_s[...] = jnp.swapaxes(x_ref[0].astype(f32), 0, 1)
        gy_s[...] = jnp.swapaxes(gy_ref[0].astype(f32), 0, 1)

    start = row_block * WIN + SHIFT
    x_rows = natural_rows(x_s, start, WIN)
    gy_rows = natural_rows(gy_s, start - 1, WIN + 2)
    base_row = info[0] * own_rows + start
    ig = block_step(
        x_rows, gy_rows, first_step, False, base_row, info[2 + image], image_side, wts, prep, acc, tmp, c_out
    )
    for r in range(WIN):
        ig_s[start + r] = jnp.transpose(ig[r])

    @pl.when(row_block == pl.num_programs(1) - 1)
    def _():
        ig_out[0] = jnp.swapaxes(ig_s[...], 0, 1)


def last_kernel(image_side, own_rows, info, x_ref, gy_ref, halo_ref, ig_ref, *refs):
    wts, refs = refs[:N_WTS], refs[N_WTS:]
    acc_in, refs = refs[:N_ACC], refs[N_ACC:]
    sr_ref, hr_ref, c_out, ig_out, ig_halo, pack_out, refs = *refs[:6], refs[6:]
    acc, refs = refs[:N_ACC], refs[N_ACC:]
    prep, tmp = refs[:N_PREP], refs[N_PREP:]
    image = pl.program_id(0)
    first_step = image == 0

    @pl.when(first_step)
    def _():
        for ref, given in zip(acc, acc_in):
            ref[...] = given[...]

    def rows_of(ref):
        return jnp.swapaxes(ref[0].astype(f32), 0, 1)

    x_own, gy_own, halo = rows_of(x_ref), rows_of(gy_ref), rows_of(halo_ref)
    natural = lambda rows: jnp.concatenate([jnp.transpose(r)[None] for r in rows], axis=0)
    x_rows = natural([x_own[SHIFT + r] for r in range(SHIFT)] + [halo[r] for r in range(SHIFT)])
    gy_rows = natural(
        [gy_own[SHIFT - 1 + r] for r in range(SHIFT + 1)] + [halo[SHIFT + r] for r in range(SHIFT + 1)]
    )
    base_row = info[0] * own_rows + own_rows - SHIFT
    ig = block_step(
        x_rows, gy_rows, first_step, info[1] == 1, base_row, info[2 + image], image_side, wts, prep, acc, tmp, c_out
    )
    kept = rows_of(ig_ref)
    new = [kept[r] for r in range(SHIFT)] + [jnp.transpose(ig[r]) for r in range(SHIFT)]
    ig_out[0] = jnp.swapaxes(jnp.stack(new), 0, 1)
    for r in range(SHIFT):
        ig_halo[0, r] = jnp.transpose(ig[SHIFT + r]).astype(bf16)

    @pl.when(image == pl.num_programs(0) - 1)
    def _():
        pack_gradients(info[2 + pl.num_programs(0)], acc, sr_ref, hr_ref, pack_out)


def pack_rows(ch):
    up = -(-ch // 8) * 8
    blocks = 17
    vec_at = (blocks + (blocks + 1) // 2) * up
    return up, blocks, vec_at, vec_at + 32, vec_at + 32 + 3 * TOK


def pack_gradients(device, acc, sr_ref, hr_ref, out):
    (acc_conv, acc_qkv, acc_proj, acc_fc1, acc_fc2, acc_ln, acc_rel) = acc
    ch = acc_fc2.shape[1]
    dim = ch // HEADS
    up, count, vec_at, rel_at, used = pack_rows(ch)
    rest = ch - LANE
    out[used:, :] = jnp.zeros((out.shape[0] - used, LANE), f32)
    out[rel_at:used, :] = acc_rel[...]
    blocks = [acc_conv[:ch, t * CPAD : t * CPAD + ch] for t in range(9)]
    qkv = [drop_lanes(acc_qkv[k], HEADS, dim) for k in range(3)]
    blocks += [qkv[k][:ch] for k in range(3)]
    blocks += [drop_rows(acc_proj[...], HEADS, dim)]
    fc1 = jnp.transpose(acc_fc1[...])
    fc2 = jnp.transpose(acc_fc2[...])
    blocks += [fc1[:ch, :ch], fc1[:ch, ch:]]
    blocks += [fc2[:, :ch], fc2[:, ch:]]
    out[:vec_at, :] = jnp.zeros((vec_at, LANE), f32)
    for k, block in enumerate(blocks):
        out[k * up : k * up + ch, :] = block[:, :LANE]
        at = (count + k // 2) * up
        half = (k % 2) * TOK
        out[at : at + ch, half : half + rest] = block[:, LANE:]
    ln = [jnp.sum(jnp.transpose(acc_ln[k]), axis=0, keepdims=True) for k in range(5)]
    vec = [
        ln[0],
        ln[1],
        qkv[0][ch : ch + 1, :],
        qkv[2][ch : ch + 1, :],
        acc_proj[dim : dim + 1, :],
        ln[2],
        ln[3],
        fc1[ch : ch + 1, :ch],
        fc1[ch : ch + 1, ch:],
        ln[4],
        acc_conv[ch : ch + 1, 4 * CPAD : 4 * CPAD + ch],
    ]
    vec = jnp.concatenate(vec, axis=0)
    diff = sr_ref[...] - hr_ref[...]
    luma = (65.481 * diff[:, 0] + 128.553 * diff[:, 1] + 24.966 * diff[:, 2]) / 255.0
    square = jnp.sum(luma * luma, axis=1, keepdims=True)
    mse = jnp.sum(square, axis=2, keepdims=True) * (1.0 / (luma.shape[1] * luma.shape[2]))
    psnr = jnp.sum(jnp.log(mse + 1e-06) * (-10.0 / 2.302585092994046), axis=0)
    out[vec_at : vec_at + 32, :] = jnp.zeros((32, LANE), f32)
    out[vec_at : vec_at + 11, :] = vec[:, :LANE]
    lane = lax.broadcasted_iota(jnp.int32, (1, LANE), 1)
    for k in range(3):
        piece = psnr.astype(bf16).astype(f32)
        out[vec_at + 11 + k : vec_at + 12 + k, :] = jnp.where(lane == device, piece, 0.0)
        psnr = psnr - piece
    out[vec_at + 16 : vec_at + 27, :rest] = vec[:, LANE:]


def whole(shape):
    return pl.BlockSpec(shape, lambda *_: (0,) * len(shape))


def acc_shapes(ch, hid):
    return [
        (CPAD, 9 * CPAD),
        (3, CPAD, CPAD),
        (CPAD, ch),
        (hid, CPAD),
        (hid, ch),
        (5, ch, LANE),
        (3 * TOK, LANE),
    ]


def scratches(ch, hid, px, vec_rows):
    v = pltpu.VMEM
    prep = [
        v((ch, vec_rows), f32),
        v((3 * CPAD, ch), bf16), v((ch, CPAD), bf16), v((hid, ch), bf16), v((ch, hid), bf16),
        v((ch, CPAD), bf16), v((ch, CPAD), bf16), v((ch, CPAD), bf16), v((CPAD, ch), bf16),
        v((ch, hid), bf16), v((hid, ch), bf16),
        v((9 * CPAD, ch), bf16),
        v((TOK, LANE), f32),
        v((TOK, LANE), f32),
        v((hid, LANE), f32),
        v((10, ch, LANE), f32),
        v((2, CPAD, LANE), f32),
    ]
    wins = px // TOK
    tmp = [
        v((px, 9 * CPAD), bf16),
        v((CPAD, px), bf16), v((CPAD, px), bf16), v((CPAD, px), bf16), v((hid, px), bf16), v((CPAD, px), bf16),
        v((wins, CPAD, LANE), bf16),
        v((wins, 3 * TOK, LANE), f32),
        v((wins, 3 * TOK, LANE), bf16),
        v((2, px, CPAD), bf16),
        v((ch, px), f32),
        v((CPAD, px), bf16),
        v((CPAD, px), bf16),
        v((2, px, CPAD), bf16),
        v((ch, px), f32),
        v((ch, px), f32),
        v((hid, px), f32),
        v((CPAD, px), bf16),
        v((CPAD, px), bf16),
        v((CPAD, px), bf16),
        v((8, px), f32),
        v((ch, px), bf16),
        v((hid, px), bf16),
        v((ch, px), f32),
    ]
    return prep + tmp


def conv_kernel(image_side, own_rows, info, hc_ref, c1_ref, c2_ref, hg_ref, ig_ref, x_ref, vec_ref, conv_ref, out_ref, ig_out, cs, wc):
    ch = x_ref.shape[1]

    @pl.when(pl.program_id(0) == 0)
    def _():
        wc[...] = jnp.zeros_like(wc)
        cs[...] = jnp.zeros_like(cs)
        for tap in range(9):
            wc[tap * TAP : tap * TAP + ch, :] = conv_ref[tap // 3, tap % 3].astype(bf16)

    first = jnp.where(info[0] == 0, 0.0, 1.0).astype(f32)
    last = jnp.where(info[1] == 1, 0.0, 1.0).astype(f32)
    need = own_rows + 2
    col = lax.broadcasted_iota(jnp.int32, (1, image_side, ch), 1)
    halo = hc_ref.shape[1]
    for r in range(need):
        if r < halo:
            row = hc_ref[0, r : r + 1]
        elif r - halo < c1_ref.shape[1]:
            row = c1_ref[0, r - halo : r - halo + 1]
        else:
            at = r - halo - c1_ref.shape[1]
            row = c2_ref[0, at : at + 1]
        row = row.astype(f32)
        if r == 0:
            row = row * first
        if r == need - 1:
            row = row * last
        left = jnp.where(col == 0, 0.0, roll_cols(row, -1))
        right = jnp.where(col == image_side - 1, 0.0, roll_cols(row, 1))
        at = slice(r * image_side, (r + 1) * image_side)
        cs[at, 0:ch] = left[0].astype(bf16)
        cs[at, TAP : TAP + ch] = row[0].astype(bf16)
        cs[at, 2 * TAP : 2 * TAP + ch] = right[0].astype(bf16)
    bias = vec_ref[10:11, :]
    x_rows = jnp.swapaxes(x_ref[0].astype(f32), 0, 1)
    done = []
    for r in range(0, own_rows, WIN):
        total = None
        for i in range(3):
            at = slice((r + i) * image_side, (r + i + WIN) * image_side)
            term = nn(cs[at, :], wc[i * 3 * TAP : (i + 1) * 3 * TAP, :])
            total = term if total is None else total + term
        total = total + bias
        for k in range(WIN):
            done.append(jnp.transpose(total[k * image_side : (k + 1) * image_side]) + x_rows[r + k])
    out_ref[0] = jnp.swapaxes(jnp.stack(done), 0, 1).astype(bf16)
    kept = jnp.swapaxes(ig_ref[0], 0, 1)
    new = [hg_ref[0, r].astype(f32) for r in range(SHIFT)] + [kept[r] for r in range(SHIFT, WIN)]
    ig_out[0] = jnp.swapaxes(jnp.stack(new), 0, 1)


def split_bits(size):
    return [b for b in range(size.bit_length() - 1)]


def exchange_kernel(stages, g_ref, out_ref, work, given, low, send_sem, recv_sem):
    rows = g_ref.shape[0]

    def meet(stage):
        axis, b = stage
        me = lax.axis_index(axis)
        step = 2**b
        bit = (me // step) % 2
        return {axis: me + (1 - 2 * bit) * step}, bit

    barrier = pltpu.get_barrier_semaphore()
    for stage in stages:
        other, _ = meet(stage)
        pl.semaphore_signal(barrier, inc=1, device_id=other, device_id_type=pl.DeviceIdType.MESH)
    pl.semaphore_wait(barrier, len(stages))

    def span(start, size):
        return pl.ds(pl.multiple_of(start, 16), size)

    start = 0
    size = rows
    starts = []
    taken = 0
    for s, stage in enumerate(stages):
        other, bit = meet(stage)
        size = size // 2
        starts.append(start)
        keep = start + bit * size
        give = start + (1 - bit) * size
        source = g_ref if s == 0 else work
        copy = pltpu.make_async_remote_copy(
            src_ref=source.at[span(give, size)],
            dst_ref=given.at[pl.ds(taken, size)],
            send_sem=send_sem.at[s],
            recv_sem=recv_sem.at[s],
            device_id=other,
            device_id_type=pl.DeviceIdType.MESH,
        )
        copy.start()
        copy.wait()
        total = source[span(keep, size), :] + given[taken : taken + size, :]
        if s < len(stages) - 1:
            work[span(keep, size), :] = total
        else:
            low[span(keep, size), :] = total.astype(bf16)
        taken += size
        start = keep
    for s in reversed(range(len(stages))):
        other, bit = meet(stages[s])
        n = len(stages) + s
        copy = pltpu.make_async_remote_copy(
            src_ref=low.at[span(start, size)],
            dst_ref=low.at[span(start, size)],
            send_sem=send_sem.at[n],
            recv_sem=recv_sem.at[n],
            device_id=other,
            device_id_type=pl.DeviceIdType.MESH,
        )
        copy.start()
        copy.wait()
        start = starts[s]
        size = size * 2
    out_ref[...] = low[...]


def reduce_all(packed, sizes):
    stages = [(axis, b) for axis, size in sizes for b in split_bits(size)]
    rows = packed.shape[0]
    vmem = pl.BlockSpec(memory_space=pltpu.VMEM)
    return pl.pallas_call(
        functools.partial(exchange_kernel, stages),
        in_specs=[vmem],
        out_specs=vmem,
        out_shape=jax.ShapeDtypeStruct(packed.shape, bf16),
        scratch_shapes=[
            pltpu.VMEM(packed.shape, f32),
            pltpu.VMEM(packed.shape, f32),
            pltpu.VMEM(packed.shape, bf16),
            pltpu.SemaphoreType.DMA((2 * len(stages),)),
            pltpu.SemaphoreType.DMA((2 * len(stages),)),
        ],
        compiler_params=pltpu.CompilerParams(
            collective_id=0, has_side_effects=True, vmem_limit_bytes=40 * 1024 * 1024
        ),
        name="sum_gradients",
    )(packed)


def adam_kernel(scal, g_ref, *refs):
    weights, firsts, seconds = refs[0:7], refs[7:14], refs[14:21]
    norm_ref, psnr_ref, outs = refs[21], refs[22], refs[23:44]
    ch = weights[2].shape[0]
    up, count, vec_at, rel_at, used = pack_rows(ch)
    rest = ch - LANE

    def block(k):
        left = g_ref[k * up : (k + 1) * up, :].astype(f32)
        at = (count + k // 2) * up
        right = g_ref[at : at + up, :].astype(f32)
        if k % 2:
            right = pltpu.roll(right, TOK, 1)
        return jnp.concatenate([left, right[:, :rest]], axis=1)[:ch]

    vec_rows = g_ref[vec_at : vec_at + 32, :].astype(f32)
    vec = jnp.concatenate([vec_rows[:11], vec_rows[16:27, :rest]], axis=1)
    psnr = vec_rows[11:12] + vec_rows[12:13] + vec_rows[13:14]
    psnr_ref[...] = jnp.sum(psnr, axis=1, keepdims=True)

    span = 2 * WIN
    wide = span * span
    at = lax.broadcasted_iota(jnp.int32, (TOK, wide), 0)
    to = lax.broadcasted_iota(jnp.int32, (TOK, wide), 1)
    place = ((at >> 3) + (WIN - 1)) * span + (at & 7) + (WIN - 1)
    expand = (to == place).astype(f32).astype(bf16)
    pairs = g_ref[rel_at:used, :]
    rel_rows = []
    for p in range(3):
        for parity in range(2):
            part = pairs[p * TOK : (p + 1) * TOK, :].astype(f32)
            if parity:
                part = pltpu.roll(part, TOK, 1)
            spread = nn(part[:, :TOK].astype(bf16), expand)
            total = jnp.zeros((WIN, wide), f32)
            for row in range(WIN):
                piece = spread[row * WIN : (row + 1) * WIN]
                piece = pltpu.roll(piece, (wide - span * row) % wide, 1)
                total = total + piece
            line = total[0:1]
            for c in range(1, WIN):
                line = line + pltpu.roll(total, wide - c, 1)[c : c + 1]
            rel_rows.append(line)
    rel = jnp.concatenate(rel_rows, axis=0)
    rel = jnp.concatenate(
        [rel[:, k * span : k * span + span - 1] for k in range(span - 1)], axis=1
    )
    qkv = jnp.concatenate([block(9), block(10), block(11)], axis=1)
    fc1 = jnp.concatenate([block(13), block(14)], axis=1)
    fc2 = jnp.concatenate([block(15), block(16)], axis=1)
    small = [vec, qkv, block(12), rel, fc1, fc2]
    taps = [block(t) for t in range(9)]
    total = jnp.zeros((1, 1), f32)
    for g in small + taps:
        total = total + jnp.sum(jnp.sum(g * g, axis=0, keepdims=True), axis=1, keepdims=True)
    norm = jnp.sqrt(total)
    norm_ref[...] = norm
    clip = jnp.minimum(1.0, max_norm / (norm + 1e-06))
    fix_one, fix_two = scal[0], scal[1]

    def update(w, m1, m2, g, rate):
        g = g * clip
        m1 = beta_one * m1 + (1.0 - beta_one) * g
        m2 = beta_two * m2 + (1.0 - beta_two) * g * g
        step = (m1 / fix_one) / (jnp.sqrt(m2 / fix_two) + adam_eps)
        return w - rate * (step + decay_rate * w), m1, m2

    for k, g in enumerate(small):
        new = update(weights[k][...], firsts[k][...], seconds[k][...], g, vector_rate if k == 0 else learn_rate)
        for ref, value in zip(outs[3 * k : 3 * k + 3], new):
            ref[...] = value
    for t, g in enumerate(taps):
        at = (t // 3, t % 3)
        new = update(weights[6][at], firsts[6][at], seconds[6][at], g, learn_rate)
        for ref, value in zip(outs[18:21], new):
            ref[at] = value


def relative_onehot_keys_first():
    position = np.arange(TOK)
    pos_row, pos_col = position // WIN, position % WIN
    span = 2 * WIN - 1
    index = (pos_row[None, :] - pos_row[:, None] + WIN - 1) * span + (
        pos_col[None, :] - pos_col[:, None] + WIN - 1
    )
    return index.reshape(-1), span * span


def on_device(
    images, cotangent, valid_size,
    vectors, vectors_first, vectors_second,
    qkv_weight, qkv_first, qkv_second,
    proj_weight, proj_first, proj_second,
    rel_table, rel_first, rel_second,
    fc1_weight, fc1_first, fc1_second,
    fc2_weight, fc2_first, fc2_second,
    conv_weight, conv_first, conv_second,
    step, sr_crops, hr_crops, psnr_running,
):
    count, own_rows, image_side, ch = images.shape
    out_shape = (count, ch, own_rows, image_side)
    hid = fc1_weight.shape[1]
    px = image_side * WIN
    blocks = own_rows // WIN
    heads = lax.axis_size("head")
    place = lax.axis_index("head")
    to_lower = [((i + 1) % heads, i) for i in range(heads)]
    to_upper = [(i, (i + 1) % heads) for i in range(heads)]
    info = jnp.concatenate(
        [
            jnp.stack([place, (place == heads - 1).astype(jnp.int32)]).astype(jnp.int32),
            valid_size.astype(jnp.int32),
            ((lax.axis_index("dp") * heads + place) % LANE)[None].astype(jnp.int32),
        ]
    )
    images = images.transpose(0, 3, 1, 2)
    cotangent = cotangent.transpose(0, 3, 1, 2)
    halo = lax.ppermute(
        jnp.concatenate([images[:, :, :SHIFT], cotangent[:, :, : SHIFT + 1]], axis=2), "head", to_lower
    )

    index, span = relative_onehot_keys_first()
    onehot = (jnp.asarray(index)[:, None] == jnp.arange(span)[None, :]).astype(f32)
    bias = jnp.dot(onehot, rel_table, precision=highest)
    bias = bias.reshape(TOK, TOK, 3, 2).transpose(2, 0, 3, 1).reshape(3, TOK, LANE)

    wts = (vectors, qkv_weight, proj_weight, fc1_weight, fc2_weight.T, conv_weight, bias)
    wts_specs = [whole(w.shape) for w in wts]
    acc_dims = acc_shapes(ch, hid)
    acc_types = [jax.ShapeDtypeStruct(s, f32) for s in acc_dims]
    smem = pl.BlockSpec(memory_space=pltpu.SMEM)
    params = pltpu.CompilerParams(
        dimension_semantics=("arbitrary", "arbitrary"), vmem_limit_bytes=60 * 1024 * 1024
    )
    view = lambda rows, at, dims: pl.BlockSpec((1, ch, rows, image_side), lambda n, *_: (n, 0, at, 0))
    c_block = lambda size: pl.BlockSpec((1, size, image_side, ch), lambda n, *_: (n, 0, 0, 0))
    row_view = pltpu.VMEM((own_rows, ch, image_side), f32)
    c1, ig, *acc = pl.pallas_call(
        functools.partial(inner_kernel, image_side, own_rows),
        grid=(count, blocks - 1),
        in_specs=[smem, view(own_rows, 0, 2), view(own_rows, 0, 2), *wts_specs],
        out_specs=[
            pl.BlockSpec((1, WIN, image_side, ch), lambda n, r: (n, r, 0, 0)),
            view(own_rows, 0, 2),
            *[whole(s) for s in acc_dims],
        ],
        out_shape=[
            jax.ShapeDtypeStruct((count, own_rows - WIN, image_side, ch), bf16),
            jax.ShapeDtypeStruct(out_shape, f32),
            *acc_types,
        ],
        scratch_shapes=[row_view] * 3 + scratches(ch, hid, px, vectors.shape[0]),
        compiler_params=params,
        name="inner_windows",
    )(info, images, cotangent, *wts)
    device_count = lax.axis_size("dp") * heads
    unit = 16 * device_count
    rows = -(-pack_rows(ch)[-1] // unit) * unit
    c2, ig, ig_halo, packed = pl.pallas_call(
        functools.partial(last_kernel, image_side, own_rows),
        grid=(count,),
        in_specs=[
            smem,
            view(WIN, blocks - 1, 1),
            view(WIN, blocks - 1, 1),
            view(2 * SHIFT + 1, 0, 1),
            view(WIN, blocks - 1, 1),
            *wts_specs,
            *[whole(s) for s in acc_dims],
            whole(sr_crops.shape),
            whole(hr_crops.shape),
        ],
        out_specs=[
            c_block(WIN),
            view(WIN, blocks - 1, 1),
            pl.BlockSpec((1, SHIFT, ch, image_side), lambda n: (n, 0, 0, 0)),
            whole((rows, LANE)),
        ],
        out_shape=[
            jax.ShapeDtypeStruct((count, WIN, image_side, ch), bf16),
            jax.ShapeDtypeStruct(out_shape, f32),
            jax.ShapeDtypeStruct((count, SHIFT, ch, image_side), bf16),
            jax.ShapeDtypeStruct((rows, LANE), f32),
        ],
        input_output_aliases={4: 1},
        scratch_shapes=[pltpu.VMEM(s, f32) for s in acc_dims] + scratches(ch, hid, px, vectors.shape[0]),
        compiler_params=pltpu.CompilerParams(
            dimension_semantics=("arbitrary",), vmem_limit_bytes=60 * 1024 * 1024
        ),
        name="last_windows",
    )(info, images, cotangent, halo, ig, *wts, *acc, sr_crops, hr_crops)

    c_halo = lax.ppermute(c2[:, WIN - SHIFT - 1 :], "head", to_upper)
    ig_halo = lax.ppermute(ig_halo, "head", to_upper)

    summed = reduce_all(packed, (("dp", lax.axis_size("dp")), ("head", heads)))

    output, image_grad = pl.pallas_call(
        functools.partial(conv_kernel, image_side, own_rows),
        grid=(count,),
        in_specs=[
            smem,
            c_block(SHIFT + 1), c_block(own_rows - WIN), c_block(WIN),
            pl.BlockSpec((1, SHIFT, ch, image_side), lambda n: (n, 0, 0, 0)),
            view(WIN, 0, 1),
            view(own_rows, 0, 1),
            whole(vectors.shape), whole(conv_weight.shape),
        ],
        out_specs=[view(own_rows, 0, 1), view(WIN, 0, 1)],
        out_shape=[jax.ShapeDtypeStruct(out_shape, bf16), jax.ShapeDtypeStruct(out_shape, f32)],
        input_output_aliases={5: 1},
        scratch_shapes=[
            pltpu.VMEM(((own_rows + 2) * image_side, 3 * TAP), bf16),
            pltpu.VMEM((9 * TAP, ch), bf16),
        ],
        compiler_params=pltpu.CompilerParams(
            dimension_semantics=("arbitrary",), vmem_limit_bytes=60 * 1024 * 1024
        ),
        name="conv_output",
    )(info, c_halo, c1, c2, ig_halo, ig, images, vectors, conv_weight)
    output, image_grad = output.transpose(0, 2, 3, 1), image_grad.transpose(0, 2, 3, 1)

    step_count = step[0].astype(f32)
    scal = jnp.stack([1.0 - beta_one**step_count, 1.0 - beta_two**step_count])
    weights = (vectors, qkv_weight, proj_weight, rel_table.T, fc1_weight, fc2_weight.T, conv_weight)
    firsts = (vectors_first, qkv_first, proj_first, rel_first.T, fc1_first, fc2_first.T, conv_first)
    seconds = (vectors_second, qkv_second, proj_second, rel_second.T, fc1_second, fc2_second.T, conv_second)
    vmem = pl.BlockSpec(memory_space=pltpu.VMEM)
    grad_norm, psnr, *updated = pl.pallas_call(
        adam_kernel,
        in_specs=[smem] + [vmem] * 22,
        out_specs=[vmem] * 23,
        out_shape=[jax.ShapeDtypeStruct((1, 1), f32)] * 2
        + [jax.ShapeDtypeStruct(w.shape, f32) for w in weights for _ in range(3)],
        compiler_params=pltpu.CompilerParams(vmem_limit_bytes=60 * 1024 * 1024),
        name="adam",
    )(scal, summed, *weights, *firsts, *seconds)
    for k in (9, 10, 11, 15, 16, 17):
        updated[k] = updated[k].T
    psnr_total = psnr_running + psnr.reshape(1)
    return (output, image_grad, grad_norm.reshape(1), psnr_total, *updated)


def solution(mesh):
    pixels = P("dp", "head", None, None)
    crops = P(("dp", "head"), None, None, None)
    placed = (pixels, pixels, P("dp")) + (P(),) * 22 + (crops, crops, P())
    return jax.shard_map(
        on_device,
        mesh=mesh,
        in_specs=placed,
        out_specs=(pixels, pixels) + (P(),) * 23,
        check_vma=False,
    )
```

```python
import functools

import jax
import jax.numpy as jnp
import numpy as np
from jax import lax
from jax.experimental import pallas as pl
from jax.experimental.pallas import tpu as pltpu
from jax.sharding import PartitionSpec as P

WIN = 8
TOK = WIN * WIN
SHIFT = WIN // 2
LANE = 128
TAP = 256
HPAD = 32
HEADS = 6
CPAD = HEADS * HPAD

eps_norm = 1e-05
neg_mask = -100.0
max_norm = 1.0
learn_rate = 0.03
vector_rate = 0.2
beta_one = 0.9
beta_two = 0.999
adam_eps = 1e-08
decay_rate = 0.01
highest = lax.Precision.HIGHEST
f32 = jnp.float32
bf16 = jnp.bfloat16


def nn(a, b):
    return lax.dot_general(a, b, (((1,), (0,)), ((), ())), preferred_element_type=f32)


def nt(a, b):
    return lax.dot_general(a, b, (((1,), (1,)), ((), ())), preferred_element_type=f32)


def pad_heads(rows, heads):
    dim = rows.shape[0] // heads
    gap = jnp.zeros((HPAD - dim, rows.shape[1]), rows.dtype)
    parts = []
    for h in range(heads):
        parts += [rows[h * dim : (h + 1) * dim], gap]
    return jnp.concatenate(parts, axis=0)


def drop_rows(rows, heads, dim):
    return jnp.concatenate([rows[h * HPAD : h * HPAD + dim] for h in range(heads)], axis=0)


def drop_lanes(rows, heads, dim):
    return jnp.concatenate([rows[:, h * HPAD : h * HPAD + dim] for h in range(heads)], axis=1)


def to_tokens(rows):
    side = rows.shape[1]
    return jnp.concatenate(
        [rows[:, w * WIN : (w + 1) * WIN, :].reshape(TOK, rows.shape[2]) for w in range(side // WIN)],
        axis=0,
    )


def from_tokens(tokens):
    count = tokens.shape[0] // TOK
    return jnp.concatenate(
        [tokens[w * TOK : (w + 1) * TOK].reshape(WIN, WIN, tokens.shape[1]) for w in range(count)],
        axis=1,
    )


def roll_cols(rows, by):
    side = rows.shape[1]
    by = by % side
    return jnp.concatenate([rows[:, by:, :], rows[:, :by, :]], axis=1)


def block_step(x_rows, gy_rows, first_step, edge, base_row, valid, image_side, wts, prep, acc, tmp, c_out):
    (vec_ref, qkv_ref, proj_ref, fc1_ref, fc2_ref, conv_ref, bias_ref) = wts
    (vecT, wqkvT, wpT, w1T, w2T, wq, wk, wv, wp, w1, w2, wcT, colmask, rowmask, b1T, wide_vec, head_vec) = prep
    (acc_conv, acc_qkv, acc_proj, acc_fc1, acc_fc2, acc_ln, acc_rel) = acc
    (g9, a_aug, o_aug, m_aug, g_aug, c_aug, qeo_s, p_s, pb_s, kv_s, first_s, do_s, dq_s, dkv_s, u2_s, xT_s, slope_s, vt_s, qt_s, kt_s, inv_s, db_s, dh_s, ds_s) = tmp
    ch = x_rows.shape[2]
    dim = ch // HEADS
    hid = fc1_ref.shape[1]
    px = x_rows.shape[1] * WIN
    pairs = px // LANE
    ones_row = dim

    @pl.when(first_step)
    def _():
        vecT[...] = jnp.transpose(vec_ref[...])
        for k in range(10):
            wide_vec[k] = jnp.broadcast_to(vecT[:, k : k + 1], (ch, LANE))
        for k in range(2):
            head_vec[k] = pad_heads(wide_vec[2 + k], HEADS)
        b1T[:ch, :] = wide_vec[7]
        b1T[ch:, :] = wide_vec[8]
        for k, dst in enumerate((wq, wk, wv)):
            part = pad_heads(jnp.transpose(qkv_ref[:, k * ch : (k + 1) * ch]), HEADS)
            wqkvT[k * CPAD : (k + 1) * CPAD, :] = part.astype(bf16)
            dst[...] = jnp.transpose(part).astype(bf16)
        padded = pad_heads(proj_ref[...], HEADS)
        wp[...] = padded.astype(bf16)
        wpT[...] = jnp.transpose(padded).astype(bf16)
        w1[...] = fc1_ref[...].astype(bf16)
        w1T[...] = jnp.transpose(fc1_ref[...]).astype(bf16)
        w2T[...] = fc2_ref[...].astype(bf16)
        w2[...] = jnp.transpose(fc2_ref[...]).astype(bf16)
        wcT[...] = jnp.zeros_like(wcT)
        g9[...] = jnp.zeros_like(g9)
        for tap in range(9):
            wcT[tap * CPAD : tap * CPAD + ch, :] = jnp.transpose(conv_ref[tap // 3, tap % 3]).astype(bf16)
        key = lax.broadcasted_iota(jnp.int32, (TOK, LANE), 0)
        query = lax.broadcasted_iota(jnp.int32, (TOK, LANE), 1) & (TOK - 1)
        one = lambda m: m.astype(f32)
        colmask[...] = one(((key & 7) < SHIFT) != ((query & 7) < SHIFT))
        rowmask[...] = one(((key >> 3) < SHIFT) != ((query >> 3) < SHIFT))
        for ref in (a_aug, m_aug, c_aug):
            pad = ref.shape[0] - ch
            ref[ch:, :] = (lax.broadcasted_iota(jnp.int32, (pad, px), 0) == 0).astype(f32).astype(bf16)

    def column(k):
        return wide_vec[k]

    def stats(v):
        mean = jnp.sum(v, axis=0, keepdims=True) * (1.0 / ch)
        cen = v - mean
        var = jnp.sum(cen * cen, axis=0, keepdims=True) * (1.0 / ch)
        inv = lax.rsqrt(var + eps_norm)
        return cen * inv, inv

    def ln_back(grad, u, inv, gain):
        t = grad * gain
        mean_t = jnp.sum(t, axis=0, keepdims=True) * (1.0 / ch)
        mean_tu = jnp.sum(t * u, axis=0, keepdims=True) * (1.0 / ch)
        return inv * (t - mean_t - u * mean_tu)

    chunks = [slice(k * LANE, (k + 1) * LANE) for k in range(px // LANE)]
    third = hid // 3
    bands = [slice(k * third, (k + 1) * third) for k in range(3)]

    keep = jnp.where(edge, 0.0, 1.0).astype(f32)
    col = lax.broadcasted_iota(jnp.int32, (1, image_side, ch), 1)
    moved = {}

    def build_tap(tap):
        i, j = tap % 3, tap // 3
        if i == 0:
            shifted = roll_cols(gy_rows, SHIFT + 1 - j)
            if j == 0:
                shifted = jnp.where(col == image_side - SHIFT - 1, 0.0, shifted)
            if j == 2:
                shifted = jnp.where(col == image_side - SHIFT, 0.0, shifted)
            moved[j] = shifted
        rows = [moved[j][r + 2 - i : r + 3 - i] for r in range(WIN)]
        if i == 0:
            rows[SHIFT - 1] = rows[SHIFT - 1] * keep
        if i == 2:
            rows[SHIFT] = rows[SHIFT] * keep
        at = (3 * i + j) * CPAD
        g9[:, at : at + ch] = to_tokens(jnp.concatenate(rows, axis=0)).astype(bf16)

    x_tok = to_tokens(roll_cols(x_rows, SHIFT))
    for at in chunks:
        xT = jnp.transpose(x_tok[at])
        xT_s[:, at] = xT
        u1, _ = stats(xT)
        a_aug[:ch, at] = (u1 * column(0) + column(1)).astype(bf16)
    scale = dim ** (-0.5)
    qkv_all = nn(wqkvT[...], a_aug[:ch, :])
    for at in chunks:
        qt_s[:, at] = ((qkv_all[:CPAD, at] + head_vec[0]) * scale).astype(bf16)
        kT = qkv_all[CPAD : 2 * CPAD, at].astype(bf16)
        vT = (qkv_all[2 * CPAD :, at] + head_vec[1]).astype(bf16)
        kt_s[:, at] = kT
        vt_s[:, at] = vT
        kv_s[0, at, :] = jnp.transpose(kT.astype(f32)).astype(bf16)
        kv_s[1, at, :] = jnp.transpose(vT.astype(f32)).astype(bf16)

    def low_lanes(rows):
        return lax.broadcasted_iota(jnp.int32, (rows, LANE), 1) < TOK

    def swap(slab):
        return pltpu.roll(slab, TOK, 1)

    def only_low(v):
        return jnp.where(low_lanes(v.shape[0]), v, jnp.zeros_like(v))

    def only_high(v):
        return jnp.where(low_lanes(v.shape[0]), jnp.zeros_like(v), v)

    def head_rows(v, h):
        return v[h * HPAD : (h + 1) * HPAD]

    def dup(slab):
        slab = slab.astype(f32)
        other = swap(slab)
        out = []
        for low, high in ((slab, other), (other, slab)):
            rows = [
                only_high(head_rows(high, h)) if h % 2 else only_low(head_rows(low, h)) for h in range(HEADS)
            ]
            out.append(jnp.concatenate(rows, axis=0).astype(bf16))
        return out

    def spread(slab):
        slab = slab.astype(f32)
        other = swap(slab)
        two = 2 * HPAD
        gap = jnp.zeros((two, TOK), f32)
        wide = jnp.zeros((two, LANE), f32)
        out = []
        for low, high in ((slab, other), (other, slab)):
            rows = [
                jnp.concatenate([only_low(low[:two]), gap], axis=1),
                jnp.concatenate([only_high(high[two : 2 * two]), gap], axis=1),
                jnp.concatenate([wide, low[2 * two :, :TOK]], axis=1),
            ]
            out.append(jnp.concatenate(rows, axis=0).astype(bf16))
        return out

    def merge(one, two):
        rows = []
        for h in range(HEADS):
            first, second = head_rows(one, h), head_rows(two, h)
            if h % 2:
                rows.append(jnp.where(low_lanes(HPAD), swap(first), second))
            else:
                rows.append(jnp.where(low_lanes(HPAD), first, swap(second)))
        return jnp.concatenate(rows, axis=0)

    def by_pair(rows):
        front, back = rows[:, :LANE], rows[:, LANE:]
        zero_back = jnp.zeros_like(back)
        return jnp.concatenate(
            [
                jnp.concatenate([only_low(front), zero_back], axis=1),
                jnp.concatenate([only_high(front), zero_back], axis=1),
                jnp.concatenate([jnp.zeros_like(front), back], axis=1),
            ],
            axis=0,
        )

    def pick_pair(stacked):
        front = jnp.where(low_lanes(TOK), stacked[:TOK, :LANE], stacked[TOK : 2 * TOK, :LANE])
        return jnp.concatenate([front, stacked[2 * TOK :, LANE:]], axis=1)

    key = lax.broadcasted_iota(jnp.int32, (TOK, LANE), 0)
    key_row = base_row + (key >> 3)
    key_row = jnp.where(key_row >= image_side, key_row - image_side, key_row)
    out_row = key_row >= valid
    edge_f = jnp.where(edge, neg_mask, 0.0).astype(f32)

    def scores_of(pp):
        q_pair = dup(qt_s[:, chunks[pp]])
        raw = []
        for half in range(2):
            w = 2 * pp + half
            qeo_s[w] = q_pair[half]
            raw.append(nn(by_pair(kv_s[0, w * TOK : (w + 1) * TOK, :]), q_pair[half]))
        return raw

    def soften(pp, raw):
        for half in range(2):
            w = 2 * pp + half
            key_col = (key & 7) + (w * WIN + SHIFT)
            apart = rowmask[...] * edge_f
            if w == 2 * pairs - 1:
                key_col = jnp.where(key_col >= image_side, key_col - image_side, key_col)
                apart = jnp.where(colmask[...] > 0.5, neg_mask, apart)
            extra = apart + jnp.where(out_row | (key_col >= valid), neg_mask, 0.0)
            s = raw[half].reshape(3, TOK, LANE) + bias_ref[...] + extra[None]
            top = jnp.max(s, axis=1, keepdims=True)
            e = jnp.exp(s - top)
            p = e / jnp.sum(e, axis=1, keepdims=True)
            p = p.reshape(3 * TOK, LANE)
            p_s[w] = p
            pb_s[w] = p.astype(bf16)

    def mix(pp):
        v_pair = spread(vt_s[:, chunks[pp]])
        return [nn(v_pair[half], pb_s[2 * pp + half]) for half in range(2)]

    def place(pp, mixed):
        o_aug[:, chunks[pp]] = merge(*mixed).astype(bf16)

    raws, mixes = {}, {}
    for t in range(pairs + 3):
        if 0 <= t - 2 < pairs:
            mixes[t - 2] = mix(t - 2)
        if t < pairs:
            raws[t] = scores_of(t)
        if 0 <= t - 1 < pairs:
            soften(t - 1, raws.pop(t - 1))
        if 0 <= t - 3 < pairs:
            place(t - 3, mixes.pop(t - 3))
        if t < 9:
            build_tap(t)
    o_aug[ones_row : ones_row + 1, :] = jnp.ones((1, px), bf16)

    attn = nn(wpT[...], o_aug[...])
    part = px // 3
    conv_back = [nn(g9[:part, :], wcT[...])]
    for at in chunks:
        first = xT_s[:, at] + (attn[:, at] + column(4))
        first_s[:, at] = first
        u2, inv2 = stats(first)
        u2_s[:, at] = u2
        inv_s[0:1, at] = inv2
        m_aug[:ch, at] = (u2 * column(5) + column(6)).astype(bf16)
    hidden_all = nn(w1T[...], m_aug[:ch, :])
    conv_back.append(nn(g9[part : 2 * part, :], wcT[...]))
    for at in chunks:
        for band in bands:
            hidden = hidden_all[band, at] + b1T[band, :]
            cdf = 0.5 * (1.0 + lax.erf(hidden * 0.7071067811865476))
            g_aug[band, at] = (hidden * cdf).astype(bf16)
            slope_s[band, at] = cdf + hidden * jnp.exp(-0.5 * hidden * hidden) * 0.3989422804014327
    branch = nn(w2T[...], g_aug[...])
    conv_back.append(nn(g9[2 * part :, :], wcT[...]))
    c_rows = []
    for at in chunks:
        cT = (first_s[:, at] + (branch[:, at] + column(9))).astype(bf16)
        c_aug[:ch, at] = cT
        c_rows.append(jnp.transpose(cT.astype(f32)))
    c_out[0] = roll_cols(from_tokens(jnp.concatenate(c_rows, axis=0)), -SHIFT).astype(bf16)

    dsecond = jnp.concatenate(conv_back, axis=0)
    for at in chunks:
        ds_chunk = jnp.transpose(dsecond[at])
        ds_s[:, at] = ds_chunk
        dbT = ds_chunk.astype(bf16)
        db_s[:, at] = dbT
        acc_ln[4] += dbT.astype(f32)
    dg = nn(w2[...], db_s[...])
    acc_fc2[...] += nt(g_aug[...], db_s[...])
    for at in chunks:
        for band in bands:
            dh_s[band, at] = (dg[band, at] * slope_s[band, at]).astype(bf16)
    dm_all = nn(w1[...], dh_s[...])
    acc_fc1[...] += nt(dh_s[...], m_aug[...])
    for at in chunks:
        u2 = u2_s[:, at]
        dm = dm_all[:, at]
        acc_ln[2] += dm * u2
        acc_ln[3] += dm
        dfirst = ds_s[:, at] + ln_back(dm, u2, inv_s[0:1, at], column(5))
        first_s[:, at] = dfirst
        db_s[:, at] = dfirst.astype(bf16)
    do_all = nn(wp[...], db_s[...])
    acc_proj[...] += nt(o_aug[...], db_s[...])
    for at in chunks:
        do_s[:, at] = do_all[:, at].astype(bf16)

    rel_sum = jnp.zeros((3 * TOK, LANE), f32)

    def probs_grad(pp):
        do_pair = dup(do_s[:, chunks[pp]])
        dps, dvs = [], []
        for half in range(2):
            w = 2 * pp + half
            dps.append(nn(by_pair(kv_s[1, w * TOK : (w + 1) * TOK, :]), do_pair[half]))
            dvs.append(nt(pb_s[w], do_pair[half]))
        return dps, dvs

    def scores_grad(pp, dps, dvs, rel_sum):
        out = []
        for half in range(2):
            w = 2 * pp + half
            p = p_s[w].reshape(3, TOK, LANE)
            dp = dps[half].reshape(3, TOK, LANE)
            ds = p * (dp - jnp.sum(p * dp, axis=1, keepdims=True))
            ds = ds.reshape(3 * TOK, LANE).astype(bf16)
            rel_sum = rel_sum + ds.astype(f32)
            out.append(ds)
            dkv_s[1, w * TOK : (w + 1) * TOK, :] = pick_pair(dvs[half]).astype(bf16)
        return out, rel_sum

    def inner_grads(pp, ds):
        k_pair = spread(kt_s[:, chunks[pp]])
        dks = [nt(ds[half], qeo_s[2 * pp + half]) for half in range(2)]
        dqs = [nn(k_pair[half], ds[half]) for half in range(2)]
        return dks, dqs

    def place_grads(pp, dks, dqs):
        for half in range(2):
            w = 2 * pp + half
            dkv_s[0, w * TOK : (w + 1) * TOK, :] = pick_pair(dks[half]).astype(bf16)
        dq_s[:, chunks[pp]] = merge(*dqs).astype(bf16)

    first_part, second_part, third_part = {}, {}, {}
    for t in range(pairs + 3):
        if 0 <= t - 2 < pairs:
            third_part[t - 2] = inner_grads(t - 2, second_part.pop(t - 2))
        if t < pairs:
            first_part[t] = probs_grad(t)
        if 0 <= t - 1 < pairs:
            second_part[t - 1], rel_sum = scores_grad(t - 1, *first_part.pop(t - 1), rel_sum)
        if 0 <= t - 3 < pairs:
            place_grads(t - 3, *third_part.pop(t - 3))
        at = slice(t * TAP, min((t + 1) * TAP, 9 * CPAD))
        if at.start < at.stop:
            acc_conv[:, at] += nn(c_aug[...], g9[:, at])
    acc_rel[...] += rel_sum

    dqT = dq_s[...]
    da_q = nn(wq[...], dqT)
    da_kv = nt(wk[...], dkv_s[0]) + nt(wv[...], dkv_s[1])
    acc_qkv[0] += nt(a_aug[...], dqT) * scale
    acc_qkv[1] += nn(a_aug[...], dkv_s[0])
    acc_qkv[2] += nn(a_aug[...], dkv_s[1])
    ig_rows = []
    for at in chunks:
        da = da_q[:, at] * scale + da_kv[:, at]
        u1, inv1 = stats(xT_s[:, at])
        acc_ln[0] += da * u1
        acc_ln[1] += da
        ig_rows.append(jnp.transpose(first_s[:, at] + ln_back(da, u1, inv1, column(0))))
    return roll_cols(from_tokens(jnp.concatenate(ig_rows, axis=0)), -SHIFT) + gy_rows[1 : 1 + WIN]


N_ACC = 7
N_PREP = 17
N_WTS = 7


def natural_rows(ref, start, count):
    return jnp.concatenate([jnp.transpose(ref[start + r])[None] for r in range(count)], axis=0)


def inner_kernel(image_side, own_rows, info, x_ref, gy_ref, *refs):
    wts, refs = refs[:N_WTS], refs[N_WTS:]
    c_out, ig_out, refs = refs[0], refs[1], refs[2:]
    acc, refs = refs[:N_ACC], refs[N_ACC:]
    x_s, gy_s, ig_s, refs = *refs[:3], refs[3:]
    prep, tmp = refs[:N_PREP], refs[N_PREP:]
    image, row_block = pl.program_id(0), pl.program_id(1)
    first_step = (image == 0) & (row_block == 0)

    @pl.when(first_step)
    def _():
        for ref in acc:
            ref[...] = jnp.zeros_like(ref)
        ig_s[...] = jnp.zeros_like(ig_s)

    @pl.when(row_block == 0)
    def _():
        x_s[...] = jnp.swapaxes(x_ref[0].astype(f32), 0, 1)
        gy_s[...] = jnp.swapaxes(gy_ref[0].astype(f32), 0, 1)

    start = row_block * WIN + SHIFT
    x_rows = natural_rows(x_s, start, WIN)
    gy_rows = natural_rows(gy_s, start - 1, WIN + 2)
    base_row = info[0] * own_rows + start
    ig = block_step(
        x_rows, gy_rows, first_step, False, base_row, info[2 + image], image_side, wts, prep, acc, tmp, c_out
    )
    for r in range(WIN):
        ig_s[start + r] = jnp.transpose(ig[r])

    @pl.when(row_block == pl.num_programs(1) - 1)
    def _():
        ig_out[0] = jnp.swapaxes(ig_s[...], 0, 1)


def last_kernel(image_side, own_rows, info, x_ref, gy_ref, halo_ref, ig_ref, *refs):
    wts, refs = refs[:N_WTS], refs[N_WTS:]
    acc_in, refs = refs[:N_ACC], refs[N_ACC:]
    sr_ref, hr_ref, c_out, ig_out, ig_halo, pack_out, refs = *refs[:6], refs[6:]
    acc, refs = refs[:N_ACC], refs[N_ACC:]
    prep, tmp = refs[:N_PREP], refs[N_PREP:]
    image = pl.program_id(0)
    first_step = image == 0

    @pl.when(first_step)
    def _():
        for ref, given in zip(acc, acc_in):
            ref[...] = given[...]

    def rows_of(ref):
        return jnp.swapaxes(ref[0].astype(f32), 0, 1)

    x_own, gy_own, halo = rows_of(x_ref), rows_of(gy_ref), rows_of(halo_ref)
    natural = lambda rows: jnp.concatenate([jnp.transpose(r)[None] for r in rows], axis=0)
    x_rows = natural([x_own[SHIFT + r] for r in range(SHIFT)] + [halo[r] for r in range(SHIFT)])
    gy_rows = natural(
        [gy_own[SHIFT - 1 + r] for r in range(SHIFT + 1)] + [halo[SHIFT + r] for r in range(SHIFT + 1)]
    )
    base_row = info[0] * own_rows + own_rows - SHIFT
    ig = block_step(
        x_rows, gy_rows, first_step, info[1] == 1, base_row, info[2 + image], image_side, wts, prep, acc, tmp, c_out
    )
    kept = rows_of(ig_ref)
    new = [kept[r] for r in range(SHIFT)] + [jnp.transpose(ig[r]) for r in range(SHIFT)]
    ig_out[0] = jnp.swapaxes(jnp.stack(new), 0, 1)
    for r in range(SHIFT):
        ig_halo[0, r] = jnp.transpose(ig[SHIFT + r]).astype(bf16)

    @pl.when(image == pl.num_programs(0) - 1)
    def _():
        pack_gradients(info[2 + pl.num_programs(0)], acc, sr_ref, hr_ref, pack_out)


def pack_rows(ch):
    up = -(-ch // 8) * 8
    blocks = 17
    vec_at = (blocks + (blocks + 1) // 2) * up
    return up, blocks, vec_at, vec_at + 32, vec_at + 32 + 3 * TOK


def pack_gradients(device, acc, sr_ref, hr_ref, out):
    (acc_conv, acc_qkv, acc_proj, acc_fc1, acc_fc2, acc_ln, acc_rel) = acc
    ch = acc_fc2.shape[1]
    dim = ch // HEADS
    up, count, vec_at, rel_at, used = pack_rows(ch)
    rest = ch - LANE
    out[used:, :] = jnp.zeros((out.shape[0] - used, LANE), f32)
    out[rel_at:used, :] = acc_rel[...]
    blocks = [acc_conv[:ch, t * CPAD : t * CPAD + ch] for t in range(9)]
    qkv = [drop_lanes(acc_qkv[k], HEADS, dim) for k in range(3)]
    blocks += [qkv[k][:ch] for k in range(3)]
    blocks += [drop_rows(acc_proj[...], HEADS, dim)]
    fc1 = jnp.transpose(acc_fc1[...])
    fc2 = jnp.transpose(acc_fc2[...])
    blocks += [fc1[:ch, :ch], fc1[:ch, ch:]]
    blocks += [fc2[:, :ch], fc2[:, ch:]]
    out[:vec_at, :] = jnp.zeros((vec_at, LANE), f32)
    for k, block in enumerate(blocks):
        out[k * up : k * up + ch, :] = block[:, :LANE]
        at = (count + k // 2) * up
        half = (k % 2) * TOK
        out[at : at + ch, half : half + rest] = block[:, LANE:]
    ln = [jnp.sum(jnp.transpose(acc_ln[k]), axis=0, keepdims=True) for k in range(5)]
    vec = [
        ln[0],
        ln[1],
        qkv[0][ch : ch + 1, :],
        qkv[2][ch : ch + 1, :],
        acc_proj[dim : dim + 1, :],
        ln[2],
        ln[3],
        fc1[ch : ch + 1, :ch],
        fc1[ch : ch + 1, ch:],
        ln[4],
        acc_conv[ch : ch + 1, 4 * CPAD : 4 * CPAD + ch],
    ]
    vec = jnp.concatenate(vec, axis=0)
    diff = sr_ref[...] - hr_ref[...]
    luma = (65.481 * diff[:, 0] + 128.553 * diff[:, 1] + 24.966 * diff[:, 2]) / 255.0
    square = jnp.sum(luma * luma, axis=1, keepdims=True)
    mse = jnp.sum(square, axis=2, keepdims=True) * (1.0 / (luma.shape[1] * luma.shape[2]))
    psnr = jnp.sum(jnp.log(mse + 1e-06) * (-10.0 / 2.302585092994046), axis=0)
    out[vec_at : vec_at + 32, :] = jnp.zeros((32, LANE), f32)
    out[vec_at : vec_at + 11, :] = vec[:, :LANE]
    lane = lax.broadcasted_iota(jnp.int32, (1, LANE), 1)
    for k in range(3):
        piece = psnr.astype(bf16).astype(f32)
        out[vec_at + 11 + k : vec_at + 12 + k, :] = jnp.where(lane == device, piece, 0.0)
        psnr = psnr - piece
    out[vec_at + 16 : vec_at + 27, :rest] = vec[:, LANE:]


def whole(shape):
    return pl.BlockSpec(shape, lambda *_: (0,) * len(shape))


def acc_shapes(ch, hid):
    return [
        (CPAD, 9 * CPAD),
        (3, CPAD, CPAD),
        (CPAD, ch),
        (hid, CPAD),
        (hid, ch),
        (5, ch, LANE),
        (3 * TOK, LANE),
    ]


def scratches(ch, hid, px, vec_rows):
    v = pltpu.VMEM
    prep = [
        v((ch, vec_rows), f32),
        v((3 * CPAD, ch), bf16), v((ch, CPAD), bf16), v((hid, ch), bf16), v((ch, hid), bf16),
        v((ch, CPAD), bf16), v((ch, CPAD), bf16), v((ch, CPAD), bf16), v((CPAD, ch), bf16),
        v((ch, hid), bf16), v((hid, ch), bf16),
        v((9 * CPAD, ch), bf16),
        v((TOK, LANE), f32),
        v((TOK, LANE), f32),
        v((hid, LANE), f32),
        v((10, ch, LANE), f32),
        v((2, CPAD, LANE), f32),
    ]
    wins = px // TOK
    tmp = [
        v((px, 9 * CPAD), bf16),
        v((CPAD, px), bf16), v((CPAD, px), bf16), v((CPAD, px), bf16), v((hid, px), bf16), v((CPAD, px), bf16),
        v((wins, CPAD, LANE), bf16),
        v((wins, 3 * TOK, LANE), f32),
        v((wins, 3 * TOK, LANE), bf16),
        v((2, px, CPAD), bf16),
        v((ch, px), f32),
        v((CPAD, px), bf16),
        v((CPAD, px), bf16),
        v((2, px, CPAD), bf16),
        v((ch, px), f32),
        v((ch, px), f32),
        v((hid, px), f32),
        v((CPAD, px), bf16),
        v((CPAD, px), bf16),
        v((CPAD, px), bf16),
        v((8, px), f32),
        v((ch, px), bf16),
        v((hid, px), bf16),
        v((ch, px), f32),
    ]
    return prep + tmp


def halo_kernel(halo_ref, ig_ref, ig_out):
    kept = jnp.swapaxes(ig_ref[0], 0, 1)
    new = [halo_ref[0, r].astype(f32) for r in range(SHIFT)] + [kept[r] for r in range(SHIFT, WIN)]
    ig_out[0] = jnp.swapaxes(jnp.stack(new), 0, 1)


def bits_of(size):
    return list(range(size.bit_length() - 1))


def exchange_plan(sizes):
    (dp_axis, dp_size), (head_axis, head_size) = sizes
    first = (dp_axis, 0)
    rest = [(dp_axis, b) for b in bits_of(dp_size)[1:]]
    last = [(head_axis, b) for b in bits_of(head_size)]
    half = len(rest) // 2
    return first, [rest + last, rest[half:] + rest[:half] + last]


def exchange_kernel(
    first, orders, head_size,
    g_in, c1_in, c2_in, x_in, halo_in, conv_in, vec_ref,
    sum_ref, out_ref, halo_out,
    g, work, given, low, c1, c2, c_halo, x, conv, wc, cs, rows_s, out_s,
    send_sem, recv_sem, local_sem,
):
    count, ch, own_rows, image_side = x.shape
    rows = g.shape[0]
    mesh_id = pl.DeviceIdType.MESH
    here = lax.axis_index("head")
    upper = {"head": (here + 1) % head_size}
    lower = {"head": (here + head_size - 1) % head_size}

    def load(k, src, dst):
        copy = pltpu.make_async_copy(src, dst, local_sem.at[k])
        copy.start()
        return copy

    loads = [
        load(0, g_in, g),
        load(1, conv_in, conv),
        load(2, c1_in, c1),
        load(3, c2_in, c2),
        load(4, x_in, x),
    ]

    def meet(stage):
        axis, b = stage
        me = lax.axis_index(axis)
        step = 2**b
        bit = (me // step) % 2
        return {axis: me + (1 - 2 * bit) * step}, bit

    barrier = pltpu.get_barrier_semaphore()
    friends = [meet(stage)[0] for stage in [first] + orders[0]] + [upper, lower]
    for other in friends:
        pl.semaphore_signal(barrier, inc=1, device_id=other, device_id_type=mesh_id)
    pl.semaphore_wait(barrier, len(friends))

    used = [0]

    def send(src, dst, other):
        k = used[0]
        used[0] += 1
        copy = pltpu.make_async_remote_copy(
            src_ref=src,
            dst_ref=dst,
            send_sem=send_sem.at[k],
            recv_sem=recv_sem.at[k],
            device_id=other,
            device_id_type=mesh_id,
        )
        copy.start()
        return copy

    def span(start, size):
        return pl.ds(pl.multiple_of(start, 16), size)

    col = lax.broadcasted_iota(jnp.int32, (1, image_side, ch), 1)
    top = jnp.where(here == 0, 0.0, 1.0).astype(f32)
    bottom = jnp.where(here == head_size - 1, 0.0, 1.0).astype(f32)

    def prepare():
        loads[1].wait()
        wc[...] = jnp.zeros_like(wc)
        cs[...] = jnp.zeros_like(cs)
        for tap in range(9):
            wc[tap * TAP : tap * TAP + ch, :] = conv[tap // 3, tap % 3].astype(bf16)

    def conv_rows(image, block):
        for k in range(WIN + 2):
            r = block * WIN + k - 1 - SHIFT
            if r < 0:
                row = c_halo[image, r + SHIFT + 1 : r + SHIFT + 2]
            elif r < c1.shape[1]:
                row = c1[image, r : r + 1]
            else:
                row = c2[image, r - c1.shape[1] : r - c1.shape[1] + 1]
            row = row.astype(f32)
            if block == 0 and k == 0:
                row = row * top
            if block == own_rows // WIN - 1 and k == WIN + 1:
                row = row * bottom
            left = jnp.where(col == 0, 0.0, roll_cols(row, -1))
            right = jnp.where(col == image_side - 1, 0.0, roll_cols(row, 1))
            at = slice(k * image_side, (k + 1) * image_side)
            cs[at, 0:ch] = left[0].astype(bf16)
            cs[at, TAP : TAP + ch] = row[0].astype(bf16)
            cs[at, 2 * TAP : 2 * TAP + ch] = right[0].astype(bf16)
        total = vec_ref[10:11, :]
        for i in range(3):
            at = slice(i * image_side, (i + WIN) * image_side)
            total = total + nn(cs[at, :], wc[i * 3 * TAP : (i + 1) * 3 * TAP, :])
        for k in range(WIN):
            rows_s[image, block * WIN + k] = jnp.transpose(total[k * image_side : (k + 1) * image_side])

    stores = []

    def finish(image):
        out_s[image] = (jnp.swapaxes(rows_s[image], 0, 1) + x[image].astype(f32)).astype(bf16)
        stores.append(load(5 + image, out_s.at[image], out_ref.at[image]))

    blocks = own_rows // WIN
    inner = [(n, b) for n in range(count) for b in range(1, blocks)]
    outer = [(n, 0) for n in range(count)]
    stage_count = 2 * (1 + len(orders[0]))
    jobs = [[] for _ in range(stage_count)]
    for k, job in enumerate(inner + outer):
        jobs[min(1 + k * (stage_count - 2) // len(inner + outer), stage_count - 2)].append(job)

    halos = []

    def work_on(stage):
        if stage == 0:
            prepare()
        if stage == 1:
            for k in (2, 3, 4):
                loads[k].wait()
        for image, block in jobs[stage]:
            if block == 0 and image == 0:
                halos[0].wait()
            conv_rows(image, block)
            if block == 0:
                finish(image)

    loads[0].wait()
    other, bit = meet(first)
    half = rows // 2
    copy = send(g.at[span((1 - bit) * half, half)], given.at[pl.ds(0, half)], other)
    halos.append(send(c2_in.at[:, WIN - SHIFT - 1 :], c_halo, upper))
    halos.append(send(halo_in, halo_out, upper))
    work_on(0)
    copy.wait()
    keep = bit * half
    work[span(keep, half), :] = g[span(keep, half), :] + given[:half, :]
    unit = 16 * 2 ** len(orders[0])
    parts = half // unit
    cut = (parts + 1) // 2 * unit
    begin = [keep, keep + cut]
    size = [cut, half - cut]
    taken = half
    trail = [[], []]
    for s in range(len(orders[0])):
        flying = []
        for p in range(2):
            if size[p] == 0:
                continue
            other, bit = meet(orders[p][s])
            size[p] //= 2
            trail[p].append(begin[p])
            give = begin[p] + (1 - bit) * size[p]
            begin[p] = begin[p] + bit * size[p]
            flying.append((p, taken, send(work.at[span(give, size[p])], given.at[pl.ds(taken, size[p])], other)))
            taken += size[p]
        work_on(1 + s)
        for p, at, copy in flying:
            copy.wait()
            total = work[span(begin[p], size[p]), :] + given[at : at + size[p], :]
            if s < len(orders[0]) - 1:
                work[span(begin[p], size[p]), :] = total
            else:
                low[span(begin[p], size[p]), :] = total.astype(bf16)

    for s in reversed(range(len(orders[0]))):
        flying = []
        for p in range(2):
            if size[p] == 0:
                continue
            other, _ = meet(orders[p][s])
            here_now = low.at[span(begin[p], size[p])]
            flying.append(send(here_now, here_now, other))
            begin[p] = trail[p][s]
            size[p] *= 2
        work_on(2 * len(orders[0]) - s)
        for copy in flying:
            copy.wait()
    other, _ = meet(first)
    here_now = low.at[span(keep, half)]
    copy = send(here_now, here_now, other)
    work_on(stage_count - 1)
    copy.wait()
    sum_ref[...] = low[...]
    halos[1].wait()
    for copy in stores:
        copy.wait()


def exchange(packed, c1, c2, images, ig_halo, conv_weight, vectors, sizes):
    first, orders = exchange_plan(sizes)
    rows = packed.shape[0]
    count, ch, own_rows, image_side = images.shape
    vmem = pl.BlockSpec(memory_space=pltpu.VMEM)
    hbm = pl.BlockSpec(memory_space=pl.ANY)
    v = pltpu.VMEM
    sends = 2 + 2 + 4 * len(orders[0])
    return pl.pallas_call(
        functools.partial(exchange_kernel, first, orders, sizes[1][1]),
        in_specs=[hbm] * 6 + [vmem],
        out_specs=[vmem, hbm, hbm],
        out_shape=[
            jax.ShapeDtypeStruct(packed.shape, bf16),
            jax.ShapeDtypeStruct(images.shape, bf16),
            jax.ShapeDtypeStruct(ig_halo.shape, bf16),
        ],
        scratch_shapes=[
            v(packed.shape, f32),
            v(packed.shape, f32),
            v(packed.shape, f32),
            v(packed.shape, bf16),
            v(c1.shape, bf16),
            v(c2.shape, bf16),
            v((count, SHIFT + 1, image_side, ch), bf16),
            v(images.shape, bf16),
            v(conv_weight.shape, f32),
            v((9 * TAP, ch), bf16),
            v(((WIN + 2) * image_side, 3 * TAP), bf16),
            v((count, own_rows, ch, image_side), f32),
            v(images.shape, bf16),
            pltpu.SemaphoreType.DMA((sends,)),
            pltpu.SemaphoreType.DMA((sends,)),
            pltpu.SemaphoreType.DMA((5 + count,)),
        ],
        compiler_params=pltpu.CompilerParams(
            collective_id=0, has_side_effects=True, vmem_limit_bytes=60 * 1024 * 1024
        ),
        name="sum_gradients",
    )(packed, c1, c2, images, ig_halo, conv_weight, vectors)


def adam_kernel(scal, g_ref, *refs):
    weights, firsts, seconds = refs[0:7], refs[7:14], refs[14:21]
    norm_ref, psnr_ref, outs = refs[21], refs[22], refs[23:44]
    ch = weights[2].shape[0]
    up, count, vec_at, rel_at, used = pack_rows(ch)
    rest = ch - LANE

    def block(k):
        left = g_ref[k * up : (k + 1) * up, :].astype(f32)
        at = (count + k // 2) * up
        right = g_ref[at : at + up, :].astype(f32)
        if k % 2:
            right = pltpu.roll(right, TOK, 1)
        return jnp.concatenate([left, right[:, :rest]], axis=1)[:ch]

    vec_rows = g_ref[vec_at : vec_at + 32, :].astype(f32)
    vec = jnp.concatenate([vec_rows[:11], vec_rows[16:27, :rest]], axis=1)
    psnr = vec_rows[11:12] + vec_rows[12:13] + vec_rows[13:14]
    psnr_ref[...] = jnp.sum(psnr, axis=1, keepdims=True)

    span = 2 * WIN
    wide = span * span
    at = lax.broadcasted_iota(jnp.int32, (TOK, wide), 0)
    to = lax.broadcasted_iota(jnp.int32, (TOK, wide), 1)
    place = ((at >> 3) + (WIN - 1)) * span + (at & 7) + (WIN - 1)
    expand = (to == place).astype(f32).astype(bf16)
    pairs = g_ref[rel_at:used, :]
    rel_rows = []
    for p in range(3):
        for parity in range(2):
            part = pairs[p * TOK : (p + 1) * TOK, :].astype(f32)
            if parity:
                part = pltpu.roll(part, TOK, 1)
            spread = nn(part[:, :TOK].astype(bf16), expand)
            total = jnp.zeros((WIN, wide), f32)
            for row in range(WIN):
                piece = spread[row * WIN : (row + 1) * WIN]
                piece = pltpu.roll(piece, (wide - span * row) % wide, 1)
                total = total + piece
            line = total[0:1]
            for c in range(1, WIN):
                line = line + pltpu.roll(total, wide - c, 1)[c : c + 1]
            rel_rows.append(line)
    rel = jnp.concatenate(rel_rows, axis=0)
    rel = jnp.concatenate(
        [rel[:, k * span : k * span + span - 1] for k in range(span - 1)], axis=1
    )
    qkv = jnp.concatenate([block(9), block(10), block(11)], axis=1)
    fc1 = jnp.concatenate([block(13), block(14)], axis=1)
    fc2 = jnp.concatenate([block(15), block(16)], axis=1)
    small = [vec, qkv, block(12), rel, fc1, fc2]
    taps = [block(t) for t in range(9)]
    total = jnp.zeros((1, 1), f32)
    for g in small + taps:
        total = total + jnp.sum(jnp.sum(g * g, axis=0, keepdims=True), axis=1, keepdims=True)
    norm = jnp.sqrt(total)
    norm_ref[...] = norm
    clip = jnp.minimum(1.0, max_norm / (norm + 1e-06))
    fix_one, fix_two = scal[0], scal[1]

    def update(w, m1, m2, g, rate):
        g = g * clip
        m1 = beta_one * m1 + (1.0 - beta_one) * g
        m2 = beta_two * m2 + (1.0 - beta_two) * g * g
        step = (m1 / fix_one) / (jnp.sqrt(m2 / fix_two) + adam_eps)
        return w - rate * (step + decay_rate * w), m1, m2

    for k, g in enumerate(small):
        new = update(weights[k][...], firsts[k][...], seconds[k][...], g, vector_rate if k == 0 else learn_rate)
        for ref, value in zip(outs[3 * k : 3 * k + 3], new):
            ref[...] = value
    for t, g in enumerate(taps):
        at = (t // 3, t % 3)
        new = update(weights[6][at], firsts[6][at], seconds[6][at], g, learn_rate)
        for ref, value in zip(outs[18:21], new):
            ref[at] = value


def relative_onehot_keys_first():
    position = np.arange(TOK)
    pos_row, pos_col = position // WIN, position % WIN
    span = 2 * WIN - 1
    index = (pos_row[None, :] - pos_row[:, None] + WIN - 1) * span + (
        pos_col[None, :] - pos_col[:, None] + WIN - 1
    )
    return index.reshape(-1), span * span


def on_device(
    images, cotangent, valid_size,
    vectors, vectors_first, vectors_second,
    qkv_weight, qkv_first, qkv_second,
    proj_weight, proj_first, proj_second,
    rel_table, rel_first, rel_second,
    fc1_weight, fc1_first, fc1_second,
    fc2_weight, fc2_first, fc2_second,
    conv_weight, conv_first, conv_second,
    step, sr_crops, hr_crops, psnr_running,
):
    count, own_rows, image_side, ch = images.shape
    out_shape = (count, ch, own_rows, image_side)
    hid = fc1_weight.shape[1]
    px = image_side * WIN
    blocks = own_rows // WIN
    heads = lax.axis_size("head")
    place = lax.axis_index("head")
    to_lower = [((i + 1) % heads, i) for i in range(heads)]
    info = jnp.concatenate(
        [
            jnp.stack([place, (place == heads - 1).astype(jnp.int32)]).astype(jnp.int32),
            valid_size.astype(jnp.int32),
            ((lax.axis_index("dp") * heads + place) % LANE)[None].astype(jnp.int32),
        ]
    )
    images = images.transpose(0, 3, 1, 2)
    cotangent = cotangent.transpose(0, 3, 1, 2)
    halo = lax.ppermute(
        jnp.concatenate([images[:, :, :SHIFT], cotangent[:, :, : SHIFT + 1]], axis=2), "head", to_lower
    )

    index, span = relative_onehot_keys_first()
    onehot = (jnp.asarray(index)[:, None] == jnp.arange(span)[None, :]).astype(f32)
    bias = jnp.dot(onehot, rel_table, precision=highest)
    bias = bias.reshape(TOK, TOK, 3, 2).transpose(2, 0, 3, 1).reshape(3, TOK, LANE)

    wts = (vectors, qkv_weight, proj_weight, fc1_weight, fc2_weight.T, conv_weight, bias)
    wts_specs = [whole(w.shape) for w in wts]
    acc_dims = acc_shapes(ch, hid)
    acc_types = [jax.ShapeDtypeStruct(s, f32) for s in acc_dims]
    smem = pl.BlockSpec(memory_space=pltpu.SMEM)
    params = pltpu.CompilerParams(
        dimension_semantics=("arbitrary", "arbitrary"), vmem_limit_bytes=60 * 1024 * 1024
    )
    view = lambda rows, at, dims: pl.BlockSpec((1, ch, rows, image_side), lambda n, *_: (n, 0, at, 0))
    c_block = lambda size: pl.BlockSpec((1, size, image_side, ch), lambda n, *_: (n, 0, 0, 0))
    row_view = pltpu.VMEM((own_rows, ch, image_side), f32)
    c1, ig, *acc = pl.pallas_call(
        functools.partial(inner_kernel, image_side, own_rows),
        grid=(count, blocks - 1),
        in_specs=[smem, view(own_rows, 0, 2), view(own_rows, 0, 2), *wts_specs],
        out_specs=[
            pl.BlockSpec((1, WIN, image_side, ch), lambda n, r: (n, r, 0, 0)),
            view(own_rows, 0, 2),
            *[whole(s) for s in acc_dims],
        ],
        out_shape=[
            jax.ShapeDtypeStruct((count, own_rows - WIN, image_side, ch), bf16),
            jax.ShapeDtypeStruct(out_shape, f32),
            *acc_types,
        ],
        scratch_shapes=[row_view] * 3 + scratches(ch, hid, px, vectors.shape[0]),
        compiler_params=params,
        name="inner_windows",
    )(info, images, cotangent, *wts)
    device_count = lax.axis_size("dp") * heads
    unit = 16 * device_count
    rows = -(-pack_rows(ch)[-1] // unit) * unit
    c2, ig, ig_halo, packed = pl.pallas_call(
        functools.partial(last_kernel, image_side, own_rows),
        grid=(count,),
        in_specs=[
            smem,
            view(WIN, blocks - 1, 1),
            view(WIN, blocks - 1, 1),
            view(2 * SHIFT + 1, 0, 1),
            view(WIN, blocks - 1, 1),
            *wts_specs,
            *[whole(s) for s in acc_dims],
            whole(sr_crops.shape),
            whole(hr_crops.shape),
        ],
        out_specs=[
            c_block(WIN),
            view(WIN, blocks - 1, 1),
            pl.BlockSpec((1, SHIFT, ch, image_side), lambda n: (n, 0, 0, 0)),
            whole((rows, LANE)),
        ],
        out_shape=[
            jax.ShapeDtypeStruct((count, WIN, image_side, ch), bf16),
            jax.ShapeDtypeStruct(out_shape, f32),
            jax.ShapeDtypeStruct((count, SHIFT, ch, image_side), bf16),
            jax.ShapeDtypeStruct((rows, LANE), f32),
        ],
        input_output_aliases={4: 1},
        scratch_shapes=[pltpu.VMEM(s, f32) for s in acc_dims] + scratches(ch, hid, px, vectors.shape[0]),
        compiler_params=pltpu.CompilerParams(
            dimension_semantics=("arbitrary",), vmem_limit_bytes=60 * 1024 * 1024
        ),
        name="last_windows",
    )(info, images, cotangent, halo, ig, *wts, *acc, sr_crops, hr_crops)

    summed, output, ig_halo = exchange(
        packed, c1, c2, images, ig_halo, conv_weight, vectors, (("dp", lax.axis_size("dp")), ("head", heads))
    )
    image_grad = pl.pallas_call(
        halo_kernel,
        grid=(count,),
        in_specs=[pl.BlockSpec((1, SHIFT, ch, image_side), lambda n: (n, 0, 0, 0)), view(WIN, 0, 1)],
        out_specs=view(WIN, 0, 1),
        out_shape=jax.ShapeDtypeStruct(out_shape, f32),
        input_output_aliases={1: 0},
        name="halo_rows",
    )(ig_halo, ig)
    output, image_grad = output.transpose(0, 2, 3, 1), image_grad.transpose(0, 2, 3, 1)

    step_count = step[0].astype(f32)
    scal = jnp.stack([1.0 - beta_one**step_count, 1.0 - beta_two**step_count])
    weights = (vectors, qkv_weight, proj_weight, rel_table.T, fc1_weight, fc2_weight.T, conv_weight)
    firsts = (vectors_first, qkv_first, proj_first, rel_first.T, fc1_first, fc2_first.T, conv_first)
    seconds = (vectors_second, qkv_second, proj_second, rel_second.T, fc1_second, fc2_second.T, conv_second)
    vmem = pl.BlockSpec(memory_space=pltpu.VMEM)
    grad_norm, psnr, *updated = pl.pallas_call(
        adam_kernel,
        in_specs=[smem] + [vmem] * 22,
        out_specs=[vmem] * 23,
        out_shape=[jax.ShapeDtypeStruct((1, 1), f32)] * 2
        + [jax.ShapeDtypeStruct(w.shape, f32) for w in weights for _ in range(3)],
        compiler_params=pltpu.CompilerParams(vmem_limit_bytes=60 * 1024 * 1024),
        name="adam",
    )(scal, summed, *weights, *firsts, *seconds)
    for k in (9, 10, 11, 15, 16, 17):
        updated[k] = updated[k].T
    psnr_total = psnr_running + psnr.reshape(1)
    return (output, image_grad, grad_norm.reshape(1), psnr_total, *updated)


def solution(mesh):
    pixels = P("dp", "head", None, None)
    crops = P(("dp", "head"), None, None, None)
    placed = (pixels, pixels, P("dp")) + (P(),) * 22 + (crops, crops, P())
    return jax.shard_map(
        on_device,
        mesh=mesh,
        in_specs=placed,
        out_specs=(pixels, pixels) + (P(),) * 23,
        check_vma=False,
    )
```

```python
import functools

import jax
import jax.numpy as jnp
import numpy as np
from jax import lax
from jax.experimental import pallas as pl
from jax.experimental.pallas import tpu as pltpu
from jax.sharding import PartitionSpec as P

WIN = 8
TOK = WIN * WIN
SHIFT = WIN // 2
LANE = 128
TAP = 256
HPAD = 32
HEADS = 6
CPAD = HEADS * HPAD

eps_norm = 1e-05
neg_mask = -100.0
max_norm = 1.0
learn_rate = 0.03
vector_rate = 0.2
beta_one = 0.9
beta_two = 0.999
adam_eps = 1e-08
decay_rate = 0.01
highest = lax.Precision.HIGHEST
f32 = jnp.float32
bf16 = jnp.bfloat16


def nn(a, b):
    return lax.dot_general(a, b, (((1,), (0,)), ((), ())), preferred_element_type=f32)


def nt(a, b):
    return lax.dot_general(a, b, (((1,), (1,)), ((), ())), preferred_element_type=f32)


def pad_heads(rows, heads):
    dim = rows.shape[0] // heads
    gap = jnp.zeros((HPAD - dim, rows.shape[1]), rows.dtype)
    parts = []
    for h in range(heads):
        parts += [rows[h * dim : (h + 1) * dim], gap]
    return jnp.concatenate(parts, axis=0)


def drop_rows(rows, heads, dim):
    return jnp.concatenate([rows[h * HPAD : h * HPAD + dim] for h in range(heads)], axis=0)


def drop_lanes(rows, heads, dim):
    return jnp.concatenate([rows[:, h * HPAD : h * HPAD + dim] for h in range(heads)], axis=1)


def to_tokens(rows):
    side = rows.shape[1]
    return jnp.concatenate(
        [rows[:, w * WIN : (w + 1) * WIN, :].reshape(TOK, rows.shape[2]) for w in range(side // WIN)],
        axis=0,
    )


def from_tokens(tokens):
    count = tokens.shape[0] // TOK
    return jnp.concatenate(
        [tokens[w * TOK : (w + 1) * TOK].reshape(WIN, WIN, tokens.shape[1]) for w in range(count)],
        axis=1,
    )


def roll_cols(rows, by):
    side = rows.shape[1]
    by = by % side
    return jnp.concatenate([rows[:, by:, :], rows[:, :by, :]], axis=1)


def block_step(x_rows, gy_rows, first_step, edge, base_row, valid, image_side, wts, prep, acc, tmp, c_out):
    (vec_ref, qkv_ref, proj_ref, fc1_ref, fc2_ref, conv_ref, bias_ref) = wts
    (vecT, wqkvT, wpT, w1T, w2T, wq, wk, wv, wp, w1, w2, wc, colmask, rowmask, b1T, wide_vec, head_vec) = prep
    (acc_conv, acc_qkv, acc_proj, acc_fc1, acc_fc2, acc_ln, acc_rel) = acc
    (g9, a_aug, o_aug, m_aug, g_aug, c_aug, qeo_s, p_s, pb_s, kv_s, first_s, do_s, dq_s, dkv_s, u2_s, xT_s, slope_s, vt_s, qt_s, kt_s, inv_s, db_s, dh_s) = tmp
    ch = x_rows.shape[2]
    dim = ch // HEADS
    hid = fc1_ref.shape[1]
    px = x_rows.shape[1] * WIN
    pairs = px // LANE
    ones_row = dim

    @pl.when(first_step)
    def _():
        vecT[...] = jnp.transpose(vec_ref[...])
        for k in range(10):
            wide_vec[k] = jnp.broadcast_to(vecT[:, k : k + 1], (ch, LANE))
        for k in range(2):
            head_vec[k] = pad_heads(wide_vec[2 + k], HEADS)
        b1T[:ch, :] = wide_vec[7]
        b1T[ch:, :] = wide_vec[8]
        for k, dst in enumerate((wq, wk, wv)):
            part = pad_heads(jnp.transpose(qkv_ref[:, k * ch : (k + 1) * ch]), HEADS)
            wqkvT[k * CPAD : (k + 1) * CPAD, :] = part.astype(bf16)
            dst[...] = jnp.transpose(part).astype(bf16)
        padded = pad_heads(proj_ref[...], HEADS)
        wp[...] = padded.astype(bf16)
        wpT[...] = jnp.transpose(padded).astype(bf16)
        w1[...] = fc1_ref[...].astype(bf16)
        w1T[...] = jnp.transpose(fc1_ref[...]).astype(bf16)
        w2T[...] = fc2_ref[...].astype(bf16)
        w2[...] = jnp.transpose(fc2_ref[...]).astype(bf16)
        wc[...] = jnp.zeros_like(wc)
        g9[...] = jnp.zeros_like(g9)
        for tap in range(9):
            wc[:, tap * CPAD : tap * CPAD + ch] = conv_ref[tap // 3, tap % 3].astype(bf16)
        key = lax.broadcasted_iota(jnp.int32, (TOK, LANE), 0)
        query = lax.broadcasted_iota(jnp.int32, (TOK, LANE), 1) & (TOK - 1)
        one = lambda m: m.astype(f32)
        colmask[...] = one(((key & 7) < SHIFT) != ((query & 7) < SHIFT))
        rowmask[...] = one(((key >> 3) < SHIFT) != ((query >> 3) < SHIFT))
        for ref in (a_aug, m_aug, c_aug):
            pad = ref.shape[0] - ch
            ref[ch:, :] = (lax.broadcasted_iota(jnp.int32, (pad, px), 0) == 0).astype(f32).astype(bf16)

    def column(k):
        return wide_vec[k]

    def stats(v):
        mean = jnp.sum(v, axis=0, keepdims=True) * (1.0 / ch)
        cen = v - mean
        var = jnp.sum(cen * cen, axis=0, keepdims=True) * (1.0 / ch)
        inv = lax.rsqrt(var + eps_norm)
        return cen * inv, inv

    def ln_back(grad, u, inv, gain):
        t = grad * gain
        mean_t = jnp.sum(t, axis=0, keepdims=True) * (1.0 / ch)
        mean_tu = jnp.sum(t * u, axis=0, keepdims=True) * (1.0 / ch)
        return inv * (t - mean_t - u * mean_tu)

    chunks = [slice(k * LANE, (k + 1) * LANE) for k in range(px // LANE)]
    third = hid // 3
    bands = [slice(k * third, (k + 1) * third) for k in range(3)]

    keep = jnp.where(edge, 0.0, 1.0).astype(f32)
    col = lax.broadcasted_iota(jnp.int32, (1, image_side, ch), 1)
    moved = {}

    def build_tap(tap):
        i, j = tap % 3, tap // 3
        if i == 0:
            shifted = roll_cols(gy_rows, SHIFT + 1 - j)
            if j == 0:
                shifted = jnp.where(col == image_side - SHIFT - 1, 0.0, shifted)
            if j == 2:
                shifted = jnp.where(col == image_side - SHIFT, 0.0, shifted)
            moved[j] = shifted
        rows = [moved[j][r + 2 - i : r + 3 - i] for r in range(WIN)]
        if i == 0:
            rows[SHIFT - 1] = rows[SHIFT - 1] * keep
        if i == 2:
            rows[SHIFT] = rows[SHIFT] * keep
        at = (3 * i + j) * CPAD
        g9[:, at : at + ch] = to_tokens(jnp.concatenate(rows, axis=0)).astype(bf16)

    x_tok = to_tokens(roll_cols(x_rows, SHIFT))
    for at in chunks:
        xT = jnp.transpose(x_tok[at])
        xT_s[:, at] = xT
        u1, _ = stats(xT)
        a_aug[:ch, at] = (u1 * column(0) + column(1)).astype(bf16)
    scale = dim ** (-0.5)
    qkv_all = nn(wqkvT[...], a_aug[:ch, :])
    for at in chunks:
        qt_s[:, at] = ((qkv_all[:CPAD, at] + head_vec[0]) * scale).astype(bf16)
        kT = qkv_all[CPAD : 2 * CPAD, at].astype(bf16)
        vT = (qkv_all[2 * CPAD :, at] + head_vec[1]).astype(bf16)
        kt_s[:, at] = kT
        vt_s[:, at] = vT
        kv_s[0, at, :] = jnp.transpose(kT.astype(f32)).astype(bf16)
        kv_s[1, at, :] = jnp.transpose(vT.astype(f32)).astype(bf16)

    def low_lanes(rows):
        return lax.broadcasted_iota(jnp.int32, (rows, LANE), 1) < TOK

    def swap(slab):
        return pltpu.roll(slab, TOK, 1)

    def only_low(v):
        return jnp.where(low_lanes(v.shape[0]), v, jnp.zeros_like(v))

    def only_high(v):
        return jnp.where(low_lanes(v.shape[0]), jnp.zeros_like(v), v)

    def head_rows(v, h):
        return v[h * HPAD : (h + 1) * HPAD]

    def dup(slab):
        slab = slab.astype(f32)
        other = swap(slab)
        out = []
        for low, high in ((slab, other), (other, slab)):
            rows = [
                only_high(head_rows(high, h)) if h % 2 else only_low(head_rows(low, h)) for h in range(HEADS)
            ]
            out.append(jnp.concatenate(rows, axis=0).astype(bf16))
        return out

    def spread(slab):
        slab = slab.astype(f32)
        other = swap(slab)
        two = 2 * HPAD
        gap = jnp.zeros((two, TOK), f32)
        wide = jnp.zeros((two, LANE), f32)
        out = []
        for low, high in ((slab, other), (other, slab)):
            rows = [
                jnp.concatenate([only_low(low[:two]), gap], axis=1),
                jnp.concatenate([only_high(high[two : 2 * two]), gap], axis=1),
                jnp.concatenate([wide, low[2 * two :, :TOK]], axis=1),
            ]
            out.append(jnp.concatenate(rows, axis=0).astype(bf16))
        return out

    def merge(one, two):
        rows = []
        for h in range(HEADS):
            first, second = head_rows(one, h), head_rows(two, h)
            if h % 2:
                rows.append(jnp.where(low_lanes(HPAD), swap(first), second))
            else:
                rows.append(jnp.where(low_lanes(HPAD), first, swap(second)))
        return jnp.concatenate(rows, axis=0)

    def by_pair(rows):
        front, back = rows[:, :LANE], rows[:, LANE:]
        zero_back = jnp.zeros_like(back)
        return jnp.concatenate(
            [
                jnp.concatenate([only_low(front), zero_back], axis=1),
                jnp.concatenate([only_high(front), zero_back], axis=1),
                jnp.concatenate([jnp.zeros_like(front), back], axis=1),
            ],
            axis=0,
        )

    def pick_pair(stacked):
        front = jnp.where(low_lanes(TOK), stacked[:TOK, :LANE], stacked[TOK : 2 * TOK, :LANE])
        return jnp.concatenate([front, stacked[2 * TOK :, LANE:]], axis=1)

    key = lax.broadcasted_iota(jnp.int32, (TOK, LANE), 0)
    key_row = base_row + (key >> 3)
    key_row = jnp.where(key_row >= image_side, key_row - image_side, key_row)
    out_row = key_row >= valid
    edge_f = jnp.where(edge, neg_mask, 0.0).astype(f32)

    def scores_of(pp):
        q_pair = dup(qt_s[:, chunks[pp]])
        raw = []
        for half in range(2):
            w = 2 * pp + half
            qeo_s[w] = q_pair[half]
            raw.append(nn(by_pair(kv_s[0, w * TOK : (w + 1) * TOK, :]), q_pair[half]))
        return raw

    def soften(pp, raw):
        for half in range(2):
            w = 2 * pp + half
            key_col = (key & 7) + (w * WIN + SHIFT)
            apart = rowmask[...] * edge_f
            if w == 2 * pairs - 1:
                key_col = jnp.where(key_col >= image_side, key_col - image_side, key_col)
                apart = jnp.where(colmask[...] > 0.5, neg_mask, apart)
            extra = apart + jnp.where(out_row | (key_col >= valid), neg_mask, 0.0)
            s = raw[half].reshape(3, TOK, LANE) + bias_ref[...] + extra[None]
            top = jnp.max(s, axis=1, keepdims=True)
            e = jnp.exp(s - top)
            p = e / jnp.sum(e, axis=1, keepdims=True)
            p = p.reshape(3 * TOK, LANE)
            p_s[w] = p
            pb_s[w] = p.astype(bf16)

    def mix(pp):
        v_pair = spread(vt_s[:, chunks[pp]])
        return [nn(v_pair[half], pb_s[2 * pp + half]) for half in range(2)]

    def place(pp, mixed):
        o_aug[:, chunks[pp]] = merge(*mixed).astype(bf16)

    raws, mixes = {}, {}
    for t in range(pairs + 3):
        if 0 <= t - 2 < pairs:
            mixes[t - 2] = mix(t - 2)
        if t < pairs:
            raws[t] = scores_of(t)
        if 0 <= t - 1 < pairs:
            soften(t - 1, raws.pop(t - 1))
        if 0 <= t - 3 < pairs:
            place(t - 3, mixes.pop(t - 3))
        if t < 9:
            build_tap(t)
    o_aug[ones_row : ones_row + 1, :] = jnp.ones((1, px), bf16)

    attn = nn(wpT[...], o_aug[...])
    part = px // 3
    conv_back = [nt(wc[...], g9[:part, :])]
    for at in chunks:
        first = xT_s[:, at] + (attn[:, at] + column(4))
        first_s[:, at] = first
        u2, inv2 = stats(first)
        u2_s[:, at] = u2
        inv_s[0:1, at] = inv2
        m_aug[:ch, at] = (u2 * column(5) + column(6)).astype(bf16)
    hidden_all = nn(w1T[...], m_aug[:ch, :])
    conv_back.append(nt(wc[...], g9[part : 2 * part, :]))
    for at in chunks:
        for band in bands:
            hidden = hidden_all[band, at] + b1T[band, :]
            cdf = 0.5 * (1.0 + lax.erf(hidden * 0.7071067811865476))
            g_aug[band, at] = (hidden * cdf).astype(bf16)
            slope_s[band, at] = cdf + hidden * jnp.exp(-0.5 * hidden * hidden) * 0.3989422804014327
    branch = nn(w2T[...], g_aug[...])
    conv_back.append(nt(wc[...], g9[2 * part :, :]))
    c_rows = []
    for at in chunks:
        cT = (first_s[:, at] + (branch[:, at] + column(9))).astype(bf16)
        c_aug[:ch, at] = cT
        c_rows.append(jnp.transpose(cT.astype(f32)))
    c_out[0] = roll_cols(from_tokens(jnp.concatenate(c_rows, axis=0)), -SHIFT).astype(bf16)

    dsecond = jnp.concatenate(conv_back, axis=1)
    for at in chunks:
        dbT = dsecond[:, at].astype(bf16)
        db_s[:, at] = dbT
        acc_ln[4] += dbT.astype(f32)
    dg = nn(w2[...], db_s[...])
    acc_fc2[...] += nt(g_aug[...], db_s[...])
    for at in chunks:
        for band in bands:
            dh_s[band, at] = (dg[band, at] * slope_s[band, at]).astype(bf16)
    dm_all = nn(w1[...], dh_s[...])
    acc_fc1[...] += nt(dh_s[...], m_aug[...])
    for at in chunks:
        u2 = u2_s[:, at]
        dm = dm_all[:, at]
        acc_ln[2] += dm * u2
        acc_ln[3] += dm
        dfirst = dsecond[:, at] + ln_back(dm, u2, inv_s[0:1, at], column(5))
        first_s[:, at] = dfirst
        db_s[:, at] = dfirst.astype(bf16)
    do_all = nn(wp[...], db_s[...])
    acc_proj[...] += nt(o_aug[...], db_s[...])
    for at in chunks:
        do_s[:, at] = do_all[:, at].astype(bf16)

    rel_sum = jnp.zeros((3 * TOK, LANE), f32)

    def probs_grad(pp):
        do_pair = dup(do_s[:, chunks[pp]])
        dps, dvs = [], []
        for half in range(2):
            w = 2 * pp + half
            dps.append(nn(by_pair(kv_s[1, w * TOK : (w + 1) * TOK, :]), do_pair[half]))
            dvs.append(nt(pb_s[w], do_pair[half]))
        return dps, dvs

    def scores_grad(pp, dps, dvs, rel_sum):
        out = []
        for half in range(2):
            w = 2 * pp + half
            p = p_s[w].reshape(3, TOK, LANE)
            dp = dps[half].reshape(3, TOK, LANE)
            ds = p * (dp - jnp.sum(p * dp, axis=1, keepdims=True))
            ds = ds.reshape(3 * TOK, LANE).astype(bf16)
            rel_sum = rel_sum + ds.astype(f32)
            out.append(ds)
            dkv_s[1, w * TOK : (w + 1) * TOK, :] = pick_pair(dvs[half]).astype(bf16)
        return out, rel_sum

    def inner_grads(pp, ds):
        k_pair = spread(kt_s[:, chunks[pp]])
        dks = [nt(ds[half], qeo_s[2 * pp + half]) for half in range(2)]
        dqs = [nn(k_pair[half], ds[half]) for half in range(2)]
        return dks, dqs

    def place_grads(pp, dks, dqs):
        for half in range(2):
            w = 2 * pp + half
            dkv_s[0, w * TOK : (w + 1) * TOK, :] = pick_pair(dks[half]).astype(bf16)
        dq_s[:, chunks[pp]] = merge(*dqs).astype(bf16)

    first_part, second_part, third_part = {}, {}, {}
    for t in range(pairs + 3):
        if 0 <= t - 2 < pairs:
            third_part[t - 2] = inner_grads(t - 2, second_part.pop(t - 2))
        if t < pairs:
            first_part[t] = probs_grad(t)
        if 0 <= t - 1 < pairs:
            second_part[t - 1], rel_sum = scores_grad(t - 1, *first_part.pop(t - 1), rel_sum)
        if 0 <= t - 3 < pairs:
            place_grads(t - 3, *third_part.pop(t - 3))
        at = slice(t * TAP, min((t + 1) * TAP, 9 * CPAD))
        if at.start < at.stop:
            acc_conv[:, at] += nn(c_aug[...], g9[:, at])
    acc_rel[...] += rel_sum

    dqT = dq_s[...]
    da_q = nn(wq[...], dqT)
    da_kv = nt(wk[...], dkv_s[0]) + nt(wv[...], dkv_s[1])
    acc_qkv[0] += nt(a_aug[...], dqT) * scale
    acc_qkv[1] += nn(a_aug[...], dkv_s[0])
    acc_qkv[2] += nn(a_aug[...], dkv_s[1])
    ig_rows = []
    for at in chunks:
        da = da_q[:, at] * scale + da_kv[:, at]
        u1, inv1 = stats(xT_s[:, at])
        acc_ln[0] += da * u1
        acc_ln[1] += da
        ig_rows.append(jnp.transpose(first_s[:, at] + ln_back(da, u1, inv1, column(0))))
    return roll_cols(from_tokens(jnp.concatenate(ig_rows, axis=0)), -SHIFT) + gy_rows[1 : 1 + WIN]


N_ACC = 7
N_PREP = 17
N_WTS = 7


def natural_rows(ref, side, every, start, count):
    ch = ref.shape[0] // every
    rows = [ref[pl.ds(start + r, ch, stride=every), :] for r in range(count)]
    return jnp.stack([jnp.transpose(row)[:side] for row in rows])


def inner_kernel(image_side, own_rows, info, x_ref, gy_ref, *refs):
    wts, refs = refs[:N_WTS], refs[N_WTS:]
    c_out, ig_out, refs = refs[0], refs[1], refs[2:]
    acc, refs = refs[:N_ACC], refs[N_ACC:]
    x_s, gy_s, ig_s, refs = *refs[:3], refs[3:]
    prep, tmp = refs[:N_PREP], refs[N_PREP:]
    image, row_block = pl.program_id(0), pl.program_id(1)
    first_step = (image == 0) & (row_block == 0)

    @pl.when(first_step)
    def _():
        for ref in acc:
            ref[...] = jnp.zeros_like(ref)
        ig_s[...] = jnp.zeros_like(ig_s)

    @pl.when(row_block == 0)
    def _():
        ch = x_ref.shape[1]
        x_s[:, :image_side] = x_ref[0].astype(f32).reshape(ch * own_rows, image_side)
        gy_s[:, :image_side] = gy_ref[0].astype(f32).reshape(ch * own_rows, image_side)

    start = row_block * WIN + SHIFT
    x_rows = natural_rows(x_s, image_side, own_rows, start, WIN)
    gy_rows = natural_rows(gy_s, image_side, own_rows, start - 1, WIN + 2)
    base_row = info[0] * own_rows + start
    ig = block_step(
        x_rows, gy_rows, first_step, False, base_row, info[2 + image], image_side, wts, prep, acc, tmp, c_out
    )
    for r in range(WIN):
        ig_s[pl.ds(start + r, ig_out.shape[1], stride=own_rows), :image_side] = jnp.transpose(ig[r])

    @pl.when(row_block == pl.num_programs(1) - 1)
    def _():
        ig_out[0] = ig_s[:, :image_side].reshape(ig_out.shape[1:])


def last_kernel(image_side, own_rows, info, x_ref, gy_ref, halo_ref, ig_ref, *refs):
    wts, refs = refs[:N_WTS], refs[N_WTS:]
    acc_in, refs = refs[:N_ACC], refs[N_ACC:]
    sr_ref, hr_ref, c_out, ig_out, ig_halo, pack_out, refs = *refs[:6], refs[6:]
    acc, refs = refs[:N_ACC], refs[N_ACC:]
    x_s, gy_s, halo_s, ig_s, refs = *refs[:4], refs[4:]
    prep, tmp = refs[:N_PREP], refs[N_PREP:]
    image = pl.program_id(0)
    first_step = image == 0

    @pl.when(first_step)
    def _():
        for ref, given in zip(acc, acc_in):
            ref[...] = given[...]

    ch = x_ref.shape[1]
    halo_rows = halo_s.shape[0] // ch
    x_s[:, :image_side] = x_ref[0].astype(f32).reshape(ch * WIN, image_side)
    gy_s[:, :image_side] = gy_ref[0].astype(f32).reshape(ch * WIN, image_side)
    halo = halo_ref[0].astype(f32)
    fill = jnp.zeros((ch, halo_rows - halo.shape[1], image_side), f32)
    halo_s[:, :image_side] = jnp.concatenate([halo, fill], axis=1).reshape(ch * halo_rows, image_side)
    x_rows = jnp.concatenate(
        [
            natural_rows(x_s, image_side, WIN, SHIFT, SHIFT),
            natural_rows(halo_s, image_side, halo_rows, 0, SHIFT),
        ],
        axis=0,
    )
    gy_rows = jnp.concatenate(
        [
            natural_rows(gy_s, image_side, WIN, SHIFT - 1, SHIFT + 1),
            natural_rows(halo_s, image_side, halo_rows, SHIFT, SHIFT + 1),
        ],
        axis=0,
    )
    base_row = info[0] * own_rows + own_rows - SHIFT
    ig = block_step(
        x_rows, gy_rows, first_step, info[1] == 1, base_row, info[2 + image], image_side, wts, prep, acc, tmp, c_out
    )
    ig_s[:, :image_side] = ig_ref[0].reshape(ch * WIN, image_side)
    for r in range(SHIFT):
        ig_s[pl.ds(SHIFT + r, ch, stride=WIN), :image_side] = jnp.transpose(ig[r])
    ig_out[0] = ig_s[:, :image_side].reshape(ch, WIN, image_side)
    ig_halo[0] = jnp.concatenate([jnp.transpose(ig[SHIFT + r]) for r in range(SHIFT)], axis=1).astype(bf16)

    @pl.when(image == pl.num_programs(0) - 1)
    def _():
        pack_gradients(info[2 + pl.num_programs(0)], acc, sr_ref, hr_ref, pack_out)


def pack_rows(ch):
    up = -(-ch // 8) * 8
    blocks = 17
    vec_at = (blocks + (blocks + 1) // 2) * up
    return up, blocks, vec_at, vec_at + 32, vec_at + 32 + 3 * TOK


def pack_gradients(device, acc, sr_ref, hr_ref, out):
    (acc_conv, acc_qkv, acc_proj, acc_fc1, acc_fc2, acc_ln, acc_rel) = acc
    ch = acc_fc2.shape[1]
    dim = ch // HEADS
    up, count, vec_at, rel_at, used = pack_rows(ch)
    rest = ch - LANE
    out[used:, :] = jnp.zeros((out.shape[0] - used, LANE), f32)
    out[rel_at:used, :] = acc_rel[...]
    blocks = [acc_conv[:ch, t * CPAD : t * CPAD + ch] for t in range(9)]
    qkv = [drop_lanes(acc_qkv[k], HEADS, dim) for k in range(3)]
    blocks += [qkv[k][:ch] for k in range(3)]
    blocks += [drop_rows(acc_proj[...], HEADS, dim)]
    fc1 = jnp.transpose(acc_fc1[...])
    fc2 = jnp.transpose(acc_fc2[...])
    blocks += [fc1[:ch, :ch], fc1[:ch, ch:]]
    blocks += [fc2[:, :ch], fc2[:, ch:]]
    out[:vec_at, :] = jnp.zeros((vec_at, LANE), f32)
    for k, block in enumerate(blocks):
        out[k * up : k * up + ch, :] = block[:, :LANE]
        at = (count + k // 2) * up
        half = (k % 2) * TOK
        out[at : at + ch, half : half + rest] = block[:, LANE:]
    ln = [jnp.sum(jnp.transpose(acc_ln[k]), axis=0, keepdims=True) for k in range(5)]
    vec = [
        ln[0],
        ln[1],
        qkv[0][ch : ch + 1, :],
        qkv[2][ch : ch + 1, :],
        acc_proj[dim : dim + 1, :],
        ln[2],
        ln[3],
        fc1[ch : ch + 1, :ch],
        fc1[ch : ch + 1, ch:],
        ln[4],
        acc_conv[ch : ch + 1, 4 * CPAD : 4 * CPAD + ch],
    ]
    vec = jnp.concatenate(vec, axis=0)
    diff = sr_ref[...] - hr_ref[...]
    luma = (65.481 * diff[:, 0] + 128.553 * diff[:, 1] + 24.966 * diff[:, 2]) / 255.0
    square = jnp.sum(luma * luma, axis=1, keepdims=True)
    mse = jnp.sum(square, axis=2, keepdims=True) * (1.0 / (luma.shape[1] * luma.shape[2]))
    psnr = jnp.sum(jnp.log(mse + 1e-06) * (-10.0 / 2.302585092994046), axis=0)
    out[vec_at : vec_at + 32, :] = jnp.zeros((32, LANE), f32)
    out[vec_at : vec_at + 11, :] = vec[:, :LANE]
    lane = lax.broadcasted_iota(jnp.int32, (1, LANE), 1)
    for k in range(3):
        piece = psnr.astype(bf16).astype(f32)
        out[vec_at + 11 + k : vec_at + 12 + k, :] = jnp.where(lane == device, piece, 0.0)
        psnr = psnr - piece
    out[vec_at + 16 : vec_at + 27, :rest] = vec[:, LANE:]


def whole(shape):
    return pl.BlockSpec(shape, lambda *_: (0,) * len(shape))


def acc_shapes(ch, hid):
    return [
        (CPAD, 9 * CPAD),
        (3, CPAD, CPAD),
        (CPAD, ch),
        (hid, CPAD),
        (hid, ch),
        (5, ch, LANE),
        (3 * TOK, LANE),
    ]


def scratches(ch, hid, px, vec_rows):
    v = pltpu.VMEM
    prep = [
        v((ch, vec_rows), f32),
        v((3 * CPAD, ch), bf16), v((ch, CPAD), bf16), v((hid, ch), bf16), v((ch, hid), bf16),
        v((ch, CPAD), bf16), v((ch, CPAD), bf16), v((ch, CPAD), bf16), v((CPAD, ch), bf16),
        v((ch, hid), bf16), v((hid, ch), bf16),
        v((ch, 9 * CPAD), bf16),
        v((TOK, LANE), f32),
        v((TOK, LANE), f32),
        v((hid, LANE), f32),
        v((10, ch, LANE), f32),
        v((2, CPAD, LANE), f32),
    ]
    wins = px // TOK
    tmp = [
        v((px, 9 * CPAD), bf16),
        v((CPAD, px), bf16), v((CPAD, px), bf16), v((CPAD, px), bf16), v((hid, px), bf16), v((CPAD, px), bf16),
        v((wins, CPAD, LANE), bf16),
        v((wins, 3 * TOK, LANE), f32),
        v((wins, 3 * TOK, LANE), bf16),
        v((2, px, CPAD), bf16),
        v((ch, px), f32),
        v((CPAD, px), bf16),
        v((CPAD, px), bf16),
        v((2, px, CPAD), bf16),
        v((ch, px), f32),
        v((ch, px), f32),
        v((hid, px), f32),
        v((CPAD, px), bf16),
        v((CPAD, px), bf16),
        v((CPAD, px), bf16),
        v((8, px), f32),
        v((ch, px), bf16),
        v((hid, px), bf16),
    ]
    return prep + tmp


def halo_kernel(halo_ref, ig_ref, ig_out, ig_s):
    _, ch, rows, image_side = ig_ref.shape
    ig_s[:, :image_side] = ig_ref[0].reshape(ch * rows, image_side)
    for r in range(SHIFT):
        row = halo_ref[0, :, r * image_side : (r + 1) * image_side]
        ig_s[pl.ds(r, ch, stride=rows), :image_side] = row.astype(f32)
    ig_out[0] = ig_s[:, :image_side].reshape(ch, rows, image_side)


def bits_of(size):
    return list(range(size.bit_length() - 1))


def exchange_plan(sizes):
    (dp_axis, dp_size), (head_axis, head_size) = sizes
    first = (dp_axis, 0)
    rest = [(dp_axis, b) for b in bits_of(dp_size)[1:]]
    last = [(head_axis, b) for b in bits_of(head_size)]
    half = len(rest) // 2
    return first, [rest + last, rest[half:] + rest[:half] + last]


def exchange_kernel(
    first, orders, head_size,
    g_in, c1_in, c2_in, x_in, conv_in, vec_ref,
    sum_ref, out_ref,
    g, work, given, low, short, given_short, c1, c2, c_halo, x, conv, wc, cs, rows_s, out_s,
    send_sem, recv_sem, local_sem,
):
    count, ch, own_rows, image_side = x.shape
    rows = g.shape[0]
    mesh_id = pl.DeviceIdType.MESH
    here = lax.axis_index("head")
    upper = {"head": (here + 1) % head_size}
    lower = {"head": (here + head_size - 1) % head_size}

    def load(k, src, dst):
        copy = pltpu.make_async_copy(src, dst, local_sem.at[k])
        copy.start()
        return copy

    loads = [
        load(0, g_in, g),
        load(1, conv_in, conv),
        load(2, c1_in, c1),
        load(3, c2_in, c2),
        load(4, x_in, x),
    ]

    def meet(stage):
        axis, b = stage
        me = lax.axis_index(axis)
        step = 2**b
        bit = (me // step) % 2
        return {axis: me + (1 - 2 * bit) * step}, bit

    barrier = pltpu.get_barrier_semaphore()
    friends = [meet(stage)[0] for stage in [first] + orders[0]] + [upper, lower]
    for other in friends:
        pl.semaphore_signal(barrier, inc=1, device_id=other, device_id_type=mesh_id)
    pl.semaphore_wait(barrier, len(friends))

    used = [0]

    def send(src, dst, other):
        k = used[0]
        used[0] += 1
        copy = pltpu.make_async_remote_copy(
            src_ref=src,
            dst_ref=dst,
            send_sem=send_sem.at[k],
            recv_sem=recv_sem.at[k],
            device_id=other,
            device_id_type=mesh_id,
        )
        copy.start()
        return copy

    def span(start, size):
        return pl.ds(pl.multiple_of(start, 16), size)

    col = lax.broadcasted_iota(jnp.int32, (1, image_side, ch), 1)
    top = jnp.where(here == 0, 0.0, 1.0).astype(f32)
    bottom = jnp.where(here == head_size - 1, 0.0, 1.0).astype(f32)

    def prepare():
        loads[1].wait()
        wc[...] = jnp.zeros_like(wc)
        cs[...] = jnp.zeros_like(cs)
        for tap in range(9):
            wc[tap * TAP : tap * TAP + ch, :] = conv[tap // 3, tap % 3].astype(bf16)

    def conv_rows(image, block):
        for k in range(WIN + 2):
            r = block * WIN + k - 1 - SHIFT
            if r < 0:
                row = c_halo[image, r + SHIFT + 1 : r + SHIFT + 2]
            elif r < c1.shape[1]:
                row = c1[image, r : r + 1]
            else:
                row = c2[image, r - c1.shape[1] : r - c1.shape[1] + 1]
            row = row.astype(f32)
            if block == 0 and k == 0:
                row = row * top
            if block == own_rows // WIN - 1 and k == WIN + 1:
                row = row * bottom
            left = jnp.where(col == 0, 0.0, roll_cols(row, -1))
            right = jnp.where(col == image_side - 1, 0.0, roll_cols(row, 1))
            at = slice(k * image_side, (k + 1) * image_side)
            cs[at, 0:ch] = left[0].astype(bf16)
            cs[at, TAP : TAP + ch] = row[0].astype(bf16)
            cs[at, 2 * TAP : 2 * TAP + ch] = right[0].astype(bf16)
        total = vec_ref[10:11, :]
        for i in range(3):
            at = slice(i * image_side, (i + WIN) * image_side)
            total = total + nn(cs[at, :], wc[i * 3 * TAP : (i + 1) * 3 * TAP, :])
        for k in range(WIN):
            rows_s[image, block * WIN + k] = jnp.transpose(total[k * image_side : (k + 1) * image_side])

    stores = []

    def finish(image):
        out_s[image] = (jnp.swapaxes(rows_s[image], 0, 1) + x[image].astype(f32)).astype(bf16)
        stores.append(load(5 + image, out_s.at[image], out_ref.at[image]))

    blocks = own_rows // WIN
    inner = [(n, b) for n in range(count) for b in range(1, blocks)]
    outer = [(n, 0) for n in range(count)]
    stage_count = 2 * (1 + len(orders[0]))
    jobs = [[] for _ in range(stage_count)]
    for k, job in enumerate(inner + outer):
        jobs[min(1 + k * (stage_count - 2) // len(inner + outer), stage_count - 2)].append(job)

    halos = []

    def work_on(stage):
        if stage == 0:
            prepare()
        if stage == 1:
            for k in (2, 3, 4):
                loads[k].wait()
        for image, block in jobs[stage]:
            if block == 0 and image == 0:
                halos[0].wait()
            conv_rows(image, block)
            if block == 0:
                finish(image)

    loads[0].wait()
    other, bit = meet(first)
    half = rows // 2
    copy = send(g.at[span((1 - bit) * half, half)], given.at[pl.ds(0, half)], other)
    halos.append(send(c2_in.at[:, WIN - SHIFT - 1 :], c_halo, upper))
    work_on(0)
    copy.wait()
    keep = bit * half
    work[span(keep, half), :] = g[span(keep, half), :] + given[:half, :]
    unit = 16 * 2 ** len(orders[0])
    parts = half // unit
    cut = (parts + 1) // 2 * unit
    begin = [keep, keep + cut]
    size = [cut, half - cut]
    taken = half
    link_stages = len([stage for stage in orders[0] if stage[0] == first[0]])
    trail = [[], []]
    for s in range(len(orders[0])):
        flying = []
        for p in range(2):
            if size[p] == 0:
                continue
            other, bit = meet(orders[p][s])
            size[p] //= 2
            trail[p].append(begin[p])
            give = begin[p] + (1 - bit) * size[p]
            begin[p] = begin[p] + bit * size[p]
            if s < link_stages:
                short[span(give, size[p]), :] = work[span(give, size[p]), :].astype(bf16)
                copy = send(short.at[span(give, size[p])], given_short.at[pl.ds(taken - half, size[p])], other)
            else:
                copy = send(work.at[span(give, size[p])], given.at[pl.ds(taken, size[p])], other)
            flying.append((p, taken, copy))
            taken += size[p]
        work_on(1 + s)
        for p, at, copy in flying:
            copy.wait()
            if s < link_stages:
                there = given_short[at - half : at - half + size[p], :].astype(f32)
            else:
                there = given[at : at + size[p], :]
            total = work[span(begin[p], size[p]), :] + there
            if s < len(orders[0]) - 1:
                work[span(begin[p], size[p]), :] = total
            else:
                low[span(begin[p], size[p]), :] = total.astype(bf16)

    for s in reversed(range(len(orders[0]))):
        flying = []
        for p in range(2):
            if size[p] == 0:
                continue
            other, _ = meet(orders[p][s])
            here_now = low.at[span(begin[p], size[p])]
            flying.append(send(here_now, here_now, other))
            begin[p] = trail[p][s]
            size[p] *= 2
        work_on(2 * len(orders[0]) - s)
        for copy in flying:
            copy.wait()
    other, _ = meet(first)
    here_now = low.at[span(keep, half)]
    copy = send(here_now, here_now, other)
    work_on(stage_count - 1)
    copy.wait()
    sum_ref[...] = low[...]
    for copy in stores:
        copy.wait()


def exchange(packed, c1, c2, images, conv_weight, vectors, sizes):
    first, orders = exchange_plan(sizes)
    rows = packed.shape[0]
    count, ch, own_rows, image_side = images.shape
    vmem = pl.BlockSpec(memory_space=pltpu.VMEM)
    hbm = pl.BlockSpec(memory_space=pl.ANY)
    v = pltpu.VMEM
    sends = 1 + 2 + 4 * len(orders[0])
    return pl.pallas_call(
        functools.partial(exchange_kernel, first, orders, sizes[1][1]),
        in_specs=[hbm] * 5 + [vmem],
        out_specs=[vmem, hbm],
        out_shape=[
            jax.ShapeDtypeStruct(packed.shape, bf16),
            jax.ShapeDtypeStruct(images.shape, bf16),
        ],
        scratch_shapes=[
            v(packed.shape, f32),
            v(packed.shape, f32),
            v(packed.shape, f32),
            v(packed.shape, bf16),
            v(packed.shape, bf16),
            v((rows // 2, LANE), bf16),
            v(c1.shape, bf16),
            v(c2.shape, bf16),
            v((count, SHIFT + 1, image_side, ch), bf16),
            v(images.shape, bf16),
            v(conv_weight.shape, f32),
            v((9 * TAP, ch), bf16),
            v(((WIN + 2) * image_side, 3 * TAP), bf16),
            v((count, own_rows, ch, image_side), f32),
            v(images.shape, bf16),
            pltpu.SemaphoreType.DMA((sends,)),
            pltpu.SemaphoreType.DMA((sends,)),
            pltpu.SemaphoreType.DMA((5 + count,)),
        ],
        compiler_params=pltpu.CompilerParams(
            collective_id=0, has_side_effects=True, vmem_limit_bytes=60 * 1024 * 1024
        ),
        name="sum_gradients",
    )(packed, c1, c2, images, conv_weight, vectors)


def adam_kernel(scal, g_ref, *refs):
    given, refs = refs[:21], refs[21:]
    norm_ref, psnr_ref, results, refs = refs[0], refs[1], refs[2:23], refs[23:]
    held, made, in_sem, out_sem = refs[:21], refs[21:42], refs[42], refs[43]
    order = [6, 1, 4, 5, 2, 0, 3]
    loads = {}
    for k in order:
        for part in range(3):
            n = 3 * k + part
            loads[n] = pltpu.make_async_copy(given[n], held[n], in_sem.at[n])
            loads[n].start()
    stores = []

    def arrived(k):
        for part in range(3):
            loads[3 * k + part].wait()
        return [held[3 * k + part] for part in range(3)]

    def leave(k):
        for part in range(3):
            n = 3 * k + part
            stores.append(pltpu.make_async_copy(made[n], results[n], out_sem.at[n]))
            stores[-1].start()

    weights = held[0::3]
    ch = weights[2].shape[0]
    up, count, vec_at, rel_at, used = pack_rows(ch)
    rest = ch - LANE

    def block(k):
        left = g_ref[k * up : (k + 1) * up, :].astype(f32)
        at = (count + k // 2) * up
        right = g_ref[at : at + up, :].astype(f32)
        if k % 2:
            right = pltpu.roll(right, TOK, 1)
        return jnp.concatenate([left, right[:, :rest]], axis=1)[:ch]

    vec_rows = g_ref[vec_at : vec_at + 32, :].astype(f32)
    vec = jnp.concatenate([vec_rows[:11], vec_rows[16:27, :rest]], axis=1)
    psnr = vec_rows[11:12] + vec_rows[12:13] + vec_rows[13:14]
    psnr_ref[...] = jnp.sum(psnr, axis=1, keepdims=True)

    span = 2 * WIN
    wide = span * span
    at = lax.broadcasted_iota(jnp.int32, (TOK, wide), 0)
    to = lax.broadcasted_iota(jnp.int32, (TOK, wide), 1)
    place = ((at >> 3) + (WIN - 1)) * span + (at & 7) + (WIN - 1)
    expand = (to == place).astype(f32).astype(bf16)
    pairs = g_ref[rel_at:used, :]
    rel_rows = []
    for p in range(3):
        for parity in range(2):
            part = pairs[p * TOK : (p + 1) * TOK, :].astype(f32)
            if parity:
                part = pltpu.roll(part, TOK, 1)
            spread = nn(part[:, :TOK].astype(bf16), expand)
            total = jnp.zeros((WIN, wide), f32)
            for row in range(WIN):
                piece = spread[row * WIN : (row + 1) * WIN]
                piece = pltpu.roll(piece, (wide - span * row) % wide, 1)
                total = total + piece
            line = total[0:1]
            for c in range(1, WIN):
                line = line + pltpu.roll(total, wide - c, 1)[c : c + 1]
            rel_rows.append(line)
    rel = jnp.concatenate(rel_rows, axis=0)
    rel = jnp.concatenate(
        [rel[:, k * span : k * span + span - 1] for k in range(span - 1)], axis=1
    )
    qkv = jnp.concatenate([block(9), block(10), block(11)], axis=1)
    fc1 = jnp.concatenate([block(13), block(14)], axis=1)
    fc2 = jnp.concatenate([block(15), block(16)], axis=1)
    small = [vec, qkv, block(12), rel, fc1, fc2]
    taps = [block(t) for t in range(9)]
    total = jnp.zeros((1, 1), f32)
    for g in small + taps:
        total = total + jnp.sum(jnp.sum(g * g, axis=0, keepdims=True), axis=1, keepdims=True)
    norm = jnp.sqrt(total)
    norm_ref[...] = norm
    clip = jnp.minimum(1.0, max_norm / (norm + 1e-06))
    fix_one, fix_two = scal[0], scal[1]

    def update(w, m1, m2, g, rate):
        g = g * clip
        m1 = beta_one * m1 + (1.0 - beta_one) * g
        m2 = beta_two * m2 + (1.0 - beta_two) * g * g
        step = (m1 / fix_one) / (jnp.sqrt(m2 / fix_two) + adam_eps)
        return w - rate * (step + decay_rate * w), m1, m2

    for k in order:
        w, m1, m2 = arrived(k)
        if k == 6:
            for t, g in enumerate(taps):
                at = (t // 3, t % 3)
                for ref, value in zip(made[18:21], update(w[at], m1[at], m2[at], g, learn_rate)):
                    ref[at] = value
        else:
            new = update(w[...], m1[...], m2[...], small[k], vector_rate if k == 0 else learn_rate)
            for ref, value in zip(made[3 * k : 3 * k + 3], new):
                ref[...] = value
        leave(k)
    for copy in stores:
        copy.wait()


def relative_onehot_keys_first():
    position = np.arange(TOK)
    pos_row, pos_col = position // WIN, position % WIN
    span = 2 * WIN - 1
    index = (pos_row[None, :] - pos_row[:, None] + WIN - 1) * span + (
        pos_col[None, :] - pos_col[:, None] + WIN - 1
    )
    return index.reshape(-1), span * span


def on_device(
    images, cotangent, valid_size,
    vectors, vectors_first, vectors_second,
    qkv_weight, qkv_first, qkv_second,
    proj_weight, proj_first, proj_second,
    rel_table, rel_first, rel_second,
    fc1_weight, fc1_first, fc1_second,
    fc2_weight, fc2_first, fc2_second,
    conv_weight, conv_first, conv_second,
    step, sr_crops, hr_crops, psnr_running,
):
    count, own_rows, image_side, ch = images.shape
    out_shape = (count, ch, own_rows, image_side)
    hid = fc1_weight.shape[1]
    px = image_side * WIN
    blocks = own_rows // WIN
    heads = lax.axis_size("head")
    place = lax.axis_index("head")
    to_lower = [((i + 1) % heads, i) for i in range(heads)]
    info = jnp.concatenate(
        [
            jnp.stack([place, (place == heads - 1).astype(jnp.int32)]).astype(jnp.int32),
            valid_size.astype(jnp.int32),
            ((lax.axis_index("dp") * heads + place) % LANE)[None].astype(jnp.int32),
        ]
    )
    images = images.transpose(0, 3, 1, 2)
    cotangent = cotangent.transpose(0, 3, 1, 2)
    halo = lax.ppermute(
        jnp.concatenate([images[:, :, :SHIFT], cotangent[:, :, : SHIFT + 1]], axis=2), "head", to_lower
    )

    index, span = relative_onehot_keys_first()
    onehot = (jnp.asarray(index)[:, None] == jnp.arange(span)[None, :]).astype(f32)
    bias = jnp.dot(onehot, rel_table, precision=highest)
    bias = bias.reshape(TOK, TOK, 3, 2).transpose(2, 0, 3, 1).reshape(3, TOK, LANE)

    wts = (vectors, qkv_weight, proj_weight, fc1_weight, fc2_weight.T, conv_weight, bias)
    wts_specs = [whole(w.shape) for w in wts]
    acc_dims = acc_shapes(ch, hid)
    acc_types = [jax.ShapeDtypeStruct(s, f32) for s in acc_dims]
    smem = pl.BlockSpec(memory_space=pltpu.SMEM)
    params = pltpu.CompilerParams(
        dimension_semantics=("arbitrary", "arbitrary"), vmem_limit_bytes=60 * 1024 * 1024
    )
    view = lambda rows, at, dims: pl.BlockSpec((1, ch, rows, image_side), lambda n, *_: (n, 0, at, 0))
    c_block = lambda size: pl.BlockSpec((1, size, image_side, ch), lambda n, *_: (n, 0, 0, 0))
    row_view = pltpu.VMEM((ch * own_rows, LANE), f32)
    c1, ig, *acc = pl.pallas_call(
        functools.partial(inner_kernel, image_side, own_rows),
        grid=(count, blocks - 1),
        in_specs=[smem, view(own_rows, 0, 2), view(own_rows, 0, 2), *wts_specs],
        out_specs=[
            pl.BlockSpec((1, WIN, image_side, ch), lambda n, r: (n, r, 0, 0)),
            view(own_rows, 0, 2),
            *[whole(s) for s in acc_dims],
        ],
        out_shape=[
            jax.ShapeDtypeStruct((count, own_rows - WIN, image_side, ch), bf16),
            jax.ShapeDtypeStruct(out_shape, f32),
            *acc_types,
        ],
        scratch_shapes=[row_view] * 3 + scratches(ch, hid, px, vectors.shape[0]),
        compiler_params=params,
        name="inner_windows",
    )(info, images, cotangent, *wts)
    device_count = lax.axis_size("dp") * heads
    unit = 16 * device_count
    rows = -(-pack_rows(ch)[-1] // unit) * unit
    c2, ig, ig_halo, packed = pl.pallas_call(
        functools.partial(last_kernel, image_side, own_rows),
        grid=(count,),
        in_specs=[
            smem,
            view(WIN, blocks - 1, 1),
            view(WIN, blocks - 1, 1),
            view(2 * SHIFT + 1, 0, 1),
            view(WIN, blocks - 1, 1),
            *wts_specs,
            *[whole(s) for s in acc_dims],
            whole(sr_crops.shape),
            whole(hr_crops.shape),
        ],
        out_specs=[
            c_block(WIN),
            view(WIN, blocks - 1, 1),
            pl.BlockSpec((1, ch, SHIFT * image_side), lambda n: (n, 0, 0)),
            whole((rows, LANE)),
        ],
        out_shape=[
            jax.ShapeDtypeStruct((count, WIN, image_side, ch), bf16),
            jax.ShapeDtypeStruct(out_shape, f32),
            jax.ShapeDtypeStruct((count, ch, SHIFT * image_side), bf16),
            jax.ShapeDtypeStruct((rows, LANE), f32),
        ],
        input_output_aliases={4: 1},
        scratch_shapes=[pltpu.VMEM(s, f32) for s in acc_dims]
        + [pltpu.VMEM((ch * k, LANE), f32) for k in (WIN, WIN, 2 * WIN, WIN)]
        + scratches(ch, hid, px, vectors.shape[0]),
        compiler_params=pltpu.CompilerParams(
            dimension_semantics=("arbitrary",), vmem_limit_bytes=60 * 1024 * 1024
        ),
        name="last_windows",
    )(info, images, cotangent, halo, ig, *wts, *acc, sr_crops, hr_crops)

    summed, output = exchange(
        packed, c1, c2, images, conv_weight, vectors, (("dp", lax.axis_size("dp")), ("head", heads))
    )
    summed, ig_halo = lax.optimization_barrier((summed, ig_halo))
    ig_halo = lax.ppermute(ig_halo, "head", [(i, (i + 1) % heads) for i in range(heads)])
    image_grad = pl.pallas_call(
        halo_kernel,
        grid=(count,),
        in_specs=[pl.BlockSpec((1, ch, SHIFT * image_side), lambda n: (n, 0, 0)), view(WIN, 0, 1)],
        out_specs=view(WIN, 0, 1),
        scratch_shapes=[pltpu.VMEM((ch * WIN, LANE), f32)],
        out_shape=jax.ShapeDtypeStruct(out_shape, f32),
        input_output_aliases={1: 0},
        name="halo_rows",
    )(ig_halo, ig)
    output, image_grad = output.transpose(0, 2, 3, 1), image_grad.transpose(0, 2, 3, 1)

    step_count = step[0].astype(f32)
    scal = jnp.stack([1.0 - beta_one**step_count, 1.0 - beta_two**step_count])
    weights = (vectors, qkv_weight, proj_weight, rel_table.T, fc1_weight, fc2_weight.T, conv_weight)
    firsts = (vectors_first, qkv_first, proj_first, rel_first.T, fc1_first, fc2_first.T, conv_first)
    seconds = (vectors_second, qkv_second, proj_second, rel_second.T, fc1_second, fc2_second.T, conv_second)
    vmem = pl.BlockSpec(memory_space=pltpu.VMEM)
    hbm = pl.BlockSpec(memory_space=pl.ANY)
    state = [array for group in zip(weights, firsts, seconds) for array in group]
    grad_norm, psnr, *updated = pl.pallas_call(
        adam_kernel,
        in_specs=[smem, vmem] + [hbm] * 21,
        out_specs=[vmem] * 2 + [hbm] * 21,
        out_shape=[jax.ShapeDtypeStruct((1, 1), f32)] * 2
        + [jax.ShapeDtypeStruct(array.shape, f32) for array in state],
        scratch_shapes=[pltpu.VMEM(array.shape, f32) for array in state * 2]
        + [pltpu.SemaphoreType.DMA((21,)), pltpu.SemaphoreType.DMA((21,))],
        compiler_params=pltpu.CompilerParams(vmem_limit_bytes=60 * 1024 * 1024),
        name="adam",
    )(scal, summed, *state)
    for k in (9, 10, 11, 15, 16, 17):
        updated[k] = updated[k].T
    psnr_total = psnr_running + psnr.reshape(1)
    return (output, image_grad, grad_norm.reshape(1), psnr_total, *updated)


def solution(mesh):
    pixels = P("dp", "head", None, None)
    crops = P(("dp", "head"), None, None, None)
    placed = (pixels, pixels, P("dp")) + (P(),) * 22 + (crops, crops, P())
    return jax.shard_map(
        on_device,
        mesh=mesh,
        in_specs=placed,
        out_specs=(pixels, pixels) + (P(),) * 23,
        check_vma=False,
    )
```

```python
import functools

import jax
import jax.numpy as jnp
import numpy as np
from jax import lax
from jax.experimental import pallas as pl
from jax.experimental.pallas import tpu as pltpu
from jax.sharding import PartitionSpec as P

WIN = 8
TOK = WIN * WIN
SHIFT = WIN // 2
LANE = 128
TAP = 256
HPAD = 32
HEADS = 6
CPAD = HEADS * HPAD

eps_norm = 1e-05
neg_mask = -100.0
max_norm = 1.0
learn_rate = 0.03
vector_rate = 0.2
beta_one = 0.9
beta_two = 0.999
adam_eps = 1e-08
decay_rate = 0.01
highest = lax.Precision.HIGHEST
f32 = jnp.float32
bf16 = jnp.bfloat16


def nn(a, b):
    return lax.dot_general(a, b, (((1,), (0,)), ((), ())), preferred_element_type=f32)


def nt(a, b):
    return lax.dot_general(a, b, (((1,), (1,)), ((), ())), preferred_element_type=f32)


def pad_heads(rows, heads):
    dim = rows.shape[0] // heads
    gap = jnp.zeros((HPAD - dim, rows.shape[1]), rows.dtype)
    parts = []
    for h in range(heads):
        parts += [rows[h * dim : (h + 1) * dim], gap]
    return jnp.concatenate(parts, axis=0)


def drop_rows(rows, heads, dim):
    return jnp.concatenate([rows[h * HPAD : h * HPAD + dim] for h in range(heads)], axis=0)


def drop_lanes(rows, heads, dim):
    return jnp.concatenate([rows[:, h * HPAD : h * HPAD + dim] for h in range(heads)], axis=1)


def to_tokens(rows):
    side = rows.shape[1]
    return jnp.concatenate(
        [rows[:, w * WIN : (w + 1) * WIN, :].reshape(TOK, rows.shape[2]) for w in range(side // WIN)],
        axis=0,
    )


def from_tokens(tokens):
    count = tokens.shape[0] // TOK
    return jnp.concatenate(
        [tokens[w * TOK : (w + 1) * TOK].reshape(WIN, WIN, tokens.shape[1]) for w in range(count)],
        axis=1,
    )


def roll_cols(rows, by):
    side = rows.shape[1]
    by = by % side
    return jnp.concatenate([rows[:, by:, :], rows[:, :by, :]], axis=1)


def block_step(x_rows, gy_rows, first_step, edge, base_row, valid, image_side, wts, prep, acc, tmp, c_out):
    (vec_ref, qkv_ref, proj_ref, fc1_ref, fc2_ref, conv_ref, bias_ref) = wts
    (vecT, wqkvT, wpT, w1T, w2T, wq, wk, wv, wp, w1, w2, wc, colmask, rowmask, b1T, wide_vec, head_vec) = prep
    (acc_conv, acc_qkv, acc_proj, acc_fc1, acc_fc2, acc_ln, acc_rel) = acc
    (g9, a_aug, o_aug, m_aug, g_aug, c_aug, qeo_s, p_s, pb_s, kv_s, first_s, do_s, dq_s, dkv_s, u2_s, xT_s, slope_s, vt_s, qt_s, kt_s, inv_s, db_s, dh_s) = tmp
    ch = x_rows.shape[2]
    dim = ch // HEADS
    hid = fc1_ref.shape[1]
    px = x_rows.shape[1] * WIN
    pairs = px // LANE
    ones_row = dim

    @pl.when(first_step)
    def _():
        vecT[...] = jnp.transpose(vec_ref[...])
        for k in range(10):
            wide_vec[k] = jnp.broadcast_to(vecT[:, k : k + 1], (ch, LANE))
        for k in range(2):
            head_vec[k] = pad_heads(wide_vec[2 + k], HEADS)
        b1T[:ch, :] = wide_vec[7]
        b1T[ch:, :] = wide_vec[8]
        for k, dst in enumerate((wq, wk, wv)):
            part = pad_heads(jnp.transpose(qkv_ref[:, k * ch : (k + 1) * ch]), HEADS)
            wqkvT[k * CPAD : (k + 1) * CPAD, :] = part.astype(bf16)
            dst[...] = jnp.transpose(part).astype(bf16)
        padded = pad_heads(proj_ref[...], HEADS)
        wp[...] = padded.astype(bf16)
        wpT[...] = jnp.transpose(padded).astype(bf16)
        w1[...] = fc1_ref[...].astype(bf16)
        w1T[...] = jnp.transpose(fc1_ref[...]).astype(bf16)
        w2T[...] = fc2_ref[...].astype(bf16)
        w2[...] = jnp.transpose(fc2_ref[...]).astype(bf16)
        wc[...] = jnp.zeros_like(wc)
        g9[...] = jnp.zeros_like(g9)
        for tap in range(9):
            wc[:, tap * CPAD : tap * CPAD + ch] = conv_ref[tap // 3, tap % 3].astype(bf16)
        key = lax.broadcasted_iota(jnp.int32, (TOK, LANE), 0)
        query = lax.broadcasted_iota(jnp.int32, (TOK, LANE), 1) & (TOK - 1)
        one = lambda m: m.astype(f32)
        colmask[...] = one(((key & 7) < SHIFT) != ((query & 7) < SHIFT))
        rowmask[...] = one(((key >> 3) < SHIFT) != ((query >> 3) < SHIFT))
        for ref in (a_aug, m_aug, c_aug):
            pad = ref.shape[0] - ch
            ref[ch:, :] = (lax.broadcasted_iota(jnp.int32, (pad, px), 0) == 0).astype(f32).astype(bf16)

    def column(k):
        return wide_vec[k]

    def stats(v):
        mean = jnp.sum(v, axis=0, keepdims=True) * (1.0 / ch)
        cen = v - mean
        var = jnp.sum(cen * cen, axis=0, keepdims=True) * (1.0 / ch)
        inv = lax.rsqrt(var + eps_norm)
        return cen * inv, inv

    def ln_back(grad, u, inv, gain):
        t = grad * gain
        mean_t = jnp.sum(t, axis=0, keepdims=True) * (1.0 / ch)
        mean_tu = jnp.sum(t * u, axis=0, keepdims=True) * (1.0 / ch)
        return inv * (t - mean_t - u * mean_tu)

    chunks = [slice(k * LANE, (k + 1) * LANE) for k in range(px // LANE)]
    third = hid // 3
    bands = [slice(k * third, (k + 1) * third) for k in range(3)]

    keep = jnp.where(edge, 0.0, 1.0).astype(f32)
    col = lax.broadcasted_iota(jnp.int32, (1, image_side, ch), 1)
    moved = {}

    def build_tap(tap):
        i, j = tap % 3, tap // 3
        if i == 0:
            shifted = roll_cols(gy_rows, SHIFT + 1 - j)
            if j == 0:
                shifted = jnp.where(col == image_side - SHIFT - 1, 0.0, shifted)
            if j == 2:
                shifted = jnp.where(col == image_side - SHIFT, 0.0, shifted)
            moved[j] = shifted
        rows = [moved[j][r + 2 - i : r + 3 - i] for r in range(WIN)]
        if i == 0:
            rows[SHIFT - 1] = rows[SHIFT - 1] * keep
        if i == 2:
            rows[SHIFT] = rows[SHIFT] * keep
        at = (3 * i + j) * CPAD
        g9[:, at : at + ch] = to_tokens(jnp.concatenate(rows, axis=0)).astype(bf16)

    x_tok = to_tokens(roll_cols(x_rows, SHIFT))
    for at in chunks:
        xT = jnp.transpose(x_tok[at])
        xT_s[:, at] = xT
        u1, _ = stats(xT)
        a_aug[:ch, at] = (u1 * column(0) + column(1)).astype(bf16)
    scale = dim ** (-0.5)
    qkv_all = nn(wqkvT[...], a_aug[:ch, :])
    for at in chunks:
        qt_s[:, at] = ((qkv_all[:CPAD, at] + head_vec[0]) * scale).astype(bf16)
        kT = qkv_all[CPAD : 2 * CPAD, at].astype(bf16)
        vT = (qkv_all[2 * CPAD :, at] + head_vec[1]).astype(bf16)
        kt_s[:, at] = kT
        vt_s[:, at] = vT
        kv_s[0, at, :] = jnp.transpose(kT.astype(f32)).astype(bf16)
        kv_s[1, at, :] = jnp.transpose(vT.astype(f32)).astype(bf16)

    def low_lanes(rows):
        return lax.broadcasted_iota(jnp.int32, (rows, LANE), 1) < TOK

    def swap(slab):
        return pltpu.roll(slab, TOK, 1)

    def only_low(v):
        return jnp.where(low_lanes(v.shape[0]), v, jnp.zeros_like(v))

    def only_high(v):
        return jnp.where(low_lanes(v.shape[0]), jnp.zeros_like(v), v)

    def head_rows(v, h):
        return v[h * HPAD : (h + 1) * HPAD]

    def dup(slab):
        slab = slab.astype(f32)
        other = swap(slab)
        out = []
        for low, high in ((slab, other), (other, slab)):
            rows = [
                only_high(head_rows(high, h)) if h % 2 else only_low(head_rows(low, h)) for h in range(HEADS)
            ]
            out.append(jnp.concatenate(rows, axis=0).astype(bf16))
        return out

    def spread(slab):
        slab = slab.astype(f32)
        other = swap(slab)
        two = 2 * HPAD
        gap = jnp.zeros((two, TOK), f32)
        wide = jnp.zeros((two, LANE), f32)
        out = []
        for low, high in ((slab, other), (other, slab)):
            rows = [
                jnp.concatenate([only_low(low[:two]), gap], axis=1),
                jnp.concatenate([only_high(high[two : 2 * two]), gap], axis=1),
                jnp.concatenate([wide, low[2 * two :, :TOK]], axis=1),
            ]
            out.append(jnp.concatenate(rows, axis=0).astype(bf16))
        return out

    def merge(one, two):
        rows = []
        for h in range(HEADS):
            first, second = head_rows(one, h), head_rows(two, h)
            if h % 2:
                rows.append(jnp.where(low_lanes(HPAD), swap(first), second))
            else:
                rows.append(jnp.where(low_lanes(HPAD), first, swap(second)))
        return jnp.concatenate(rows, axis=0)

    def by_pair(rows):
        front, back = rows[:, :LANE], rows[:, LANE:]
        zero_back = jnp.zeros_like(back)
        return jnp.concatenate(
            [
                jnp.concatenate([only_low(front), zero_back], axis=1),
                jnp.concatenate([only_high(front), zero_back], axis=1),
                jnp.concatenate([jnp.zeros_like(front), back], axis=1),
            ],
            axis=0,
        )

    def pick_pair(stacked):
        front = jnp.where(low_lanes(TOK), stacked[:TOK, :LANE], stacked[TOK : 2 * TOK, :LANE])
        return jnp.concatenate([front, stacked[2 * TOK :, LANE:]], axis=1)

    key = lax.broadcasted_iota(jnp.int32, (TOK, LANE), 0)
    key_row = base_row + (key >> 3)
    key_row = jnp.where(key_row >= image_side, key_row - image_side, key_row)
    out_row = key_row >= valid
    edge_f = jnp.where(edge, neg_mask, 0.0).astype(f32)

    def scores_of(pp):
        q_pair = dup(qt_s[:, chunks[pp]])
        raw = []
        for half in range(2):
            w = 2 * pp + half
            qeo_s[w] = q_pair[half]
            raw.append(nn(by_pair(kv_s[0, w * TOK : (w + 1) * TOK, :]), q_pair[half]))
        return raw

    def soften(pp, raw):
        for half in range(2):
            w = 2 * pp + half
            key_col = (key & 7) + (w * WIN + SHIFT)
            apart = rowmask[...] * edge_f
            if w == 2 * pairs - 1:
                key_col = jnp.where(key_col >= image_side, key_col - image_side, key_col)
                apart = jnp.where(colmask[...] > 0.5, neg_mask, apart)
            extra = apart + jnp.where(out_row | (key_col >= valid), neg_mask, 0.0)
            s = raw[half].reshape(3, TOK, LANE) + bias_ref[...] + extra[None]
            top = jnp.max(s, axis=1, keepdims=True)
            e = jnp.exp(s - top)
            p = e / jnp.sum(e, axis=1, keepdims=True)
            p = p.reshape(3 * TOK, LANE)
            p_s[w] = p
            pb_s[w] = p.astype(bf16)

    def mix(pp):
        v_pair = spread(vt_s[:, chunks[pp]])
        return [nn(v_pair[half], pb_s[2 * pp + half]) for half in range(2)]

    def place(pp, mixed):
        o_aug[:, chunks[pp]] = merge(*mixed).astype(bf16)

    raws, mixes = {}, {}
    for t in range(pairs + 3):
        if 0 <= t - 2 < pairs:
            mixes[t - 2] = mix(t - 2)
        if t < pairs:
            raws[t] = scores_of(t)
        if 0 <= t - 1 < pairs:
            soften(t - 1, raws.pop(t - 1))
        if 0 <= t - 3 < pairs:
            place(t - 3, mixes.pop(t - 3))
        if t < 9:
            build_tap(t)
    o_aug[ones_row : ones_row + 1, :] = jnp.ones((1, px), bf16)

    attn = nn(wpT[...], o_aug[...])
    part = px // 3
    conv_back = [nt(wc[...], g9[:part, :])]
    for at in chunks:
        first = xT_s[:, at] + (attn[:, at] + column(4))
        first_s[:, at] = first
        u2, inv2 = stats(first)
        u2_s[:, at] = u2
        inv_s[0:1, at] = inv2
        m_aug[:ch, at] = (u2 * column(5) + column(6)).astype(bf16)
    hidden_all = nn(w1T[...], m_aug[:ch, :])
    conv_back.append(nt(wc[...], g9[part : 2 * part, :]))
    for at in chunks:
        for band in bands:
            hidden = hidden_all[band, at] + b1T[band, :]
            cdf = 0.5 * (1.0 + lax.erf(hidden * 0.7071067811865476))
            g_aug[band, at] = (hidden * cdf).astype(bf16)
            slope_s[band, at] = cdf + hidden * jnp.exp(-0.5 * hidden * hidden) * 0.3989422804014327
    branch = nn(w2T[...], g_aug[...])
    conv_back.append(nt(wc[...], g9[2 * part :, :]))
    c_rows = []
    for at in chunks:
        cT = (first_s[:, at] + (branch[:, at] + column(9))).astype(bf16)
        c_aug[:ch, at] = cT
        c_rows.append(jnp.transpose(cT.astype(f32)))
    c_out[0] = roll_cols(from_tokens(jnp.concatenate(c_rows, axis=0)), -SHIFT).astype(bf16)

    def conv_grad(k):
        at = slice(k * TAP, min((k + 1) * TAP, 9 * CPAD))
        if at.start < at.stop:
            acc_conv[:, at] += nn(c_aug[...], g9[:, at])

    dsecond = jnp.concatenate(conv_back, axis=1)
    for at in chunks:
        dbT = dsecond[:, at].astype(bf16)
        db_s[:, at] = dbT
        acc_ln[4] += dbT.astype(f32)
    dg = nn(w2[...], db_s[...])
    acc_fc2[...] += nt(g_aug[...], db_s[...])
    for at in chunks:
        for band in bands:
            dh_s[band, at] = (dg[band, at] * slope_s[band, at]).astype(bf16)
    dm_all = nn(w1[...], dh_s[...])
    for at in chunks:
        u2 = u2_s[:, at]
        dm = dm_all[:, at]
        acc_ln[2] += dm * u2
        acc_ln[3] += dm
        dfirst = dsecond[:, at] + ln_back(dm, u2, inv_s[0:1, at], column(5))
        first_s[:, at] = dfirst
        db_s[:, at] = dfirst.astype(bf16)
    do_all = nn(wp[...], db_s[...])
    for at in chunks:
        do_s[:, at] = do_all[:, at].astype(bf16)

    rel_sum = jnp.zeros((3 * TOK, LANE), f32)

    def probs_grad(pp):
        do_pair = dup(do_s[:, chunks[pp]])
        dps, dvs = [], []
        for half in range(2):
            w = 2 * pp + half
            dps.append(nn(by_pair(kv_s[1, w * TOK : (w + 1) * TOK, :]), do_pair[half]))
            dvs.append(nt(pb_s[w], do_pair[half]))
        return dps, dvs

    def scores_grad(pp, dps, dvs, rel_sum):
        out = []
        for half in range(2):
            w = 2 * pp + half
            p = p_s[w].reshape(3, TOK, LANE)
            dp = dps[half].reshape(3, TOK, LANE)
            ds = p * (dp - jnp.sum(p * dp, axis=1, keepdims=True))
            ds = ds.reshape(3 * TOK, LANE).astype(bf16)
            rel_sum = rel_sum + ds.astype(f32)
            out.append(ds)
            dkv_s[1, w * TOK : (w + 1) * TOK, :] = pick_pair(dvs[half]).astype(bf16)
        return out, rel_sum

    def inner_grads(pp, ds):
        k_pair = spread(kt_s[:, chunks[pp]])
        dks = [nt(ds[half], qeo_s[2 * pp + half]) for half in range(2)]
        dqs = [nn(k_pair[half], ds[half]) for half in range(2)]
        return dks, dqs

    def place_grads(pp, dks, dqs):
        for half in range(2):
            w = 2 * pp + half
            dkv_s[0, w * TOK : (w + 1) * TOK, :] = pick_pair(dks[half]).astype(bf16)
        dq_s[:, chunks[pp]] = merge(*dqs).astype(bf16)

    first_part, second_part, third_part = {}, {}, {}
    for t in range(pairs + 3):
        if 0 <= t - 2 < pairs:
            third_part[t - 2] = inner_grads(t - 2, second_part.pop(t - 2))
        if t < pairs:
            first_part[t] = probs_grad(t)
        if 0 <= t - 1 < pairs:
            second_part[t - 1], rel_sum = scores_grad(t - 1, *first_part.pop(t - 1), rel_sum)
        if 0 <= t - 3 < pairs:
            place_grads(t - 3, *third_part.pop(t - 3))
        conv_grad(t)
    acc_rel[...] += rel_sum

    dqT = dq_s[...]
    da_q = nn(wq[...], dqT)
    da_kv = nt(wk[...], dkv_s[0]) + nt(wv[...], dkv_s[1])
    acc_qkv[0] += nt(a_aug[...], dqT) * scale
    acc_qkv[1] += nn(a_aug[...], dkv_s[0])
    acc_qkv[2] += nn(a_aug[...], dkv_s[1])
    acc_fc1[...] += nt(dh_s[...], m_aug[...])
    acc_proj[...] += nt(o_aug[...], db_s[...])
    ig_rows = []
    for at in chunks:
        da = da_q[:, at] * scale + da_kv[:, at]
        u1, inv1 = stats(xT_s[:, at])
        acc_ln[0] += da * u1
        acc_ln[1] += da
        ig_rows.append(jnp.transpose(first_s[:, at] + ln_back(da, u1, inv1, column(0))))
    return roll_cols(from_tokens(jnp.concatenate(ig_rows, axis=0)), -SHIFT) + gy_rows[1 : 1 + WIN]


N_ACC = 7
N_PREP = 17
N_WTS = 7


def natural_rows(ref, side, every, start, count):
    ch = ref.shape[0] // every
    rows = [ref[pl.ds(start + r, ch, stride=every), :] for r in range(count)]
    return jnp.stack([jnp.transpose(row)[:side] for row in rows])


def edge_kernel(x_ref, gy_ref, out_ref, x_s, gy_s):
    _, ch, rows, side = x_ref.shape
    x_s[:, :side] = x_ref[0].astype(f32).reshape(ch * rows, side)
    gy_s[:, :side] = gy_ref[0].astype(f32).reshape(ch * rows, side)
    parts = [x_s[pl.ds(r, ch, stride=rows), :][:, :side] for r in range(SHIFT)]
    parts += [gy_s[pl.ds(r, ch, stride=rows), :][:, :side] for r in range(SHIFT + 1)]
    out_ref[0] = jnp.concatenate(parts, axis=1).astype(bf16)


def inner_kernel(image_side, own_rows, info, x_ref, gy_ref, *refs):
    wts, refs = refs[:N_WTS], refs[N_WTS:]
    c_out, ig_out, refs = refs[0], refs[1], refs[2:]
    acc, refs = refs[:N_ACC], refs[N_ACC:]
    x_s, gy_s, ig_s, refs = *refs[:3], refs[3:]
    prep, tmp = refs[:N_PREP], refs[N_PREP:]
    image, row_block = pl.program_id(0), pl.program_id(1)
    first_step = (image == 0) & (row_block == 0)

    @pl.when(first_step)
    def _():
        for ref in acc:
            ref[...] = jnp.zeros_like(ref)
        ig_s[...] = jnp.zeros_like(ig_s)

    @pl.when(row_block == 0)
    def _():
        ch = x_ref.shape[1]
        x_s[:, :image_side] = x_ref[0].astype(f32).reshape(ch * own_rows, image_side)
        gy_s[:, :image_side] = gy_ref[0].astype(f32).reshape(ch * own_rows, image_side)

    start = row_block * WIN + SHIFT
    x_rows = natural_rows(x_s, image_side, own_rows, start, WIN)
    gy_rows = natural_rows(gy_s, image_side, own_rows, start - 1, WIN + 2)
    base_row = info[0] * own_rows + start
    ig = block_step(
        x_rows, gy_rows, first_step, False, base_row, info[2 + image], image_side, wts, prep, acc, tmp, c_out
    )
    for r in range(WIN):
        ig_s[pl.ds(start + r, ig_out.shape[1], stride=own_rows), :image_side] = jnp.transpose(ig[r])

    @pl.when(row_block == pl.num_programs(1) - 1)
    def _():
        ig_out[0] = ig_s[:, :image_side].reshape(ig_out.shape[1:])


def last_kernel(image_side, own_rows, info, x_ref, gy_ref, halo_ref, ig_ref, *refs):
    wts, refs = refs[:N_WTS], refs[N_WTS:]
    acc_in, refs = refs[:N_ACC], refs[N_ACC:]
    sr_ref, hr_ref, c_out, ig_out, ig_halo, pack_out, refs = *refs[:6], refs[6:]
    acc, refs = refs[:N_ACC], refs[N_ACC:]
    x_s, gy_s, ig_s, refs = *refs[:3], refs[3:]
    prep, tmp = refs[:N_PREP], refs[N_PREP:]
    image = pl.program_id(0)
    first_step = image == 0

    @pl.when(first_step)
    def _():
        for ref, given in zip(acc, acc_in):
            ref[...] = given[...]

    ch = x_ref.shape[1]
    x_s[:, :image_side] = x_ref[0].astype(f32).reshape(ch * WIN, image_side)
    gy_s[:, :image_side] = gy_ref[0].astype(f32).reshape(ch * WIN, image_side)

    def halo_rows(start, size):
        rows = [halo_ref[0, :, r * image_side : (r + 1) * image_side] for r in range(start, start + size)]
        return jnp.stack([jnp.transpose(row.astype(f32)) for row in rows])

    x_rows = jnp.concatenate(
        [natural_rows(x_s, image_side, WIN, SHIFT, SHIFT), halo_rows(0, SHIFT)], axis=0
    )
    gy_rows = jnp.concatenate(
        [natural_rows(gy_s, image_side, WIN, SHIFT - 1, SHIFT + 1), halo_rows(SHIFT, SHIFT + 1)], axis=0
    )
    base_row = info[0] * own_rows + own_rows - SHIFT
    ig = block_step(
        x_rows, gy_rows, first_step, info[1] == 1, base_row, info[2 + image], image_side, wts, prep, acc, tmp, c_out
    )
    ig_s[:, :image_side] = ig_ref[0].reshape(ch * WIN, image_side)
    for r in range(SHIFT):
        ig_s[pl.ds(SHIFT + r, ch, stride=WIN), :image_side] = jnp.transpose(ig[r])
    ig_out[0] = ig_s[:, :image_side].reshape(ch, WIN, image_side)
    ig_halo[0] = jnp.concatenate([jnp.transpose(ig[SHIFT + r]) for r in range(SHIFT)], axis=1).astype(bf16)

    @pl.when(image == pl.num_programs(0) - 1)
    def _():
        pack_gradients(info[2 + pl.num_programs(0)], acc, sr_ref, hr_ref, pack_out)


def pack_rows(ch):
    up = -(-ch // 8) * 8
    blocks = 17
    vec_at = (blocks + (blocks + 1) // 2) * up
    return up, blocks, vec_at, vec_at + 32, vec_at + 32 + 3 * TOK


def pack_gradients(device, acc, sr_ref, hr_ref, out):
    (acc_conv, acc_qkv, acc_proj, acc_fc1, acc_fc2, acc_ln, acc_rel) = acc
    ch = acc_fc2.shape[1]
    dim = ch // HEADS
    up, count, vec_at, rel_at, used = pack_rows(ch)
    rest = ch - LANE
    out[used:, :] = jnp.zeros((out.shape[0] - used, LANE), f32)
    out[rel_at:used, :] = acc_rel[...]
    blocks = [acc_conv[:ch, t * CPAD : t * CPAD + ch] for t in range(9)]
    qkv = [drop_lanes(acc_qkv[k], HEADS, dim) for k in range(3)]
    blocks += [qkv[k][:ch] for k in range(3)]
    blocks += [drop_rows(acc_proj[...], HEADS, dim)]
    fc1 = jnp.transpose(acc_fc1[...])
    fc2 = jnp.transpose(acc_fc2[...])
    blocks += [fc1[:ch, :ch], fc1[:ch, ch:]]
    blocks += [fc2[:, :ch], fc2[:, ch:]]
    out[:vec_at, :] = jnp.zeros((vec_at, LANE), f32)
    for k, block in enumerate(blocks):
        out[k * up : k * up + ch, :] = block[:, :LANE]
        at = (count + k // 2) * up
        half = (k % 2) * TOK
        out[at : at + ch, half : half + rest] = block[:, LANE:]
    ln = [jnp.sum(jnp.transpose(acc_ln[k]), axis=0, keepdims=True) for k in range(5)]
    vec = [
        ln[0],
        ln[1],
        qkv[0][ch : ch + 1, :],
        qkv[2][ch : ch + 1, :],
        acc_proj[dim : dim + 1, :],
        ln[2],
        ln[3],
        fc1[ch : ch + 1, :ch],
        fc1[ch : ch + 1, ch:],
        ln[4],
        acc_conv[ch : ch + 1, 4 * CPAD : 4 * CPAD + ch],
    ]
    vec = jnp.concatenate(vec, axis=0)
    diff = sr_ref[...] - hr_ref[...]
    luma = (65.481 * diff[:, 0] + 128.553 * diff[:, 1] + 24.966 * diff[:, 2]) / 255.0
    square = jnp.sum(luma * luma, axis=1, keepdims=True)
    mse = jnp.sum(square, axis=2, keepdims=True) * (1.0 / (luma.shape[1] * luma.shape[2]))
    psnr = jnp.sum(jnp.log(mse + 1e-06) * (-10.0 / 2.302585092994046), axis=0)
    out[vec_at : vec_at + 32, :] = jnp.zeros((32, LANE), f32)
    out[vec_at : vec_at + 11, :] = vec[:, :LANE]
    lane = lax.broadcasted_iota(jnp.int32, (1, LANE), 1)
    for k in range(3):
        piece = psnr.astype(bf16).astype(f32)
        out[vec_at + 11 + k : vec_at + 12 + k, :] = jnp.where(lane == device, piece, 0.0)
        psnr = psnr - piece
    out[vec_at + 16 : vec_at + 27, :rest] = vec[:, LANE:]


def whole(shape):
    return pl.BlockSpec(shape, lambda *_: (0,) * len(shape))


def acc_shapes(ch, hid):
    return [
        (CPAD, 9 * CPAD),
        (3, CPAD, CPAD),
        (CPAD, ch),
        (hid, CPAD),
        (hid, ch),
        (5, ch, LANE),
        (3 * TOK, LANE),
    ]


def scratches(ch, hid, px, vec_rows):
    v = pltpu.VMEM
    prep = [
        v((ch, vec_rows), f32),
        v((3 * CPAD, ch), bf16), v((ch, CPAD), bf16), v((hid, ch), bf16), v((ch, hid), bf16),
        v((ch, CPAD), bf16), v((ch, CPAD), bf16), v((ch, CPAD), bf16), v((CPAD, ch), bf16),
        v((ch, hid), bf16), v((hid, ch), bf16),
        v((ch, 9 * CPAD), bf16),
        v((TOK, LANE), f32),
        v((TOK, LANE), f32),
        v((hid, LANE), f32),
        v((10, ch, LANE), f32),
        v((2, CPAD, LANE), f32),
    ]
    wins = px // TOK
    tmp = [
        v((px, 9 * CPAD), bf16),
        v((CPAD, px), bf16), v((CPAD, px), bf16), v((CPAD, px), bf16), v((hid, px), bf16), v((CPAD, px), bf16),
        v((wins, CPAD, LANE), bf16),
        v((wins, 3 * TOK, LANE), f32),
        v((wins, 3 * TOK, LANE), bf16),
        v((2, px, CPAD), bf16),
        v((ch, px), f32),
        v((CPAD, px), bf16),
        v((CPAD, px), bf16),
        v((2, px, CPAD), bf16),
        v((ch, px), f32),
        v((ch, px), f32),
        v((hid, px), f32),
        v((CPAD, px), bf16),
        v((CPAD, px), bf16),
        v((CPAD, px), bf16),
        v((8, px), f32),
        v((ch, px), bf16),
        v((hid, px), bf16),
    ]
    return prep + tmp


def halo_kernel(halo_ref, ig_ref, ig_out, ig_s):
    _, ch, rows, image_side = ig_ref.shape
    ig_s[:, :image_side] = ig_ref[0].reshape(ch * rows, image_side)
    for r in range(SHIFT):
        row = halo_ref[0, :, r * image_side : (r + 1) * image_side]
        ig_s[pl.ds(r, ch, stride=rows), :image_side] = row.astype(f32)
    ig_out[0] = ig_s[:, :image_side].reshape(ch, rows, image_side)


def bits_of(size):
    return list(range(size.bit_length() - 1))


def exchange_plan(sizes):
    (dp_axis, dp_size), (head_axis, head_size) = sizes
    first = (dp_axis, 0)
    rest = [(dp_axis, b) for b in bits_of(dp_size)[1:]]
    last = [(head_axis, b) for b in bits_of(head_size)]
    half = len(rest) // 2
    return first, [rest + last, rest[half:] + rest[:half] + last]


def exchange_kernel(
    first, orders, head_size,
    g_in, c1_in, c2_in, x_in, ig_in, conv_in, vec_ref,
    sum_ref, out_ref, ig_out,
    g, work, given, low, short, given_short, c1, c2, c_halo, ig_mine, ig_given, x, conv, wc, cs, rows_s, out_s,
    send_sem, recv_sem, local_sem,
):
    count, ch, own_rows, image_side = x.shape
    rows = g.shape[0]
    mesh_id = pl.DeviceIdType.MESH
    here = lax.axis_index("head")
    upper = {"head": (here + 1) % head_size}
    lower = {"head": (here + head_size - 1) % head_size}

    def load(k, src, dst):
        copy = pltpu.make_async_copy(src, dst, local_sem.at[k])
        copy.start()
        return copy

    loads = [
        load(0, g_in, g),
        load(1, conv_in, conv),
        load(2, c1_in, c1),
        load(3, c2_in, c2),
        load(4, x_in, x),
        load(5, ig_in, ig_mine),
    ]

    def meet(stage):
        axis, b = stage
        me = lax.axis_index(axis)
        step = 2**b
        bit = (me // step) % 2
        return {axis: me + (1 - 2 * bit) * step}, bit

    barrier = pltpu.get_barrier_semaphore()
    friends = [meet(stage)[0] for stage in [first] + orders[0]] + [upper, lower]
    for other in friends:
        pl.semaphore_signal(barrier, inc=1, device_id=other, device_id_type=mesh_id)
    pl.semaphore_wait(barrier, len(friends))

    used = [0]

    def send(src, dst, other):
        k = used[0]
        used[0] += 1
        copy = pltpu.make_async_remote_copy(
            src_ref=src,
            dst_ref=dst,
            send_sem=send_sem.at[k],
            recv_sem=recv_sem.at[k],
            device_id=other,
            device_id_type=mesh_id,
        )
        copy.start()
        return copy

    def span(start, size):
        return pl.ds(pl.multiple_of(start, 16), size)

    col = lax.broadcasted_iota(jnp.int32, (1, image_side, ch), 1)
    top = jnp.where(here == 0, 0.0, 1.0).astype(f32)
    bottom = jnp.where(here == head_size - 1, 0.0, 1.0).astype(f32)

    def prepare():
        loads[1].wait()
        wc[...] = jnp.zeros_like(wc)
        cs[...] = jnp.zeros_like(cs)
        for tap in range(9):
            wc[tap * TAP : tap * TAP + ch, :] = conv[tap // 3, tap % 3].astype(bf16)

    def conv_rows(image, block):
        for k in range(WIN + 2):
            r = block * WIN + k - 1 - SHIFT
            if r < 0:
                row = c_halo[image, r + SHIFT + 1 : r + SHIFT + 2]
            elif r < c1.shape[1]:
                row = c1[image, r : r + 1]
            else:
                row = c2[image, r - c1.shape[1] : r - c1.shape[1] + 1]
            row = row.astype(f32)
            if block == 0 and k == 0:
                row = row * top
            if block == own_rows // WIN - 1 and k == WIN + 1:
                row = row * bottom
            left = jnp.where(col == 0, 0.0, roll_cols(row, -1))
            right = jnp.where(col == image_side - 1, 0.0, roll_cols(row, 1))
            at = slice(k * image_side, (k + 1) * image_side)
            cs[at, 0:ch] = left[0].astype(bf16)
            cs[at, TAP : TAP + ch] = row[0].astype(bf16)
            cs[at, 2 * TAP : 2 * TAP + ch] = right[0].astype(bf16)
        total = vec_ref[10:11, :]
        for i in range(3):
            at = slice(i * image_side, (i + WIN) * image_side)
            total = total + nn(cs[at, :], wc[i * 3 * TAP : (i + 1) * 3 * TAP, :])
        for k in range(WIN):
            rows_s[image, block * WIN + k] = jnp.transpose(total[k * image_side : (k + 1) * image_side])

    stores = []

    def finish(image):
        out_s[image] = (jnp.swapaxes(rows_s[image], 0, 1) + x[image].astype(f32)).astype(bf16)
        stores.append(load(6 + image, out_s.at[image], out_ref.at[image]))

    blocks = own_rows // WIN
    inner = [(n, b) for n in range(count) for b in range(1, blocks)]
    outer = [(n, 0) for n in range(count)]
    stage_count = 2 * (1 + len(orders[0]))
    jobs = [[] for _ in range(stage_count)]
    for k, job in enumerate(inner + outer):
        jobs[min(1 + k * (stage_count - 2) // len(inner + outer), stage_count - 2)].append(job)

    halos = []

    def work_on(stage):
        if stage == 0:
            prepare()
        if stage == 1:
            for k in (2, 4, 5):
                loads[k].wait()
        for image, block in jobs[stage]:
            if block == 0 and image == 0:
                halos[0].wait()
            conv_rows(image, block)
            if block == 0:
                finish(image)

    loads[0].wait()
    other, bit = meet(first)
    half = rows // 2
    copy = send(g.at[span((1 - bit) * half, half)], given.at[pl.ds(0, half)], other)
    loads[3].wait()
    halos.append(send(c2.at[:, WIN - SHIFT - 1 :], c_halo, upper))
    work_on(0)
    copy.wait()
    keep = bit * half
    work[span(keep, half), :] = g[span(keep, half), :] + given[:half, :]
    unit = 16 * 2 ** len(orders[0])
    parts = half // unit
    cut = (parts + 1) // 2 * unit
    begin = [keep, keep + cut]
    size = [cut, half - cut]
    taken = half
    link_stages = len([stage for stage in orders[0] if stage[0] == first[0]])
    trail = [[], []]
    for s in range(len(orders[0])):
        flying = []
        for p in range(2):
            if size[p] == 0:
                continue
            other, bit = meet(orders[p][s])
            size[p] //= 2
            trail[p].append(begin[p])
            give = begin[p] + (1 - bit) * size[p]
            begin[p] = begin[p] + bit * size[p]
            if s < link_stages:
                short[span(give, size[p]), :] = work[span(give, size[p]), :].astype(bf16)
                copy = send(short.at[span(give, size[p])], given_short.at[pl.ds(taken - half, size[p])], other)
            else:
                copy = send(work.at[span(give, size[p])], given.at[pl.ds(taken, size[p])], other)
            flying.append((p, taken, copy))
            taken += size[p]
        work_on(1 + s)
        for p, at, copy in flying:
            copy.wait()
            if s < link_stages:
                there = given_short[at - half : at - half + size[p], :].astype(f32)
            else:
                there = given[at : at + size[p], :]
            total = work[span(begin[p], size[p]), :] + there
            if s < len(orders[0]) - 1:
                work[span(begin[p], size[p]), :] = total
            else:
                low[span(begin[p], size[p]), :] = total.astype(bf16)

    for s in reversed(range(len(orders[0]))):
        flying = []
        for p in range(2):
            if size[p] == 0:
                continue
            if s == link_stages - 1 and p == 0:
                halos.append(send(ig_mine, ig_given, upper))
            other, _ = meet(orders[p][s])
            here_now = low.at[span(begin[p], size[p])]
            flying.append(send(here_now, here_now, other))
            begin[p] = trail[p][s]
            size[p] *= 2
        work_on(2 * len(orders[0]) - s)
        for copy in flying:
            copy.wait()
    other, _ = meet(first)
    here_now = low.at[span(keep, half)]
    copy = send(here_now, here_now, other)
    work_on(stage_count - 1)
    copy.wait()
    sum_ref[...] = low[...]
    halos[1].wait()
    stores.append(load(6 + count, ig_given, ig_out))
    for copy in stores:
        copy.wait()


def exchange(packed, c1, c2, images, ig_halo, conv_weight, vectors, sizes):
    first, orders = exchange_plan(sizes)
    rows = packed.shape[0]
    count, ch, own_rows, image_side = images.shape
    vmem = pl.BlockSpec(memory_space=pltpu.VMEM)
    hbm = pl.BlockSpec(memory_space=pl.ANY)
    v = pltpu.VMEM
    sends = 2 + 2 + 4 * len(orders[0])
    return pl.pallas_call(
        functools.partial(exchange_kernel, first, orders, sizes[1][1]),
        in_specs=[hbm] * 6 + [vmem],
        out_specs=[vmem, hbm, hbm],
        out_shape=[
            jax.ShapeDtypeStruct(packed.shape, bf16),
            jax.ShapeDtypeStruct(images.shape, bf16),
            jax.ShapeDtypeStruct(ig_halo.shape, bf16),
        ],
        scratch_shapes=[
            v(packed.shape, f32),
            v(packed.shape, f32),
            v(packed.shape, f32),
            v(packed.shape, bf16),
            v(packed.shape, bf16),
            v((rows // 2, LANE), bf16),
            v(c1.shape, bf16),
            v(c2.shape, bf16),
            v((count, SHIFT + 1, image_side, ch), bf16),
            v(ig_halo.shape, bf16),
            v(ig_halo.shape, bf16),
            v(images.shape, bf16),
            v(conv_weight.shape, f32),
            v((9 * TAP, ch), bf16),
            v(((WIN + 2) * image_side, 3 * TAP), bf16),
            v((count, own_rows, ch, image_side), f32),
            v(images.shape, bf16),
            pltpu.SemaphoreType.DMA((sends,)),
            pltpu.SemaphoreType.DMA((sends,)),
            pltpu.SemaphoreType.DMA((7 + count,)),
        ],
        compiler_params=pltpu.CompilerParams(
            collective_id=0, has_side_effects=True, vmem_limit_bytes=40 * 1024 * 1024
        ),
        name="sum_gradients",
    )(packed, c1, c2, images, ig_halo, conv_weight, vectors)


def adam_kernel(scal, g_ref, *refs):
    given, refs = refs[:21], refs[21:]
    norm_ref, psnr_ref, results, refs = refs[0], refs[1], refs[2:23], refs[23:]
    held, made, in_sem, out_sem = refs[:21], refs[21:42], refs[42], refs[43]
    order = [6, 1, 4, 5, 2, 0, 3]
    loads = {}
    for k in order:
        for part in range(3):
            n = 3 * k + part
            loads[n] = pltpu.make_async_copy(given[n], held[n], in_sem.at[n])
            loads[n].start()
    stores = []

    def arrived(k):
        for part in range(3):
            loads[3 * k + part].wait()
        return [held[3 * k + part] for part in range(3)]

    def leave(k):
        for part in range(3):
            n = 3 * k + part
            stores.append(pltpu.make_async_copy(made[n], results[n], out_sem.at[n]))
            stores[-1].start()

    weights = held[0::3]
    ch = weights[2].shape[0]
    up, count, vec_at, rel_at, used = pack_rows(ch)
    rest = ch - LANE

    def block(k):
        left = g_ref[k * up : (k + 1) * up, :].astype(f32)
        at = (count + k // 2) * up
        right = g_ref[at : at + up, :].astype(f32)
        if k % 2:
            right = pltpu.roll(right, TOK, 1)
        return jnp.concatenate([left, right[:, :rest]], axis=1)[:ch]

    vec_rows = g_ref[vec_at : vec_at + 32, :].astype(f32)
    vec = jnp.concatenate([vec_rows[:11], vec_rows[16:27, :rest]], axis=1)
    psnr = vec_rows[11:12] + vec_rows[12:13] + vec_rows[13:14]
    psnr_ref[...] = jnp.sum(psnr, axis=1, keepdims=True)

    span = 2 * WIN
    wide = span * span
    at = lax.broadcasted_iota(jnp.int32, (TOK, wide), 0)
    to = lax.broadcasted_iota(jnp.int32, (TOK, wide), 1)
    place = ((at >> 3) + (WIN - 1)) * span + (at & 7) + (WIN - 1)
    expand = (to == place).astype(f32).astype(bf16)
    pairs = g_ref[rel_at:used, :]
    rel_rows = []
    for p in range(3):
        for parity in range(2):
            part = pairs[p * TOK : (p + 1) * TOK, :].astype(f32)
            if parity:
                part = pltpu.roll(part, TOK, 1)
            spread = nn(part[:, :TOK].astype(bf16), expand)
            total = jnp.zeros((WIN, wide), f32)
            for row in range(WIN):
                piece = spread[row * WIN : (row + 1) * WIN]
                piece = pltpu.roll(piece, (wide - span * row) % wide, 1)
                total = total + piece
            line = total[0:1]
            for c in range(1, WIN):
                line = line + pltpu.roll(total, wide - c, 1)[c : c + 1]
            rel_rows.append(line)
    rel = jnp.concatenate(rel_rows, axis=0)
    rel = jnp.concatenate(
        [rel[:, k * span : k * span + span - 1] for k in range(span - 1)], axis=1
    )
    qkv = jnp.concatenate([block(9), block(10), block(11)], axis=1)
    fc1 = jnp.concatenate([block(13), block(14)], axis=1)
    fc2 = jnp.concatenate([block(15), block(16)], axis=1)
    small = [vec, qkv, block(12), rel, fc1, fc2]
    taps = [block(t) for t in range(9)]
    total = jnp.zeros((1, 1), f32)
    for g in small + taps:
        total = total + jnp.sum(jnp.sum(g * g, axis=0, keepdims=True), axis=1, keepdims=True)
    norm = jnp.sqrt(total)
    norm_ref[...] = norm
    clip = jnp.minimum(1.0, max_norm / (norm + 1e-06))
    fix_one, fix_two = scal[0], scal[1]

    def update(w, m1, m2, g, rate):
        g = g * clip
        m1 = beta_one * m1 + (1.0 - beta_one) * g
        m2 = beta_two * m2 + (1.0 - beta_two) * g * g
        step = (m1 / fix_one) / (jnp.sqrt(m2 / fix_two) + adam_eps)
        return w - rate * (step + decay_rate * w), m1, m2

    for k in order:
        w, m1, m2 = arrived(k)
        if k == 6:
            for t, g in enumerate(taps):
                at = (t // 3, t % 3)
                for ref, value in zip(made[18:21], update(w[at], m1[at], m2[at], g, learn_rate)):
                    ref[at] = value
        else:
            new = update(w[...], m1[...], m2[...], small[k], vector_rate if k == 0 else learn_rate)
            for ref, value in zip(made[3 * k : 3 * k + 3], new):
                ref[...] = value
        leave(k)
    for copy in stores:
        copy.wait()


def relative_onehot_keys_first():
    position = np.arange(TOK)
    pos_row, pos_col = position // WIN, position % WIN
    span = 2 * WIN - 1
    index = (pos_row[None, :] - pos_row[:, None] + WIN - 1) * span + (
        pos_col[None, :] - pos_col[:, None] + WIN - 1
    )
    return index.reshape(-1), span * span


def on_device(
    images, cotangent, valid_size,
    vectors, vectors_first, vectors_second,
    qkv_weight, qkv_first, qkv_second,
    proj_weight, proj_first, proj_second,
    rel_table, rel_first, rel_second,
    fc1_weight, fc1_first, fc1_second,
    fc2_weight, fc2_first, fc2_second,
    conv_weight, conv_first, conv_second,
    step, sr_crops, hr_crops, psnr_running,
):
    count, own_rows, image_side, ch = images.shape
    out_shape = (count, ch, own_rows, image_side)
    hid = fc1_weight.shape[1]
    px = image_side * WIN
    blocks = own_rows // WIN
    heads = lax.axis_size("head")
    place = lax.axis_index("head")
    to_lower = [((i + 1) % heads, i) for i in range(heads)]
    info = jnp.concatenate(
        [
            jnp.stack([place, (place == heads - 1).astype(jnp.int32)]).astype(jnp.int32),
            valid_size.astype(jnp.int32),
            ((lax.axis_index("dp") * heads + place) % LANE)[None].astype(jnp.int32),
        ]
    )
    images = images.transpose(0, 3, 1, 2)
    cotangent = cotangent.transpose(0, 3, 1, 2)
    top_rows = pl.BlockSpec((1, ch, WIN, image_side), lambda n: (n, 0, 0, 0))
    edge = pl.pallas_call(
        edge_kernel,
        grid=(count,),
        in_specs=[top_rows, top_rows],
        out_specs=pl.BlockSpec((1, ch, (2 * SHIFT + 1) * image_side), lambda n: (n, 0, 0)),
        out_shape=jax.ShapeDtypeStruct((count, ch, (2 * SHIFT + 1) * image_side), bf16),
        scratch_shapes=[pltpu.VMEM((ch * WIN, LANE), f32)] * 2,
        name="edge_rows",
    )(images, cotangent)
    halo = lax.ppermute(edge, "head", to_lower)

    index, span = relative_onehot_keys_first()
    onehot = (jnp.asarray(index)[:, None] == jnp.arange(span)[None, :]).astype(f32)
    bias = jnp.dot(onehot, rel_table, precision=highest)
    bias = bias.reshape(TOK, TOK, 3, 2).transpose(2, 0, 3, 1).reshape(3, TOK, LANE)

    wts = (vectors, qkv_weight, proj_weight, fc1_weight, fc2_weight.T, conv_weight, bias)
    wts_specs = [whole(w.shape) for w in wts]
    acc_dims = acc_shapes(ch, hid)
    acc_types = [jax.ShapeDtypeStruct(s, f32) for s in acc_dims]
    smem = pl.BlockSpec(memory_space=pltpu.SMEM)
    params = pltpu.CompilerParams(
        dimension_semantics=("arbitrary", "arbitrary"), vmem_limit_bytes=46 * 1024 * 1024
    )
    view = lambda rows, at, dims: pl.BlockSpec((1, ch, rows, image_side), lambda n, *_: (n, 0, at, 0))
    c_block = lambda size: pl.BlockSpec((1, size, image_side, ch), lambda n, *_: (n, 0, 0, 0))
    row_view = pltpu.VMEM((ch * own_rows, LANE), f32)
    c1, ig, *acc = pl.pallas_call(
        functools.partial(inner_kernel, image_side, own_rows),
        grid=(count, blocks - 1),
        in_specs=[smem, view(own_rows, 0, 2), view(own_rows, 0, 2), *wts_specs],
        out_specs=[
            pl.BlockSpec((1, WIN, image_side, ch), lambda n, r: (n, r, 0, 0)),
            view(own_rows, 0, 2),
            *[whole(s) for s in acc_dims],
        ],
        out_shape=[
            jax.ShapeDtypeStruct((count, own_rows - WIN, image_side, ch), bf16),
            jax.ShapeDtypeStruct(out_shape, f32),
            *acc_types,
        ],
        scratch_shapes=[row_view] * 3 + scratches(ch, hid, px, vectors.shape[0]),
        compiler_params=params,
        name="inner_windows",
    )(info, images, cotangent, *wts)
    device_count = lax.axis_size("dp") * heads
    unit = 16 * device_count
    rows = -(-pack_rows(ch)[-1] // unit) * unit
    c2, ig, ig_halo, packed = pl.pallas_call(
        functools.partial(last_kernel, image_side, own_rows),
        grid=(count,),
        in_specs=[
            smem,
            view(WIN, blocks - 1, 1),
            view(WIN, blocks - 1, 1),
            pl.BlockSpec((1, ch, halo.shape[2]), lambda n: (n, 0, 0)),
            view(WIN, blocks - 1, 1),
            *wts_specs,
            *[whole(s) for s in acc_dims],
            whole(sr_crops.shape),
            whole(hr_crops.shape),
        ],
        out_specs=[
            c_block(WIN),
            view(WIN, blocks - 1, 1),
            pl.BlockSpec((1, ch, SHIFT * image_side), lambda n: (n, 0, 0)),
            whole((rows, LANE)),
        ],
        out_shape=[
            jax.ShapeDtypeStruct((count, WIN, image_side, ch), bf16),
            jax.ShapeDtypeStruct(out_shape, f32),
            jax.ShapeDtypeStruct((count, ch, SHIFT * image_side), bf16),
            jax.ShapeDtypeStruct((rows, LANE), f32),
        ],
        input_output_aliases={4: 1},
        scratch_shapes=[pltpu.VMEM(s, f32) for s in acc_dims]
        + [pltpu.VMEM((ch * k, LANE), f32) for k in (WIN, WIN, WIN)]
        + scratches(ch, hid, px, vectors.shape[0]),
        compiler_params=pltpu.CompilerParams(
            dimension_semantics=("arbitrary",), vmem_limit_bytes=46 * 1024 * 1024
        ),
        name="last_windows",
    )(info, images, cotangent, halo, ig, *wts, *acc, sr_crops, hr_crops)

    summed, output, ig_halo = exchange(
        packed, c1, c2, images, ig_halo, conv_weight, vectors, (("dp", lax.axis_size("dp")), ("head", heads))
    )
    image_grad = pl.pallas_call(
        halo_kernel,
        grid=(count,),
        in_specs=[pl.BlockSpec((1, ch, SHIFT * image_side), lambda n: (n, 0, 0)), view(WIN, 0, 1)],
        out_specs=view(WIN, 0, 1),
        scratch_shapes=[pltpu.VMEM((ch * WIN, LANE), f32)],
        out_shape=jax.ShapeDtypeStruct(out_shape, f32),
        input_output_aliases={1: 0},
        name="halo_rows",
    )(ig_halo, ig)
    output, image_grad = output.transpose(0, 2, 3, 1), image_grad.transpose(0, 2, 3, 1)

    step_count = step[0].astype(f32)
    scal = jnp.stack([1.0 - beta_one**step_count, 1.0 - beta_two**step_count])
    weights = (vectors, qkv_weight, proj_weight, rel_table.T, fc1_weight, fc2_weight.T, conv_weight)
    firsts = (vectors_first, qkv_first, proj_first, rel_first.T, fc1_first, fc2_first.T, conv_first)
    seconds = (vectors_second, qkv_second, proj_second, rel_second.T, fc1_second, fc2_second.T, conv_second)
    vmem = pl.BlockSpec(memory_space=pltpu.VMEM)
    hbm = pl.BlockSpec(memory_space=pl.ANY)
    state = [array for group in zip(weights, firsts, seconds) for array in group]
    grad_norm, psnr, *updated = pl.pallas_call(
        adam_kernel,
        in_specs=[smem, vmem] + [hbm] * 21,
        out_specs=[vmem] * 2 + [hbm] * 21,
        out_shape=[jax.ShapeDtypeStruct((1, 1), f32)] * 2
        + [jax.ShapeDtypeStruct(array.shape, f32) for array in state],
        scratch_shapes=[pltpu.VMEM(array.shape, f32) for array in state * 2]
        + [pltpu.SemaphoreType.DMA((21,)), pltpu.SemaphoreType.DMA((21,))],
        compiler_params=pltpu.CompilerParams(vmem_limit_bytes=60 * 1024 * 1024),
        name="adam",
    )(scal, summed, *state)
    for k in (9, 10, 11, 15, 16, 17):
        updated[k] = updated[k].T
    psnr_total = psnr_running + psnr.reshape(1)
    return (output, image_grad, grad_norm.reshape(1), psnr_total, *updated)


def solution(mesh):
    pixels = P("dp", "head", None, None)
    crops = P(("dp", "head"), None, None, None)
    placed = (pixels, pixels, P("dp")) + (P(),) * 22 + (crops, crops, P())
    return jax.shard_map(
        on_device,
        mesh=mesh,
        in_specs=placed,
        out_specs=(pixels, pixels) + (P(),) * 23,
        check_vma=False,
    )
```

```python
import functools

import jax
import jax.numpy as jnp
import numpy as np
from jax import lax
from jax.experimental import pallas as pl
from jax.experimental.pallas import tpu as pltpu
from jax.sharding import PartitionSpec as P

WIN = 8
TOK = WIN * WIN
SHIFT = WIN // 2
LANE = 128
TAP = 256
HPAD = 32
HEADS = 6
CPAD = HEADS * HPAD

eps_norm = 1e-05
neg_mask = -100.0
max_norm = 1.0
learn_rate = 0.03
vector_rate = 0.2
beta_one = 0.9
beta_two = 0.999
adam_eps = 1e-08
decay_rate = 0.01
highest = lax.Precision.HIGHEST
f32 = jnp.float32
bf16 = jnp.bfloat16


def nn(a, b):
    return lax.dot_general(a, b, (((1,), (0,)), ((), ())), preferred_element_type=f32)


def nt(a, b):
    return lax.dot_general(a, b, (((1,), (1,)), ((), ())), preferred_element_type=f32)


def pad_heads(rows, heads):
    dim = rows.shape[0] // heads
    gap = jnp.zeros((HPAD - dim, rows.shape[1]), rows.dtype)
    parts = []
    for h in range(heads):
        parts += [rows[h * dim : (h + 1) * dim], gap]
    return jnp.concatenate(parts, axis=0)


def drop_rows(rows, heads, dim):
    return jnp.concatenate([rows[h * HPAD : h * HPAD + dim] for h in range(heads)], axis=0)


def drop_lanes(rows, heads, dim):
    return jnp.concatenate([rows[:, h * HPAD : h * HPAD + dim] for h in range(heads)], axis=1)


def to_tokens(rows):
    side = rows.shape[1]
    return jnp.concatenate(
        [rows[:, w * WIN : (w + 1) * WIN, :].reshape(TOK, rows.shape[2]) for w in range(side // WIN)],
        axis=0,
    )


def from_tokens(tokens):
    count = tokens.shape[0] // TOK
    return jnp.concatenate(
        [tokens[w * TOK : (w + 1) * TOK].reshape(WIN, WIN, tokens.shape[1]) for w in range(count)],
        axis=1,
    )


def roll_cols(rows, by):
    side = rows.shape[1]
    by = by % side
    return jnp.concatenate([rows[:, by:, :], rows[:, :by, :]], axis=1)


def block_step(x_rows, gy_rows, first_step, edge, base_row, valid, image_side, wts, prep, acc, tmp, c_out):
    (vec_ref, qkv_ref, proj_ref, fc1_ref, fc2_ref, conv_ref, bias_ref) = wts
    (vecT, wqkvT, wpT, w1T, w2T, wq, wk, wv, wp, w1, w2, wc, colmask, rowmask, b1T, wide_vec, head_vec) = prep
    (acc_conv, acc_qkv, acc_proj, acc_fc1, acc_fc2, acc_ln, acc_rel) = acc
    (g9, a_aug, o_aug, m_aug, g_aug, c_aug, qeo_s, p_s, pb_s, kv_s, first_s, do_s, dq_s, dkv_s, u2_s, xT_s, slope_s, vt_s, qt_s, kt_s, inv_s, db_s, dh_s) = tmp
    ch = x_rows.shape[2]
    dim = ch // HEADS
    hid = fc1_ref.shape[1]
    px = x_rows.shape[1] * WIN
    pairs = px // LANE
    ones_row = dim

    @pl.when(first_step)
    def _():
        vecT[...] = jnp.transpose(vec_ref[...])
        for k in range(10):
            wide_vec[k] = jnp.broadcast_to(vecT[:, k : k + 1], (ch, LANE))
        for k in range(2):
            head_vec[k] = pad_heads(wide_vec[2 + k], HEADS)
        b1T[:ch, :] = wide_vec[7]
        b1T[ch:, :] = wide_vec[8]
        for k, dst in enumerate((wq, wk, wv)):
            part = pad_heads(jnp.transpose(qkv_ref[:, k * ch : (k + 1) * ch]), HEADS)
            wqkvT[k * CPAD : (k + 1) * CPAD, :] = part.astype(bf16)
            dst[...] = jnp.transpose(part).astype(bf16)
        padded = pad_heads(proj_ref[...], HEADS)
        wp[...] = padded.astype(bf16)
        wpT[...] = jnp.transpose(padded).astype(bf16)
        w1[...] = fc1_ref[...].astype(bf16)
        w1T[...] = jnp.transpose(fc1_ref[...]).astype(bf16)
        w2T[...] = fc2_ref[...].astype(bf16)
        w2[...] = jnp.transpose(fc2_ref[...]).astype(bf16)
        wc[...] = jnp.zeros_like(wc)
        g9[...] = jnp.zeros_like(g9)
        for tap in range(9):
            wc[:, tap * CPAD : tap * CPAD + ch] = conv_ref[tap // 3, tap % 3].astype(bf16)
        key = lax.broadcasted_iota(jnp.int32, (TOK, LANE), 0)
        query = lax.broadcasted_iota(jnp.int32, (TOK, LANE), 1) & (TOK - 1)
        one = lambda m: m.astype(f32)
        colmask[...] = one(((key & 7) < SHIFT) != ((query & 7) < SHIFT))
        rowmask[...] = one(((key >> 3) < SHIFT) != ((query >> 3) < SHIFT))
        for ref in (a_aug, m_aug, c_aug):
            pad = ref.shape[0] - ch
            ref[ch:, :] = (lax.broadcasted_iota(jnp.int32, (pad, px), 0) == 0).astype(f32).astype(bf16)

    def column(k):
        return wide_vec[k]

    def stats(v):
        mean = jnp.sum(v, axis=0, keepdims=True) * (1.0 / ch)
        cen = v - mean
        var = jnp.sum(cen * cen, axis=0, keepdims=True) * (1.0 / ch)
        inv = lax.rsqrt(var + eps_norm)
        return cen * inv, inv

    def ln_back(grad, u, inv, gain):
        t = grad * gain
        mean_t = jnp.sum(t, axis=0, keepdims=True) * (1.0 / ch)
        mean_tu = jnp.sum(t * u, axis=0, keepdims=True) * (1.0 / ch)
        return inv * (t - mean_t - u * mean_tu)

    chunks = [slice(k * LANE, (k + 1) * LANE) for k in range(px // LANE)]
    third = hid // 3
    bands = [slice(k * third, (k + 1) * third) for k in range(3)]

    keep = jnp.where(edge, 0.0, 1.0).astype(f32)
    col = lax.broadcasted_iota(jnp.int32, (1, image_side, ch), 1)
    moved = {}

    def build_tap(tap):
        i, j = tap % 3, tap // 3
        if i == 0:
            shifted = roll_cols(gy_rows, SHIFT + 1 - j)
            if j == 0:
                shifted = jnp.where(col == image_side - SHIFT - 1, 0.0, shifted)
            if j == 2:
                shifted = jnp.where(col == image_side - SHIFT, 0.0, shifted)
            moved[j] = shifted
        rows = [moved[j][r + 2 - i : r + 3 - i] for r in range(WIN)]
        if i == 0:
            rows[SHIFT - 1] = rows[SHIFT - 1] * keep
        if i == 2:
            rows[SHIFT] = rows[SHIFT] * keep
        at = (3 * i + j) * CPAD
        g9[:, at : at + ch] = to_tokens(jnp.concatenate(rows, axis=0)).astype(bf16)

    x_tok = to_tokens(roll_cols(x_rows, SHIFT))
    for at in chunks:
        xT = jnp.transpose(x_tok[at])
        xT_s[:, at] = xT
        u1, _ = stats(xT)
        a_aug[:ch, at] = (u1 * column(0) + column(1)).astype(bf16)
    scale = dim ** (-0.5)
    qkv_all = nn(wqkvT[...], a_aug[:ch, :])
    for at in chunks:
        qt_s[:, at] = ((qkv_all[:CPAD, at] + head_vec[0]) * scale).astype(bf16)
        kT = qkv_all[CPAD : 2 * CPAD, at].astype(bf16)
        vT = (qkv_all[2 * CPAD :, at] + head_vec[1]).astype(bf16)
        kt_s[:, at] = kT
        vt_s[:, at] = vT
        kv_s[0, at, :] = jnp.transpose(kT.astype(f32)).astype(bf16)
        kv_s[1, at, :] = jnp.transpose(vT.astype(f32)).astype(bf16)

    def low_lanes(rows):
        return lax.broadcasted_iota(jnp.int32, (rows, LANE), 1) < TOK

    def swap(slab):
        return pltpu.roll(slab, TOK, 1)

    def only_low(v):
        return jnp.where(low_lanes(v.shape[0]), v, jnp.zeros_like(v))

    def only_high(v):
        return jnp.where(low_lanes(v.shape[0]), jnp.zeros_like(v), v)

    def head_rows(v, h):
        return v[h * HPAD : (h + 1) * HPAD]

    def dup(slab):
        slab = slab.astype(f32)
        other = swap(slab)
        out = []
        for low, high in ((slab, other), (other, slab)):
            rows = [
                only_high(head_rows(high, h)) if h % 2 else only_low(head_rows(low, h)) for h in range(HEADS)
            ]
            out.append(jnp.concatenate(rows, axis=0).astype(bf16))
        return out

    def spread(slab):
        slab = slab.astype(f32)
        other = swap(slab)
        two = 2 * HPAD
        gap = jnp.zeros((two, TOK), f32)
        wide = jnp.zeros((two, LANE), f32)
        out = []
        for low, high in ((slab, other), (other, slab)):
            rows = [
                jnp.concatenate([only_low(low[:two]), gap], axis=1),
                jnp.concatenate([only_high(high[two : 2 * two]), gap], axis=1),
                jnp.concatenate([wide, low[2 * two :, :TOK]], axis=1),
            ]
            out.append(jnp.concatenate(rows, axis=0).astype(bf16))
        return out

    def merge(one, two):
        rows = []
        for h in range(HEADS):
            first, second = head_rows(one, h), head_rows(two, h)
            if h % 2:
                rows.append(jnp.where(low_lanes(HPAD), swap(first), second))
            else:
                rows.append(jnp.where(low_lanes(HPAD), first, swap(second)))
        return jnp.concatenate(rows, axis=0)

    def by_pair(rows):
        front, back = rows[:, :LANE], rows[:, LANE:]
        zero_back = jnp.zeros_like(back)
        return jnp.concatenate(
            [
                jnp.concatenate([only_low(front), zero_back], axis=1),
                jnp.concatenate([only_high(front), zero_back], axis=1),
                jnp.concatenate([jnp.zeros_like(front), back], axis=1),
            ],
            axis=0,
        )

    def pick_pair(stacked):
        front = jnp.where(low_lanes(TOK), stacked[:TOK, :LANE], stacked[TOK : 2 * TOK, :LANE])
        return jnp.concatenate([front, stacked[2 * TOK :, LANE:]], axis=1)

    key = lax.broadcasted_iota(jnp.int32, (TOK, LANE), 0)
    key_row = base_row + (key >> 3)
    key_row = jnp.where(key_row >= image_side, key_row - image_side, key_row)
    out_row = key_row >= valid
    edge_f = jnp.where(edge, neg_mask, 0.0).astype(f32)

    def scores_of(pp):
        q_pair = dup(qt_s[:, chunks[pp]])
        raw = []
        for half in range(2):
            w = 2 * pp + half
            qeo_s[w] = q_pair[half]
            raw.append(nn(by_pair(kv_s[0, w * TOK : (w + 1) * TOK, :]), q_pair[half]))
        return raw

    def soften(pp, raw):
        for half in range(2):
            w = 2 * pp + half
            key_col = (key & 7) + (w * WIN + SHIFT)
            apart = rowmask[...] * edge_f
            if w == 2 * pairs - 1:
                key_col = jnp.where(key_col >= image_side, key_col - image_side, key_col)
                apart = jnp.where(colmask[...] > 0.5, neg_mask, apart)
            extra = apart + jnp.where(out_row | (key_col >= valid), neg_mask, 0.0)
            s = raw[half].reshape(3, TOK, LANE) + bias_ref[...] + extra[None]
            top = jnp.max(s, axis=1, keepdims=True)
            e = jnp.exp(s - top)
            p = e / jnp.sum(e, axis=1, keepdims=True)
            p = p.reshape(3 * TOK, LANE)
            p_s[w] = p
            pb_s[w] = p.astype(bf16)

    def mix(pp):
        v_pair = spread(vt_s[:, chunks[pp]])
        return [nn(v_pair[half], pb_s[2 * pp + half]) for half in range(2)]

    def place(pp, mixed):
        o_aug[:, chunks[pp]] = merge(*mixed).astype(bf16)

    raws, mixes = {}, {}
    for t in range(pairs + 3):
        if 0 <= t - 2 < pairs:
            mixes[t - 2] = mix(t - 2)
        if t < pairs:
            raws[t] = scores_of(t)
        if 0 <= t - 1 < pairs:
            soften(t - 1, raws.pop(t - 1))
        if 0 <= t - 3 < pairs:
            place(t - 3, mixes.pop(t - 3))
        if t < 9:
            build_tap(t)
    o_aug[ones_row : ones_row + 1, :] = jnp.ones((1, px), bf16)

    attn = nn(wpT[...], o_aug[...])
    part = px // 3
    conv_back = [nt(wc[...], g9[:part, :])]
    for at in chunks:
        first = xT_s[:, at] + (attn[:, at] + column(4))
        first_s[:, at] = first
        u2, inv2 = stats(first)
        u2_s[:, at] = u2
        inv_s[0:1, at] = inv2
        m_aug[:ch, at] = (u2 * column(5) + column(6)).astype(bf16)
    hidden_all = nn(w1T[...], m_aug[:ch, :])
    conv_back.append(nt(wc[...], g9[part : 2 * part, :]))
    for at in chunks:
        for band in bands:
            hidden = hidden_all[band, at] + b1T[band, :]
            cdf = 0.5 * (1.0 + lax.erf(hidden * 0.7071067811865476))
            g_aug[band, at] = (hidden * cdf).astype(bf16)
            slope_s[band, at] = cdf + hidden * jnp.exp(-0.5 * hidden * hidden) * 0.3989422804014327
    branch = nn(w2T[...], g_aug[...])
    conv_back.append(nt(wc[...], g9[2 * part :, :]))
    c_rows = []
    for at in chunks:
        cT = (first_s[:, at] + (branch[:, at] + column(9))).astype(bf16)
        c_aug[:ch, at] = cT
        c_rows.append(jnp.transpose(cT.astype(f32)))
    c_out[0] = roll_cols(from_tokens(jnp.concatenate(c_rows, axis=0)), -SHIFT).astype(bf16)

    def conv_grad(k):
        at = slice(k * TAP, min((k + 1) * TAP, 9 * CPAD))
        if at.start < at.stop:
            acc_conv[:, at] += nn(c_aug[...], g9[:, at])

    dsecond = jnp.concatenate(conv_back, axis=1)
    for at in chunks:
        dbT = dsecond[:, at].astype(bf16)
        db_s[:, at] = dbT
        acc_ln[4] += dbT.astype(f32)
    dg = nn(w2[...], db_s[...])
    acc_fc2[...] += nt(g_aug[...], db_s[...])
    for at in chunks:
        for band in bands:
            dh_s[band, at] = (dg[band, at] * slope_s[band, at]).astype(bf16)
    dm_all = nn(w1[...], dh_s[...])
    for at in chunks:
        u2 = u2_s[:, at]
        dm = dm_all[:, at]
        acc_ln[2] += dm * u2
        acc_ln[3] += dm
        dfirst = dsecond[:, at] + ln_back(dm, u2, inv_s[0:1, at], column(5))
        first_s[:, at] = dfirst
        db_s[:, at] = dfirst.astype(bf16)
    do_all = nn(wp[...], db_s[...])
    for at in chunks:
        do_s[:, at] = do_all[:, at].astype(bf16)

    rel_sum = jnp.zeros((3 * TOK, LANE), f32)

    def probs_grad(pp):
        do_pair = dup(do_s[:, chunks[pp]])
        dps, dvs = [], []
        for half in range(2):
            w = 2 * pp + half
            dps.append(nn(by_pair(kv_s[1, w * TOK : (w + 1) * TOK, :]), do_pair[half]))
            dvs.append(nt(pb_s[w], do_pair[half]))
        return dps, dvs

    def scores_grad(pp, dps, dvs, rel_sum):
        out = []
        for half in range(2):
            w = 2 * pp + half
            p = p_s[w].reshape(3, TOK, LANE)
            dp = dps[half].reshape(3, TOK, LANE)
            ds = p * (dp - jnp.sum(p * dp, axis=1, keepdims=True))
            ds = ds.reshape(3 * TOK, LANE).astype(bf16)
            rel_sum = rel_sum + ds.astype(f32)
            out.append(ds)
            dkv_s[1, w * TOK : (w + 1) * TOK, :] = pick_pair(dvs[half]).astype(bf16)
        return out, rel_sum

    def inner_grads(pp, ds):
        k_pair = spread(kt_s[:, chunks[pp]])
        dks = [nt(ds[half], qeo_s[2 * pp + half]) for half in range(2)]
        dqs = [nn(k_pair[half], ds[half]) for half in range(2)]
        return dks, dqs

    def place_grads(pp, dks, dqs):
        for half in range(2):
            w = 2 * pp + half
            dkv_s[0, w * TOK : (w + 1) * TOK, :] = pick_pair(dks[half]).astype(bf16)
        dq_s[:, chunks[pp]] = merge(*dqs).astype(bf16)

    first_part, second_part, third_part = {}, {}, {}
    for t in range(pairs + 3):
        if 0 <= t - 2 < pairs:
            third_part[t - 2] = inner_grads(t - 2, second_part.pop(t - 2))
        if t < pairs:
            first_part[t] = probs_grad(t)
        if 0 <= t - 1 < pairs:
            second_part[t - 1], rel_sum = scores_grad(t - 1, *first_part.pop(t - 1), rel_sum)
        if 0 <= t - 3 < pairs:
            place_grads(t - 3, *third_part.pop(t - 3))
        conv_grad(t)
    acc_rel[...] += rel_sum

    dqT = dq_s[...]
    da_q = nn(wq[...], dqT)
    da_kv = nt(wk[...], dkv_s[0]) + nt(wv[...], dkv_s[1])
    acc_qkv[0] += nt(a_aug[...], dqT) * scale
    acc_qkv[1] += nn(a_aug[...], dkv_s[0])
    acc_qkv[2] += nn(a_aug[...], dkv_s[1])
    acc_fc1[...] += nt(dh_s[...], m_aug[...])
    acc_proj[...] += nt(o_aug[...], db_s[...])
    ig_rows = []
    for at in chunks:
        da = da_q[:, at] * scale + da_kv[:, at]
        u1, inv1 = stats(xT_s[:, at])
        acc_ln[0] += da * u1
        acc_ln[1] += da
        ig_rows.append(jnp.transpose(first_s[:, at] + ln_back(da, u1, inv1, column(0))))
    return roll_cols(from_tokens(jnp.concatenate(ig_rows, axis=0)), -SHIFT) + gy_rows[1 : 1 + WIN]


N_ACC = 7
N_PREP = 17
N_WTS = 7


def natural_rows(ref, side, every, start, count):
    ch = ref.shape[0] // every
    rows = [ref[pl.ds(start + r, ch, stride=every), :] for r in range(count)]
    return jnp.stack([jnp.transpose(row)[:side] for row in rows])


def edge_kernel(x_ref, gy_ref, out_ref, x_s, gy_s):
    _, ch, rows, side = x_ref.shape
    x_s[:, :side] = x_ref[0].astype(f32).reshape(ch * rows, side)
    gy_s[:, :side] = gy_ref[0].astype(f32).reshape(ch * rows, side)
    parts = [x_s[pl.ds(r, ch, stride=rows), :][:, :side] for r in range(SHIFT)]
    parts += [gy_s[pl.ds(r, ch, stride=rows), :][:, :side] for r in range(SHIFT + 1)]
    out_ref[0] = jnp.concatenate(parts, axis=1).astype(bf16)


def inner_kernel(image_side, own_rows, info, x_ref, gy_ref, *refs):
    wts, refs = refs[:N_WTS], refs[N_WTS:]
    c_out, ig_out, refs = refs[0], refs[1], refs[2:]
    acc, refs = refs[:N_ACC], refs[N_ACC:]
    x_s, gy_s, ig_s, refs = *refs[:3], refs[3:]
    prep, tmp = refs[:N_PREP], refs[N_PREP:]
    image, row_block = pl.program_id(0), pl.program_id(1)
    first_step = (image == 0) & (row_block == 0)

    @pl.when(first_step)
    def _():
        for ref in acc:
            ref[...] = jnp.zeros_like(ref)
        ig_s[...] = jnp.zeros_like(ig_s)

    @pl.when(row_block == 0)
    def _():
        ch = x_ref.shape[1]
        x_s[:, :image_side] = x_ref[0].astype(f32).reshape(ch * own_rows, image_side)
        gy_s[:, :image_side] = gy_ref[0].astype(f32).reshape(ch * own_rows, image_side)

    start = row_block * WIN + SHIFT
    x_rows = natural_rows(x_s, image_side, own_rows, start, WIN)
    gy_rows = natural_rows(gy_s, image_side, own_rows, start - 1, WIN + 2)
    base_row = info[0] * own_rows + start
    ig = block_step(
        x_rows, gy_rows, first_step, False, base_row, info[2 + image], image_side, wts, prep, acc, tmp, c_out
    )
    for r in range(WIN):
        ig_s[pl.ds(start + r, ig_out.shape[1], stride=own_rows), :image_side] = jnp.transpose(ig[r])

    @pl.when(row_block == pl.num_programs(1) - 1)
    def _():
        ig_out[0] = ig_s[:, :image_side].reshape(ig_out.shape[1:])


def last_kernel(image_side, own_rows, info, x_ref, gy_ref, halo_ref, ig_ref, *refs):
    wts, refs = refs[:N_WTS], refs[N_WTS:]
    acc_in, refs = refs[:N_ACC], refs[N_ACC:]
    sr_ref, hr_ref, c_out, ig_out, ig_halo, pack_out, refs = *refs[:6], refs[6:]
    acc, refs = refs[:N_ACC], refs[N_ACC:]
    x_s, gy_s, ig_s, refs = *refs[:3], refs[3:]
    prep, tmp = refs[:N_PREP], refs[N_PREP:]
    image = pl.program_id(0)
    first_step = image == 0

    @pl.when(first_step)
    def _():
        for ref, given in zip(acc, acc_in):
            ref[...] = given[...]

    ch = x_ref.shape[1]
    x_s[:, :image_side] = x_ref[0].astype(f32).reshape(ch * WIN, image_side)
    gy_s[:, :image_side] = gy_ref[0].astype(f32).reshape(ch * WIN, image_side)

    def halo_rows(start, size):
        rows = [halo_ref[0, :, r * image_side : (r + 1) * image_side] for r in range(start, start + size)]
        return jnp.stack([jnp.transpose(row.astype(f32)) for row in rows])

    x_rows = jnp.concatenate(
        [natural_rows(x_s, image_side, WIN, SHIFT, SHIFT), halo_rows(0, SHIFT)], axis=0
    )
    gy_rows = jnp.concatenate(
        [natural_rows(gy_s, image_side, WIN, SHIFT - 1, SHIFT + 1), halo_rows(SHIFT, SHIFT + 1)], axis=0
    )
    base_row = info[0] * own_rows + own_rows - SHIFT
    ig = block_step(
        x_rows, gy_rows, first_step, info[1] == 1, base_row, info[2 + image], image_side, wts, prep, acc, tmp, c_out
    )
    ig_s[:, :image_side] = ig_ref[0].reshape(ch * WIN, image_side)
    for r in range(SHIFT):
        ig_s[pl.ds(SHIFT + r, ch, stride=WIN), :image_side] = jnp.transpose(ig[r])
    ig_out[0] = ig_s[:, :image_side].reshape(ch, WIN, image_side)
    ig_halo[0] = jnp.concatenate([jnp.transpose(ig[SHIFT + r]) for r in range(SHIFT)], axis=1).astype(bf16)

    @pl.when(image == pl.num_programs(0) - 1)
    def _():
        pack_gradients(info[2 + pl.num_programs(0)], acc, sr_ref, hr_ref, pack_out)


def pack_rows(ch):
    up = -(-ch // 8) * 8
    blocks = 17
    vec_at = (blocks + (blocks + 1) // 2) * up
    return up, blocks, vec_at, vec_at + 32, vec_at + 32 + 3 * TOK


def pack_gradients(device, acc, sr_ref, hr_ref, out):
    (acc_conv, acc_qkv, acc_proj, acc_fc1, acc_fc2, acc_ln, acc_rel) = acc
    ch = acc_fc2.shape[1]
    dim = ch // HEADS
    up, count, vec_at, rel_at, used = pack_rows(ch)
    rest = ch - LANE
    out[used:, :] = jnp.zeros((out.shape[0] - used, LANE), f32)
    out[rel_at:used, :] = acc_rel[...]
    blocks = [acc_conv[:ch, t * CPAD : t * CPAD + ch] for t in range(9)]
    qkv = [drop_lanes(acc_qkv[k], HEADS, dim) for k in range(3)]
    blocks += [qkv[k][:ch] for k in range(3)]
    blocks += [drop_rows(acc_proj[...], HEADS, dim)]
    fc1 = jnp.transpose(acc_fc1[...])
    fc2 = jnp.transpose(acc_fc2[...])
    blocks += [fc1[:ch, :ch], fc1[:ch, ch:]]
    blocks += [fc2[:, :ch], fc2[:, ch:]]
    out[:vec_at, :] = jnp.zeros((vec_at, LANE), f32)
    for k, block in enumerate(blocks):
        out[k * up : k * up + ch, :] = block[:, :LANE]
        at = (count + k // 2) * up
        half = (k % 2) * TOK
        out[at : at + ch, half : half + rest] = block[:, LANE:]
    ln = [jnp.sum(jnp.transpose(acc_ln[k]), axis=0, keepdims=True) for k in range(5)]
    vec = [
        ln[0],
        ln[1],
        qkv[0][ch : ch + 1, :],
        qkv[2][ch : ch + 1, :],
        acc_proj[dim : dim + 1, :],
        ln[2],
        ln[3],
        fc1[ch : ch + 1, :ch],
        fc1[ch : ch + 1, ch:],
        ln[4],
        acc_conv[ch : ch + 1, 4 * CPAD : 4 * CPAD + ch],
    ]
    vec = jnp.concatenate(vec, axis=0)
    diff = sr_ref[...] - hr_ref[...]
    luma = (65.481 * diff[:, 0] + 128.553 * diff[:, 1] + 24.966 * diff[:, 2]) / 255.0
    square = jnp.sum(luma * luma, axis=1, keepdims=True)
    mse = jnp.sum(square, axis=2, keepdims=True) * (1.0 / (luma.shape[1] * luma.shape[2]))
    psnr = jnp.sum(jnp.log(mse + 1e-06) * (-10.0 / 2.302585092994046), axis=0)
    out[vec_at : vec_at + 32, :] = jnp.zeros((32, LANE), f32)
    out[vec_at : vec_at + 11, :] = vec[:, :LANE]
    lane = lax.broadcasted_iota(jnp.int32, (1, LANE), 1)
    for k in range(3):
        piece = psnr.astype(bf16).astype(f32)
        out[vec_at + 11 + k : vec_at + 12 + k, :] = jnp.where(lane == device, piece, 0.0)
        psnr = psnr - piece
    out[vec_at + 16 : vec_at + 27, :rest] = vec[:, LANE:]


def whole(shape):
    return pl.BlockSpec(shape, lambda *_: (0,) * len(shape))


def acc_shapes(ch, hid):
    return [
        (CPAD, 9 * CPAD),
        (3, CPAD, CPAD),
        (CPAD, ch),
        (hid, CPAD),
        (hid, ch),
        (5, ch, LANE),
        (3 * TOK, LANE),
    ]


def scratches(ch, hid, px, vec_rows):
    v = pltpu.VMEM
    prep = [
        v((ch, vec_rows), f32),
        v((3 * CPAD, ch), bf16), v((ch, CPAD), bf16), v((hid, ch), bf16), v((ch, hid), bf16),
        v((ch, CPAD), bf16), v((ch, CPAD), bf16), v((ch, CPAD), bf16), v((CPAD, ch), bf16),
        v((ch, hid), bf16), v((hid, ch), bf16),
        v((ch, 9 * CPAD), bf16),
        v((TOK, LANE), f32),
        v((TOK, LANE), f32),
        v((hid, LANE), f32),
        v((10, ch, LANE), f32),
        v((2, CPAD, LANE), f32),
    ]
    wins = px // TOK
    tmp = [
        v((px, 9 * CPAD), bf16),
        v((CPAD, px), bf16), v((CPAD, px), bf16), v((CPAD, px), bf16), v((hid, px), bf16), v((CPAD, px), bf16),
        v((wins, CPAD, LANE), bf16),
        v((wins, 3 * TOK, LANE), f32),
        v((wins, 3 * TOK, LANE), bf16),
        v((2, px, CPAD), bf16),
        v((ch, px), f32),
        v((CPAD, px), bf16),
        v((CPAD, px), bf16),
        v((2, px, CPAD), bf16),
        v((ch, px), f32),
        v((ch, px), f32),
        v((hid, px), f32),
        v((CPAD, px), bf16),
        v((CPAD, px), bf16),
        v((CPAD, px), bf16),
        v((8, px), f32),
        v((ch, px), bf16),
        v((hid, px), bf16),
    ]
    return prep + tmp


def halo_kernel(halo_ref, ig_ref, ig_out, ig_s):
    _, ch, rows, image_side = ig_ref.shape
    ig_s[:, :image_side] = ig_ref[0].reshape(ch * rows, image_side)
    for r in range(SHIFT):
        row = halo_ref[0, :, r * image_side : (r + 1) * image_side]
        ig_s[pl.ds(r, ch, stride=rows), :image_side] = row.astype(f32)
    ig_out[0] = ig_s[:, :image_side].reshape(ch, rows, image_side)


def bits_of(size):
    return list(range(size.bit_length() - 1))


def exchange_plan(sizes):
    (dp_axis, dp_size), (head_axis, head_size) = sizes
    first = (dp_axis, 0)
    rest = [(dp_axis, b) for b in bits_of(dp_size)[1:]]
    last = [(head_axis, b) for b in bits_of(head_size)]
    half = len(rest) // 2
    return first, [rest + last, rest[half:] + rest[:half] + last]


def exchange_kernel(
    first, orders, head_size,
    g_in, c1_in, c2_in, x_in, ig_in, conv_in, vec_ref,
    sum_ref, out_ref, ig_out,
    g, work, given, low, short, given_short, c1, c2, c_halo, ig_mine, ig_given, x, conv, wc, cs, rows_s, out_s,
    send_sem, recv_sem, local_sem,
):
    count, ch, own_rows, image_side = x.shape
    rows = g.shape[0]
    mesh_id = pl.DeviceIdType.MESH
    here = lax.axis_index("head")
    upper = {"head": (here + 1) % head_size}
    lower = {"head": (here + head_size - 1) % head_size}

    def load(k, src, dst):
        copy = pltpu.make_async_copy(src, dst, local_sem.at[k])
        copy.start()
        return copy

    loads = [
        load(0, g_in, g),
        load(1, conv_in, conv),
        load(2, c1_in, c1),
        load(3, c2_in, c2),
        load(4, x_in, x),
        load(5, ig_in, ig_mine),
    ]

    def meet(stage):
        axis, b = stage
        me = lax.axis_index(axis)
        step = 2**b
        bit = (me // step) % 2
        return {axis: me + (1 - 2 * bit) * step}, bit

    barrier = pltpu.get_barrier_semaphore()
    friends = [meet(stage)[0] for stage in [first] + orders[0]] + [upper, lower]
    for other in friends:
        pl.semaphore_signal(barrier, inc=1, device_id=other, device_id_type=mesh_id)
    pl.semaphore_wait(barrier, len(friends))

    used = [0]

    def send(src, dst, other):
        k = used[0]
        used[0] += 1
        copy = pltpu.make_async_remote_copy(
            src_ref=src,
            dst_ref=dst,
            send_sem=send_sem.at[k],
            recv_sem=recv_sem.at[k],
            device_id=other,
            device_id_type=mesh_id,
        )
        copy.start()
        return copy

    def span(start, size):
        return pl.ds(pl.multiple_of(start, 16), size)

    col = lax.broadcasted_iota(jnp.int32, (1, image_side, ch), 1)
    top = jnp.where(here == 0, 0.0, 1.0).astype(f32)
    bottom = jnp.where(here == head_size - 1, 0.0, 1.0).astype(f32)

    def prepare():
        loads[1].wait()
        wc[...] = jnp.zeros_like(wc)
        cs[...] = jnp.zeros_like(cs)
        for tap in range(9):
            wc[tap * TAP : tap * TAP + ch, :] = conv[tap // 3, tap % 3].astype(bf16)

    def conv_rows(image, block):
        for k in range(WIN + 2):
            r = block * WIN + k - 1 - SHIFT
            if r < 0:
                row = c_halo[image, r + SHIFT + 1 : r + SHIFT + 2]
            elif r < c1.shape[1]:
                row = c1[image, r : r + 1]
            else:
                row = c2[image, r - c1.shape[1] : r - c1.shape[1] + 1]
            row = row.astype(f32)
            if block == 0 and k == 0:
                row = row * top
            if block == own_rows // WIN - 1 and k == WIN + 1:
                row = row * bottom
            left = jnp.where(col == 0, 0.0, roll_cols(row, -1))
            right = jnp.where(col == image_side - 1, 0.0, roll_cols(row, 1))
            at = slice(k * image_side, (k + 1) * image_side)
            cs[at, 0:ch] = left[0].astype(bf16)
            cs[at, TAP : TAP + ch] = row[0].astype(bf16)
            cs[at, 2 * TAP : 2 * TAP + ch] = right[0].astype(bf16)
        total = vec_ref[10:11, :]
        for i in range(3):
            at = slice(i * image_side, (i + WIN) * image_side)
            total = total + nn(cs[at, :], wc[i * 3 * TAP : (i + 1) * 3 * TAP, :])
        for k in range(WIN):
            rows_s[image, block * WIN + k] = jnp.transpose(total[k * image_side : (k + 1) * image_side])

    stores = []

    def finish(image):
        out_s[image] = (jnp.swapaxes(rows_s[image], 0, 1) + x[image].astype(f32)).astype(bf16)
        stores.append(load(6 + image, out_s.at[image], out_ref.at[image]))

    blocks = own_rows // WIN
    inner = [(n, b) for n in range(count) for b in range(1, blocks)]
    outer = [(n, 0) for n in range(count)]
    stage_count = 2 * (1 + len(orders[0]))
    jobs = [[] for _ in range(stage_count)]
    for k, job in enumerate(inner + outer):
        jobs[min(1 + k * (stage_count - 2) // len(inner + outer), stage_count - 2)].append(job)

    halos = []

    def work_on(stage):
        if stage == 0:
            prepare()
        if stage == 1:
            for k in (2, 4, 5):
                loads[k].wait()
        for image, block in jobs[stage]:
            if block == 0 and image == 0:
                halos[0].wait()
            conv_rows(image, block)
            if block == 0:
                finish(image)

    loads[0].wait()
    other, bit = meet(first)
    half = rows // 2
    copy = send(g.at[span((1 - bit) * half, half)], given.at[pl.ds(0, half)], other)
    loads[3].wait()
    halos.append(send(c2.at[:, WIN - SHIFT - 1 :], c_halo, upper))
    work_on(0)
    copy.wait()
    keep = bit * half
    work[span(keep, half), :] = g[span(keep, half), :] + given[:half, :]
    unit = 16 * 2 ** len(orders[0])
    parts = half // unit
    cut = (parts + 1) // 2 * unit
    begin = [keep, keep + cut]
    size = [cut, half - cut]
    taken = half
    link_stages = len([stage for stage in orders[0] if stage[0] == first[0]])
    trail = [[], []]
    for s in range(len(orders[0])):
        flying = []
        for p in range(2):
            if size[p] == 0:
                continue
            other, bit = meet(orders[p][s])
            size[p] //= 2
            trail[p].append(begin[p])
            give = begin[p] + (1 - bit) * size[p]
            begin[p] = begin[p] + bit * size[p]
            if s < link_stages:
                short[span(give, size[p]), :] = work[span(give, size[p]), :].astype(bf16)
                copy = send(short.at[span(give, size[p])], given_short.at[pl.ds(taken - half, size[p])], other)
            else:
                copy = send(work.at[span(give, size[p])], given.at[pl.ds(taken, size[p])], other)
            flying.append((p, taken, copy))
            taken += size[p]
        work_on(1 + s)
        for p, at, copy in flying:
            copy.wait()
            if s < link_stages:
                there = given_short[at - half : at - half + size[p], :].astype(f32)
            else:
                there = given[at : at + size[p], :]
            total = work[span(begin[p], size[p]), :] + there
            if s < len(orders[0]) - 1:
                work[span(begin[p], size[p]), :] = total
            else:
                low[span(begin[p], size[p]), :] = total.astype(bf16)

    for s in reversed(range(len(orders[0]))):
        flying = []
        for p in range(2):
            if size[p] == 0:
                continue
            if s == link_stages - 1 and p == 0:
                halos.append(send(ig_mine, ig_given, upper))
            other, _ = meet(orders[p][s])
            here_now = low.at[span(begin[p], size[p])]
            flying.append(send(here_now, here_now, other))
            begin[p] = trail[p][s]
            size[p] *= 2
        work_on(2 * len(orders[0]) - s)
        for copy in flying:
            copy.wait()
    other, _ = meet(first)
    here_now = low.at[span(keep, half)]
    copy = send(here_now, here_now, other)
    work_on(stage_count - 1)
    copy.wait()
    sum_ref[...] = low[...]
    halos[1].wait()
    stores.append(load(6 + count, ig_given, ig_out))
    for copy in stores:
        copy.wait()


def exchange(packed, c1, c2, images, ig_halo, conv_weight, vectors, sizes):
    first, orders = exchange_plan(sizes)
    rows = packed.shape[0]
    count, ch, own_rows, image_side = images.shape
    vmem = pl.BlockSpec(memory_space=pltpu.VMEM)
    hbm = pl.BlockSpec(memory_space=pl.ANY)
    v = pltpu.VMEM
    sends = 2 + 2 + 4 * len(orders[0])
    return pl.pallas_call(
        functools.partial(exchange_kernel, first, orders, sizes[1][1]),
        in_specs=[hbm] * 6 + [vmem],
        out_specs=[vmem, hbm, hbm],
        out_shape=[
            jax.ShapeDtypeStruct(packed.shape, bf16),
            jax.ShapeDtypeStruct(images.shape, bf16),
            jax.ShapeDtypeStruct(ig_halo.shape, bf16),
        ],
        scratch_shapes=[
            v(packed.shape, f32),
            v(packed.shape, f32),
            v(packed.shape, f32),
            v(packed.shape, bf16),
            v(packed.shape, bf16),
            v((rows // 2, LANE), bf16),
            v(c1.shape, bf16),
            v(c2.shape, bf16),
            v((count, SHIFT + 1, image_side, ch), bf16),
            v(ig_halo.shape, bf16),
            v(ig_halo.shape, bf16),
            v(images.shape, bf16),
            v(conv_weight.shape, f32),
            v((9 * TAP, ch), bf16),
            v(((WIN + 2) * image_side, 3 * TAP), bf16),
            v((count, own_rows, ch, image_side), f32),
            v(images.shape, bf16),
            pltpu.SemaphoreType.DMA((sends,)),
            pltpu.SemaphoreType.DMA((sends,)),
            pltpu.SemaphoreType.DMA((7 + count,)),
        ],
        compiler_params=pltpu.CompilerParams(
            collective_id=0, has_side_effects=True, vmem_limit_bytes=40 * 1024 * 1024
        ),
        name="sum_gradients",
    )(packed, c1, c2, images, ig_halo, conv_weight, vectors)


def adam_kernel(scal, g_ref, *refs):
    given, norm_ref, psnr_ref, results = refs[:21], refs[21], refs[22], refs[23:]
    weights = given[0::3]
    ch = weights[2].shape[0]
    up, count, vec_at, rel_at, used = pack_rows(ch)
    rest = ch - LANE

    def block(k):
        left = g_ref[k * up : (k + 1) * up, :].astype(f32)
        at = (count + k // 2) * up
        right = g_ref[at : at + up, :].astype(f32)
        if k % 2:
            right = pltpu.roll(right, TOK, 1)
        return jnp.concatenate([left, right[:, :rest]], axis=1)[:ch]

    vec_rows = g_ref[vec_at : vec_at + 32, :].astype(f32)
    vec = jnp.concatenate([vec_rows[:11], vec_rows[16:27, :rest]], axis=1)
    psnr = vec_rows[11:12] + vec_rows[12:13] + vec_rows[13:14]
    psnr_ref[...] = jnp.sum(psnr, axis=1, keepdims=True)

    span = 2 * WIN
    wide = span * span
    at = lax.broadcasted_iota(jnp.int32, (TOK, wide), 0)
    to = lax.broadcasted_iota(jnp.int32, (TOK, wide), 1)
    place = ((at >> 3) + (WIN - 1)) * span + (at & 7) + (WIN - 1)
    expand = (to == place).astype(f32).astype(bf16)
    pairs = g_ref[rel_at:used, :]
    rel_rows = []
    for p in range(3):
        for parity in range(2):
            part = pairs[p * TOK : (p + 1) * TOK, :].astype(f32)
            if parity:
                part = pltpu.roll(part, TOK, 1)
            spread = nn(part[:, :TOK].astype(bf16), expand)
            total = jnp.zeros((WIN, wide), f32)
            for row in range(WIN):
                piece = spread[row * WIN : (row + 1) * WIN]
                piece = pltpu.roll(piece, (wide - span * row) % wide, 1)
                total = total + piece
            line = total[0:1]
            for c in range(1, WIN):
                line = line + pltpu.roll(total, wide - c, 1)[c : c + 1]
            rel_rows.append(line)
    rel = jnp.concatenate(rel_rows, axis=0)
    rel = jnp.concatenate(
        [rel[:, k * span : k * span + span - 1] for k in range(span - 1)], axis=1
    )
    qkv = jnp.concatenate([block(9), block(10), block(11)], axis=1)
    fc1 = jnp.concatenate([block(13), block(14)], axis=1)
    fc2 = jnp.concatenate([block(15), block(16)], axis=1)
    small = [vec, qkv, block(12), rel, fc1, fc2]
    taps = [block(t) for t in range(9)]
    total = jnp.zeros((1, 1), f32)
    for g in small + taps:
        total = total + jnp.sum(jnp.sum(g * g, axis=0, keepdims=True), axis=1, keepdims=True)
    norm = jnp.sqrt(total)
    norm_ref[...] = norm
    clip = jnp.minimum(1.0, max_norm / (norm + 1e-06))
    fix_one, fix_two = scal[0], scal[1]

    def update(w, m1, m2, g, rate):
        g = g * clip
        m1 = beta_one * m1 + (1.0 - beta_one) * g
        m2 = beta_two * m2 + (1.0 - beta_two) * g * g
        step = (m1 / fix_one) / (jnp.sqrt(m2 / fix_two) + adam_eps)
        return w - rate * (step + decay_rate * w), m1, m2

    for k in range(7):
        w, m1, m2 = given[3 * k : 3 * k + 3]
        new = results[3 * k : 3 * k + 3]
        if k == 6:
            for t, g in enumerate(taps):
                at = (t // 3, t % 3)
                for ref, value in zip(new, update(w[at], m1[at], m2[at], g, learn_rate)):
                    ref[at] = value
        else:
            rate = vector_rate if k == 0 else learn_rate
            for ref, value in zip(new, update(w[...], m1[...], m2[...], small[k], rate)):
                ref[...] = value


def relative_onehot_keys_first():
    position = np.arange(TOK)
    pos_row, pos_col = position // WIN, position % WIN
    span = 2 * WIN - 1
    index = (pos_row[None, :] - pos_row[:, None] + WIN - 1) * span + (
        pos_col[None, :] - pos_col[:, None] + WIN - 1
    )
    return index.reshape(-1), span * span


def on_device(
    images, cotangent, valid_size,
    vectors, vectors_first, vectors_second,
    qkv_weight, qkv_first, qkv_second,
    proj_weight, proj_first, proj_second,
    rel_table, rel_first, rel_second,
    fc1_weight, fc1_first, fc1_second,
    fc2_weight, fc2_first, fc2_second,
    conv_weight, conv_first, conv_second,
    step, sr_crops, hr_crops, psnr_running,
):
    count, own_rows, image_side, ch = images.shape
    out_shape = (count, ch, own_rows, image_side)
    hid = fc1_weight.shape[1]
    px = image_side * WIN
    blocks = own_rows // WIN
    heads = lax.axis_size("head")
    place = lax.axis_index("head")
    to_lower = [((i + 1) % heads, i) for i in range(heads)]
    info = jnp.concatenate(
        [
            jnp.stack([place, (place == heads - 1).astype(jnp.int32)]).astype(jnp.int32),
            valid_size.astype(jnp.int32),
            ((lax.axis_index("dp") * heads + place) % LANE)[None].astype(jnp.int32),
        ]
    )
    images = images.transpose(0, 3, 1, 2)
    cotangent = cotangent.transpose(0, 3, 1, 2)
    top_rows = pl.BlockSpec((1, ch, WIN, image_side), lambda n: (n, 0, 0, 0))
    edge = pl.pallas_call(
        edge_kernel,
        grid=(count,),
        in_specs=[top_rows, top_rows],
        out_specs=pl.BlockSpec((1, ch, (2 * SHIFT + 1) * image_side), lambda n: (n, 0, 0)),
        out_shape=jax.ShapeDtypeStruct((count, ch, (2 * SHIFT + 1) * image_side), bf16),
        scratch_shapes=[pltpu.VMEM((ch * WIN, LANE), f32)] * 2,
        name="edge_rows",
    )(images, cotangent)
    halo = lax.ppermute(edge, "head", to_lower)

    index, span = relative_onehot_keys_first()
    onehot = (jnp.asarray(index)[:, None] == jnp.arange(span)[None, :]).astype(f32)
    bias = jnp.dot(onehot, rel_table, precision=highest)
    bias = bias.reshape(TOK, TOK, 3, 2).transpose(2, 0, 3, 1).reshape(3, TOK, LANE)

    wts = (vectors, qkv_weight, proj_weight, fc1_weight, fc2_weight.T, conv_weight, bias)
    wts_specs = [whole(w.shape) for w in wts]
    acc_dims = acc_shapes(ch, hid)
    acc_types = [jax.ShapeDtypeStruct(s, f32) for s in acc_dims]
    smem = pl.BlockSpec(memory_space=pltpu.SMEM)
    params = pltpu.CompilerParams(
        dimension_semantics=("arbitrary", "arbitrary"), vmem_limit_bytes=46 * 1024 * 1024
    )
    view = lambda rows, at, dims: pl.BlockSpec((1, ch, rows, image_side), lambda n, *_: (n, 0, at, 0))
    c_block = lambda size: pl.BlockSpec((1, size, image_side, ch), lambda n, *_: (n, 0, 0, 0))
    row_view = pltpu.VMEM((ch * own_rows, LANE), f32)
    c1, ig, *acc = pl.pallas_call(
        functools.partial(inner_kernel, image_side, own_rows),
        grid=(count, blocks - 1),
        in_specs=[smem, view(own_rows, 0, 2), view(own_rows, 0, 2), *wts_specs],
        out_specs=[
            pl.BlockSpec((1, WIN, image_side, ch), lambda n, r: (n, r, 0, 0)),
            view(own_rows, 0, 2),
            *[whole(s) for s in acc_dims],
        ],
        out_shape=[
            jax.ShapeDtypeStruct((count, own_rows - WIN, image_side, ch), bf16),
            jax.ShapeDtypeStruct(out_shape, f32),
            *acc_types,
        ],
        scratch_shapes=[row_view] * 3 + scratches(ch, hid, px, vectors.shape[0]),
        compiler_params=params,
        name="inner_windows",
    )(info, images, cotangent, *wts)
    device_count = lax.axis_size("dp") * heads
    unit = 16 * device_count
    rows = -(-pack_rows(ch)[-1] // unit) * unit
    c2, ig, ig_halo, packed = pl.pallas_call(
        functools.partial(last_kernel, image_side, own_rows),
        grid=(count,),
        in_specs=[
            smem,
            view(WIN, blocks - 1, 1),
            view(WIN, blocks - 1, 1),
            pl.BlockSpec((1, ch, halo.shape[2]), lambda n: (n, 0, 0)),
            view(WIN, blocks - 1, 1),
            *wts_specs,
            *[whole(s) for s in acc_dims],
            whole(sr_crops.shape),
            whole(hr_crops.shape),
        ],
        out_specs=[
            c_block(WIN),
            view(WIN, blocks - 1, 1),
            pl.BlockSpec((1, ch, SHIFT * image_side), lambda n: (n, 0, 0)),
            whole((rows, LANE)),
        ],
        out_shape=[
            jax.ShapeDtypeStruct((count, WIN, image_side, ch), bf16),
            jax.ShapeDtypeStruct(out_shape, f32),
            jax.ShapeDtypeStruct((count, ch, SHIFT * image_side), bf16),
            jax.ShapeDtypeStruct((rows, LANE), f32),
        ],
        input_output_aliases={4: 1},
        scratch_shapes=[pltpu.VMEM(s, f32) for s in acc_dims]
        + [pltpu.VMEM((ch * k, LANE), f32) for k in (WIN, WIN, WIN)]
        + scratches(ch, hid, px, vectors.shape[0]),
        compiler_params=pltpu.CompilerParams(
            dimension_semantics=("arbitrary",), vmem_limit_bytes=46 * 1024 * 1024
        ),
        name="last_windows",
    )(info, images, cotangent, halo, ig, *wts, *acc, sr_crops, hr_crops)

    summed, output, ig_halo = exchange(
        packed, c1, c2, images, ig_halo, conv_weight, vectors, (("dp", lax.axis_size("dp")), ("head", heads))
    )
    image_grad = pl.pallas_call(
        halo_kernel,
        grid=(count,),
        in_specs=[pl.BlockSpec((1, ch, SHIFT * image_side), lambda n: (n, 0, 0)), view(WIN, 0, 1)],
        out_specs=view(WIN, 0, 1),
        scratch_shapes=[pltpu.VMEM((ch * WIN, LANE), f32)],
        out_shape=jax.ShapeDtypeStruct(out_shape, f32),
        input_output_aliases={1: 0},
        name="halo_rows",
    )(ig_halo, ig)
    output, image_grad = output.transpose(0, 2, 3, 1), image_grad.transpose(0, 2, 3, 1)

    step_count = step[0].astype(f32)
    scal = jnp.stack([1.0 - beta_one**step_count, 1.0 - beta_two**step_count])
    weights = (vectors, qkv_weight, proj_weight, rel_table.T, fc1_weight, fc2_weight.T, conv_weight)
    firsts = (vectors_first, qkv_first, proj_first, rel_first.T, fc1_first, fc2_first.T, conv_first)
    seconds = (vectors_second, qkv_second, proj_second, rel_second.T, fc1_second, fc2_second.T, conv_second)
    vmem = pl.BlockSpec(memory_space=pltpu.VMEM)
    state = [array for group in zip(weights, firsts, seconds) for array in group]
    grad_norm, psnr, *updated = pl.pallas_call(
        adam_kernel,
        in_specs=[smem] + [vmem] * 22,
        out_specs=[vmem] * 23,
        out_shape=[jax.ShapeDtypeStruct((1, 1), f32)] * 2
        + [jax.ShapeDtypeStruct(array.shape, f32) for array in state],
        compiler_params=pltpu.CompilerParams(vmem_limit_bytes=60 * 1024 * 1024),
        name="adam",
    )(scal, summed, *state)
    for k in (9, 10, 11, 15, 16, 17):
        updated[k] = updated[k].T
    psnr_total = psnr_running + psnr.reshape(1)
    return (output, image_grad, grad_norm.reshape(1), psnr_total, *updated)


def solution(mesh):
    pixels = P("dp", "head", None, None)
    crops = P(("dp", "head"), None, None, None)
    placed = (pixels, pixels, P("dp")) + (P(),) * 22 + (crops, crops, P())
    return jax.shard_map(
        on_device,
        mesh=mesh,
        in_specs=placed,
        out_specs=(pixels, pixels) + (P(),) * 23,
        check_vma=False,
    )
```

```python
import functools

import jax
import jax.numpy as jnp
import numpy as np
from jax import lax
from jax.experimental import pallas as pl
from jax.experimental.pallas import tpu as pltpu
from jax.sharding import PartitionSpec as P

WIN = 8
TOK = WIN * WIN
SHIFT = WIN // 2
LANE = 128
TAP = 256
HPAD = 32
HEADS = 6
CPAD = HEADS * HPAD

eps_norm = 1e-05
neg_mask = -100.0
max_norm = 1.0
learn_rate = 0.03
vector_rate = 0.2
beta_one = 0.9
beta_two = 0.999
adam_eps = 1e-08
decay_rate = 0.01
highest = lax.Precision.HIGHEST
f32 = jnp.float32
bf16 = jnp.bfloat16


def nn(a, b):
    return lax.dot_general(a, b, (((1,), (0,)), ((), ())), preferred_element_type=f32)


def nt(a, b):
    return lax.dot_general(a, b, (((1,), (1,)), ((), ())), preferred_element_type=f32)


def pad_heads(rows, heads):
    dim = rows.shape[0] // heads
    gap = jnp.zeros((HPAD - dim, rows.shape[1]), rows.dtype)
    parts = []
    for h in range(heads):
        parts += [rows[h * dim : (h + 1) * dim], gap]
    return jnp.concatenate(parts, axis=0)


def drop_rows(rows, heads, dim):
    return jnp.concatenate([rows[h * HPAD : h * HPAD + dim] for h in range(heads)], axis=0)


def drop_lanes(rows, heads, dim):
    return jnp.concatenate([rows[:, h * HPAD : h * HPAD + dim] for h in range(heads)], axis=1)


def to_tokens(rows):
    side = rows.shape[1]
    return jnp.concatenate(
        [rows[:, w * WIN : (w + 1) * WIN, :].reshape(TOK, rows.shape[2]) for w in range(side // WIN)],
        axis=0,
    )


def from_tokens(tokens):
    count = tokens.shape[0] // TOK
    return jnp.concatenate(
        [tokens[w * TOK : (w + 1) * TOK].reshape(WIN, WIN, tokens.shape[1]) for w in range(count)],
        axis=1,
    )


def roll_cols(rows, by):
    side = rows.shape[1]
    by = by % side
    return jnp.concatenate([rows[:, by:, :], rows[:, :by, :]], axis=1)


def block_step(x_rows, gy_rows, first_step, edge, base_row, valid, image_side, wts, prep, acc, tmp, c_out):
    (vec_ref, qkv_ref, proj_ref, fc1_ref, fc2_ref, conv_ref, bias_ref) = wts
    (vecT, wqkvT, wpT, w1T, w2T, wq, wk, wv, wp, w1, w2, wc, colmask, rowmask, b1T, wide_vec, head_vec) = prep
    (acc_conv, acc_qkv, acc_proj, acc_fc1, acc_fc2, acc_ln, acc_rel) = acc
    (g9, a_aug, o_aug, m_aug, g_aug, c_aug, qeo_s, p_s, pb_s, kv_s, first_s, do_s, dq_s, dkv_s, u2_s, xT_s, slope_s, vt_s, qt_s, kt_s, inv_s, db_s, dh_s) = tmp
    ch = x_rows.shape[2]
    dim = ch // HEADS
    hid = fc1_ref.shape[1]
    px = x_rows.shape[1] * WIN
    pairs = px // LANE
    ones_row = dim

    @pl.when(first_step)
    def _():
        vecT[...] = jnp.transpose(vec_ref[...])
        for k in range(10):
            wide_vec[k] = jnp.broadcast_to(vecT[:, k : k + 1], (ch, LANE))
        for k in range(2):
            head_vec[k] = pad_heads(wide_vec[2 + k], HEADS)
        b1T[:ch, :] = wide_vec[7]
        b1T[ch:, :] = wide_vec[8]
        for k, dst in enumerate((wq, wk, wv)):
            part = pad_heads(jnp.transpose(qkv_ref[:, k * ch : (k + 1) * ch]), HEADS)
            wqkvT[k * CPAD : (k + 1) * CPAD, :] = part.astype(bf16)
            dst[...] = jnp.transpose(part).astype(bf16)
        padded = pad_heads(proj_ref[...], HEADS)
        wp[...] = padded.astype(bf16)
        wpT[...] = jnp.transpose(padded).astype(bf16)
        w1[...] = fc1_ref[...].astype(bf16)
        w1T[...] = jnp.transpose(fc1_ref[...]).astype(bf16)
        w2T[...] = fc2_ref[...].astype(bf16)
        w2[...] = jnp.transpose(fc2_ref[...]).astype(bf16)
        wc[...] = jnp.zeros_like(wc)
        g9[...] = jnp.zeros_like(g9)
        for tap in range(9):
            wc[:, tap * CPAD : tap * CPAD + ch] = conv_ref[tap // 3, tap % 3].astype(bf16)
        key = lax.broadcasted_iota(jnp.int32, (TOK, LANE), 0)
        query = lax.broadcasted_iota(jnp.int32, (TOK, LANE), 1) & (TOK - 1)
        one = lambda m: m.astype(f32)
        colmask[...] = one(((key & 7) < SHIFT) != ((query & 7) < SHIFT))
        rowmask[...] = one(((key >> 3) < SHIFT) != ((query >> 3) < SHIFT))
        for ref in (a_aug, m_aug, c_aug):
            pad = ref.shape[0] - ch
            ref[ch:, :] = (lax.broadcasted_iota(jnp.int32, (pad, px), 0) == 0).astype(f32).astype(bf16)

    def column(k):
        return wide_vec[k]

    def stats(v):
        mean = jnp.sum(v, axis=0, keepdims=True) * (1.0 / ch)
        cen = v - mean
        var = jnp.sum(cen * cen, axis=0, keepdims=True) * (1.0 / ch)
        inv = lax.rsqrt(var + eps_norm)
        return cen * inv, inv

    def ln_back(grad, u, inv, gain):
        t = grad * gain
        mean_t = jnp.sum(t, axis=0, keepdims=True) * (1.0 / ch)
        mean_tu = jnp.sum(t * u, axis=0, keepdims=True) * (1.0 / ch)
        return inv * (t - mean_t - u * mean_tu)

    chunks = [slice(k * LANE, (k + 1) * LANE) for k in range(px // LANE)]
    third = hid // 3
    bands = [slice(k * third, (k + 1) * third) for k in range(3)]

    keep = jnp.where(edge, 0.0, 1.0).astype(f32)
    col = lax.broadcasted_iota(jnp.int32, (1, image_side, ch), 1)
    moved = {}

    def build_tap(tap):
        i, j = tap % 3, tap // 3
        if i == 0:
            shifted = roll_cols(gy_rows, SHIFT + 1 - j)
            if j == 0:
                shifted = jnp.where(col == image_side - SHIFT - 1, 0.0, shifted)
            if j == 2:
                shifted = jnp.where(col == image_side - SHIFT, 0.0, shifted)
            moved[j] = shifted
        rows = [moved[j][r + 2 - i : r + 3 - i] for r in range(WIN)]
        if i == 0:
            rows[SHIFT - 1] = rows[SHIFT - 1] * keep
        if i == 2:
            rows[SHIFT] = rows[SHIFT] * keep
        at = (3 * i + j) * CPAD
        g9[:, at : at + ch] = to_tokens(jnp.concatenate(rows, axis=0)).astype(bf16)

    x_tok = to_tokens(roll_cols(x_rows, SHIFT))
    for at in chunks:
        xT = jnp.transpose(x_tok[at])
        xT_s[:, at] = xT
        u1, _ = stats(xT)
        a_aug[:ch, at] = (u1 * column(0) + column(1)).astype(bf16)
    scale = dim ** (-0.5)
    qkv_all = nn(wqkvT[...], a_aug[:ch, :])
    for at in chunks:
        qt_s[:, at] = ((qkv_all[:CPAD, at] + head_vec[0]) * scale).astype(bf16)
        kT = qkv_all[CPAD : 2 * CPAD, at].astype(bf16)
        vT = (qkv_all[2 * CPAD :, at] + head_vec[1]).astype(bf16)
        kt_s[:, at] = kT
        vt_s[:, at] = vT
        kv_s[0, at, :] = jnp.transpose(kT.astype(f32)).astype(bf16)
        kv_s[1, at, :] = jnp.transpose(vT.astype(f32)).astype(bf16)

    def low_lanes(rows):
        return lax.broadcasted_iota(jnp.int32, (rows, LANE), 1) < TOK

    def swap(slab):
        return pltpu.roll(slab, TOK, 1)

    def only_low(v):
        return jnp.where(low_lanes(v.shape[0]), v, jnp.zeros_like(v))

    def only_high(v):
        return jnp.where(low_lanes(v.shape[0]), jnp.zeros_like(v), v)

    def head_rows(v, h):
        return v[h * HPAD : (h + 1) * HPAD]

    def dup(slab):
        slab = slab.astype(f32)
        other = swap(slab)
        out = []
        for low, high in ((slab, other), (other, slab)):
            rows = [
                only_high(head_rows(high, h)) if h % 2 else only_low(head_rows(low, h)) for h in range(HEADS)
            ]
            out.append(jnp.concatenate(rows, axis=0).astype(bf16))
        return out

    def spread(slab):
        slab = slab.astype(f32)
        other = swap(slab)
        two = 2 * HPAD
        gap = jnp.zeros((two, TOK), f32)
        wide = jnp.zeros((two, LANE), f32)
        out = []
        for low, high in ((slab, other), (other, slab)):
            rows = [
                jnp.concatenate([only_low(low[:two]), gap], axis=1),
                jnp.concatenate([only_high(high[two : 2 * two]), gap], axis=1),
                jnp.concatenate([wide, low[2 * two :, :TOK]], axis=1),
            ]
            out.append(jnp.concatenate(rows, axis=0).astype(bf16))
        return out

    def merge(one, two):
        rows = []
        for h in range(HEADS):
            first, second = head_rows(one, h), head_rows(two, h)
            if h % 2:
                rows.append(jnp.where(low_lanes(HPAD), swap(first), second))
            else:
                rows.append(jnp.where(low_lanes(HPAD), first, swap(second)))
        return jnp.concatenate(rows, axis=0)

    def by_pair(rows):
        front, back = rows[:, :LANE], rows[:, LANE:]
        zero_back = jnp.zeros_like(back)
        return jnp.concatenate(
            [
                jnp.concatenate([only_low(front), zero_back], axis=1),
                jnp.concatenate([only_high(front), zero_back], axis=1),
                jnp.concatenate([jnp.zeros_like(front), back], axis=1),
            ],
            axis=0,
        )

    def pick_pair(stacked):
        front = jnp.where(low_lanes(TOK), stacked[:TOK, :LANE], stacked[TOK : 2 * TOK, :LANE])
        return jnp.concatenate([front, stacked[2 * TOK :, LANE:]], axis=1)

    key = lax.broadcasted_iota(jnp.int32, (TOK, LANE), 0)
    key_row = base_row + (key >> 3)
    key_row = jnp.where(key_row >= image_side, key_row - image_side, key_row)
    out_row = key_row >= valid
    edge_f = jnp.where(edge, neg_mask, 0.0).astype(f32)

    def scores_of(pp):
        q_pair = dup(qt_s[:, chunks[pp]])
        raw = []
        for half in range(2):
            w = 2 * pp + half
            qeo_s[w] = q_pair[half]
            raw.append(nn(by_pair(kv_s[0, w * TOK : (w + 1) * TOK, :]), q_pair[half]))
        return raw

    def soften(pp, raw):
        for half in range(2):
            w = 2 * pp + half
            key_col = (key & 7) + (w * WIN + SHIFT)
            apart = rowmask[...] * edge_f
            if w == 2 * pairs - 1:
                key_col = jnp.where(key_col >= image_side, key_col - image_side, key_col)
                apart = jnp.where(colmask[...] > 0.5, neg_mask, apart)
            extra = apart + jnp.where(out_row | (key_col >= valid), neg_mask, 0.0)
            s = raw[half].reshape(3, TOK, LANE) + bias_ref[...] + extra[None]
            top = jnp.max(s, axis=1, keepdims=True)
            e = jnp.exp(s - top)
            p = e / jnp.sum(e, axis=1, keepdims=True)
            p = p.reshape(3 * TOK, LANE)
            p_s[w] = p
            pb_s[w] = p.astype(bf16)

    def mix(pp):
        v_pair = spread(vt_s[:, chunks[pp]])
        return [nn(v_pair[half], pb_s[2 * pp + half]) for half in range(2)]

    def place(pp, mixed):
        o_aug[:, chunks[pp]] = merge(*mixed).astype(bf16)

    raws, mixes = {}, {}
    for t in range(pairs + 3):
        if 0 <= t - 2 < pairs:
            mixes[t - 2] = mix(t - 2)
        if t < pairs:
            raws[t] = scores_of(t)
        if 0 <= t - 1 < pairs:
            soften(t - 1, raws.pop(t - 1))
        if 0 <= t - 3 < pairs:
            place(t - 3, mixes.pop(t - 3))
        if t < 9:
            build_tap(t)
    o_aug[ones_row : ones_row + 1, :] = jnp.ones((1, px), bf16)

    attn = nn(wpT[...], o_aug[...])
    part = px // 3
    conv_back = [nt(wc[...], g9[:part, :])]
    for at in chunks:
        first = xT_s[:, at] + (attn[:, at] + column(4))
        first_s[:, at] = first
        u2, inv2 = stats(first)
        u2_s[:, at] = u2
        inv_s[0:1, at] = inv2
        m_aug[:ch, at] = (u2 * column(5) + column(6)).astype(bf16)
    hidden_all = nn(w1T[...], m_aug[:ch, :])
    conv_back.append(nt(wc[...], g9[part : 2 * part, :]))
    for at in chunks:
        for band in bands:
            hidden = hidden_all[band, at] + b1T[band, :]
            cdf = 0.5 * (1.0 + lax.erf(hidden * 0.7071067811865476))
            g_aug[band, at] = (hidden * cdf).astype(bf16)
            slope_s[band, at] = cdf + hidden * jnp.exp(-0.5 * hidden * hidden) * 0.3989422804014327
    branch = nn(w2T[...], g_aug[...])
    conv_back.append(nt(wc[...], g9[2 * part :, :]))
    c_rows = []
    for at in chunks:
        cT = (first_s[:, at] + (branch[:, at] + column(9))).astype(bf16)
        c_aug[:ch, at] = cT
        c_rows.append(jnp.transpose(cT.astype(f32)))
    c_out[0] = roll_cols(from_tokens(jnp.concatenate(c_rows, axis=0)), -SHIFT).astype(bf16)

    def conv_grad(k):
        at = slice(k * TAP, min((k + 1) * TAP, 9 * CPAD))
        if at.start < at.stop:
            acc_conv[:, at] += nn(c_aug[...], g9[:, at])

    dsecond = jnp.concatenate(conv_back, axis=1)
    for at in chunks:
        dbT = dsecond[:, at].astype(bf16)
        db_s[:, at] = dbT
        acc_ln[4] += dbT.astype(f32)
    dg = nn(w2[...], db_s[...])
    acc_fc2[...] += nt(g_aug[...], db_s[...])
    for at in chunks:
        for band in bands:
            dh_s[band, at] = (dg[band, at] * slope_s[band, at]).astype(bf16)
    dm_all = nn(w1[...], dh_s[...])
    for at in chunks:
        u2 = u2_s[:, at]
        dm = dm_all[:, at]
        acc_ln[2] += dm * u2
        acc_ln[3] += dm
        dfirst = dsecond[:, at] + ln_back(dm, u2, inv_s[0:1, at], column(5))
        first_s[:, at] = dfirst
        db_s[:, at] = dfirst.astype(bf16)
    do_all = nn(wp[...], db_s[...])
    for at in chunks:
        do_s[:, at] = do_all[:, at].astype(bf16)

    rel_sum = jnp.zeros((3 * TOK, LANE), f32)

    def probs_grad(pp):
        do_pair = dup(do_s[:, chunks[pp]])
        dps, dvs = [], []
        for half in range(2):
            w = 2 * pp + half
            dps.append(nn(by_pair(kv_s[1, w * TOK : (w + 1) * TOK, :]), do_pair[half]))
            dvs.append(nt(pb_s[w], do_pair[half]))
        return dps, dvs

    def scores_grad(pp, dps, dvs, rel_sum):
        out = []
        for half in range(2):
            w = 2 * pp + half
            p = p_s[w].reshape(3, TOK, LANE)
            dp = dps[half].reshape(3, TOK, LANE)
            ds = p * (dp - jnp.sum(p * dp, axis=1, keepdims=True))
            ds = ds.reshape(3 * TOK, LANE).astype(bf16)
            rel_sum = rel_sum + ds.astype(f32)
            out.append(ds)
            dkv_s[1, w * TOK : (w + 1) * TOK, :] = pick_pair(dvs[half]).astype(bf16)
        return out, rel_sum

    def inner_grads(pp, ds):
        k_pair = spread(kt_s[:, chunks[pp]])
        dks = [nt(ds[half], qeo_s[2 * pp + half]) for half in range(2)]
        dqs = [nn(k_pair[half], ds[half]) for half in range(2)]
        return dks, dqs

    def place_grads(pp, dks, dqs):
        for half in range(2):
            w = 2 * pp + half
            dkv_s[0, w * TOK : (w + 1) * TOK, :] = pick_pair(dks[half]).astype(bf16)
        dq_s[:, chunks[pp]] = merge(*dqs).astype(bf16)

    first_part, second_part, third_part = {}, {}, {}
    for t in range(pairs + 3):
        if 0 <= t - 2 < pairs:
            third_part[t - 2] = inner_grads(t - 2, second_part.pop(t - 2))
        if t < pairs:
            first_part[t] = probs_grad(t)
        if 0 <= t - 1 < pairs:
            second_part[t - 1], rel_sum = scores_grad(t - 1, *first_part.pop(t - 1), rel_sum)
        if 0 <= t - 3 < pairs:
            place_grads(t - 3, *third_part.pop(t - 3))
        conv_grad(t)
    acc_rel[...] += rel_sum

    dqT = dq_s[...]
    da_q = nn(wq[...], dqT)
    da_kv = nt(wk[...], dkv_s[0]) + nt(wv[...], dkv_s[1])
    acc_qkv[0] += nt(a_aug[...], dqT) * scale
    acc_qkv[1] += nn(a_aug[...], dkv_s[0])
    acc_qkv[2] += nn(a_aug[...], dkv_s[1])
    acc_fc1[...] += nt(dh_s[...], m_aug[...])
    acc_proj[...] += nt(o_aug[...], db_s[...])
    ig_rows = []
    for at in chunks:
        da = da_q[:, at] * scale + da_kv[:, at]
        u1, inv1 = stats(xT_s[:, at])
        acc_ln[0] += da * u1
        acc_ln[1] += da
        ig_rows.append(jnp.transpose(first_s[:, at] + ln_back(da, u1, inv1, column(0))))
    return roll_cols(from_tokens(jnp.concatenate(ig_rows, axis=0)), -SHIFT) + gy_rows[1 : 1 + WIN]


N_ACC = 7
N_PREP = 17
N_WTS = 7


def natural_rows(ref, side, every, start, count):
    ch = ref.shape[0] // every
    rows = [ref[pl.ds(start + r, ch, stride=every), :] for r in range(count)]
    return jnp.stack([jnp.transpose(row)[:side] for row in rows])


def edge_kernel(x_ref, gy_ref, out_ref, x_s, gy_s):
    _, ch, rows, side = x_ref.shape
    x_s[:, :side] = x_ref[0].astype(f32).reshape(ch * rows, side)
    gy_s[:, :side] = gy_ref[0].astype(f32).reshape(ch * rows, side)
    parts = [x_s[pl.ds(r, ch, stride=rows), :][:, :side] for r in range(SHIFT)]
    parts += [gy_s[pl.ds(r, ch, stride=rows), :][:, :side] for r in range(SHIFT + 1)]
    out_ref[0] = jnp.concatenate(parts, axis=1).astype(bf16)


def inner_kernel(image_side, own_rows, info, x_ref, gy_ref, *refs):
    wts, refs = refs[:N_WTS], refs[N_WTS:]
    c_out, ig_out, refs = refs[0], refs[1], refs[2:]
    acc, refs = refs[:N_ACC], refs[N_ACC:]
    x_s, gy_s, ig_s, refs = *refs[:3], refs[3:]
    prep, tmp = refs[:N_PREP], refs[N_PREP:]
    image, row_block = pl.program_id(0), pl.program_id(1)
    first_step = (image == 0) & (row_block == 0)

    @pl.when(first_step)
    def _():
        for ref in acc:
            ref[...] = jnp.zeros_like(ref)
        ig_s[...] = jnp.zeros_like(ig_s)

    @pl.when(row_block == 0)
    def _():
        ch = x_ref.shape[1]
        x_s[:, :image_side] = x_ref[0].astype(f32).reshape(ch * own_rows, image_side)
        gy_s[:, :image_side] = gy_ref[0].astype(f32).reshape(ch * own_rows, image_side)

    start = row_block * WIN + SHIFT
    x_rows = natural_rows(x_s, image_side, own_rows, start, WIN)
    gy_rows = natural_rows(gy_s, image_side, own_rows, start - 1, WIN + 2)
    base_row = info[0] * own_rows + start
    ig = block_step(
        x_rows, gy_rows, first_step, False, base_row, info[2 + image], image_side, wts, prep, acc, tmp, c_out
    )
    for r in range(WIN):
        ig_s[pl.ds(start + r, ig_out.shape[1], stride=own_rows), :image_side] = jnp.transpose(ig[r])

    @pl.when(row_block == pl.num_programs(1) - 1)
    def _():
        ig_out[0] = ig_s[:, :image_side].reshape(ig_out.shape[1:])


def last_kernel(image_side, own_rows, info, x_ref, gy_ref, halo_ref, ig_ref, *refs):
    wts, refs = refs[:N_WTS], refs[N_WTS:]
    acc_in, refs = refs[:N_ACC], refs[N_ACC:]
    sr_ref, hr_ref, c_out, ig_out, ig_halo, pack_out, refs = *refs[:6], refs[6:]
    acc, refs = refs[:N_ACC], refs[N_ACC:]
    x_s, gy_s, ig_s, refs = *refs[:3], refs[3:]
    prep, tmp = refs[:N_PREP], refs[N_PREP:]
    image = pl.program_id(0)
    first_step = image == 0

    @pl.when(first_step)
    def _():
        for ref, given in zip(acc, acc_in):
            ref[...] = given[...]

    ch = x_ref.shape[1]
    x_s[:, :image_side] = x_ref[0].astype(f32).reshape(ch * WIN, image_side)
    gy_s[:, :image_side] = gy_ref[0].astype(f32).reshape(ch * WIN, image_side)

    def halo_rows(start, size):
        rows = [halo_ref[0, :, r * image_side : (r + 1) * image_side] for r in range(start, start + size)]
        return jnp.stack([jnp.transpose(row.astype(f32)) for row in rows])

    x_rows = jnp.concatenate(
        [natural_rows(x_s, image_side, WIN, SHIFT, SHIFT), halo_rows(0, SHIFT)], axis=0
    )
    gy_rows = jnp.concatenate(
        [natural_rows(gy_s, image_side, WIN, SHIFT - 1, SHIFT + 1), halo_rows(SHIFT, SHIFT + 1)], axis=0
    )
    base_row = info[0] * own_rows + own_rows - SHIFT
    ig = block_step(
        x_rows, gy_rows, first_step, info[1] == 1, base_row, info[2 + image], image_side, wts, prep, acc, tmp, c_out
    )
    ig_s[:, :image_side] = ig_ref[0].reshape(ch * WIN, image_side)
    for r in range(SHIFT):
        ig_s[pl.ds(SHIFT + r, ch, stride=WIN), :image_side] = jnp.transpose(ig[r])
    ig_out[0] = ig_s[:, :image_side].reshape(ch, WIN, image_side)
    ig_halo[0] = jnp.concatenate([jnp.transpose(ig[SHIFT + r]) for r in range(SHIFT)], axis=1).astype(bf16)

    @pl.when(image == pl.num_programs(0) - 1)
    def _():
        pack_gradients(info[2 + pl.num_programs(0)], acc, sr_ref, hr_ref, pack_out)


def pack_rows(ch):
    up = -(-ch // 8) * 8
    blocks = 17
    vec_at = (blocks + (blocks + 1) // 2) * up
    return up, blocks, vec_at, vec_at + 32, vec_at + 32 + 3 * TOK


def pack_gradients(device, acc, sr_ref, hr_ref, out):
    (acc_conv, acc_qkv, acc_proj, acc_fc1, acc_fc2, acc_ln, acc_rel) = acc
    ch = acc_fc2.shape[1]
    dim = ch // HEADS
    up, count, vec_at, rel_at, used = pack_rows(ch)
    rest = ch - LANE
    out[used:, :] = jnp.zeros((out.shape[0] - used, LANE), f32)
    out[rel_at:used, :] = acc_rel[...]
    blocks = [acc_conv[:ch, t * CPAD : t * CPAD + ch] for t in range(9)]
    qkv = [drop_lanes(acc_qkv[k], HEADS, dim) for k in range(3)]
    blocks += [qkv[k][:ch] for k in range(3)]
    blocks += [drop_rows(acc_proj[...], HEADS, dim)]
    fc1 = jnp.transpose(acc_fc1[...])
    fc2 = jnp.transpose(acc_fc2[...])
    blocks += [fc1[:ch, :ch], fc1[:ch, ch:]]
    blocks += [fc2[:, :ch], fc2[:, ch:]]
    out[:vec_at, :] = jnp.zeros((vec_at, LANE), f32)
    for k, block in enumerate(blocks):
        out[k * up : k * up + ch, :] = block[:, :LANE]
        at = (count + k // 2) * up
        half = (k % 2) * TOK
        out[at : at + ch, half : half + rest] = block[:, LANE:]
    ln = [jnp.sum(jnp.transpose(acc_ln[k]), axis=0, keepdims=True) for k in range(5)]
    vec = [
        ln[0],
        ln[1],
        qkv[0][ch : ch + 1, :],
        qkv[2][ch : ch + 1, :],
        acc_proj[dim : dim + 1, :],
        ln[2],
        ln[3],
        fc1[ch : ch + 1, :ch],
        fc1[ch : ch + 1, ch:],
        ln[4],
        acc_conv[ch : ch + 1, 4 * CPAD : 4 * CPAD + ch],
    ]
    vec = jnp.concatenate(vec, axis=0)
    diff = sr_ref[...] - hr_ref[...]
    luma = (65.481 * diff[:, 0] + 128.553 * diff[:, 1] + 24.966 * diff[:, 2]) / 255.0
    square = jnp.sum(luma * luma, axis=1, keepdims=True)
    mse = jnp.sum(square, axis=2, keepdims=True) * (1.0 / (luma.shape[1] * luma.shape[2]))
    psnr = jnp.sum(jnp.log(mse + 1e-06) * (-10.0 / 2.302585092994046), axis=0)
    out[vec_at : vec_at + 32, :] = jnp.zeros((32, LANE), f32)
    out[vec_at : vec_at + 11, :] = vec[:, :LANE]
    lane = lax.broadcasted_iota(jnp.int32, (1, LANE), 1)
    for k in range(3):
        piece = psnr.astype(bf16).astype(f32)
        out[vec_at + 11 + k : vec_at + 12 + k, :] = jnp.where(lane == device, piece, 0.0)
        psnr = psnr - piece
    out[vec_at + 16 : vec_at + 27, :rest] = vec[:, LANE:]


def whole(shape):
    return pl.BlockSpec(shape, lambda *_: (0,) * len(shape))


def acc_shapes(ch, hid):
    return [
        (CPAD, 9 * CPAD),
        (3, CPAD, CPAD),
        (CPAD, ch),
        (hid, CPAD),
        (hid, ch),
        (5, ch, LANE),
        (3 * TOK, LANE),
    ]


def scratches(ch, hid, px, vec_rows):
    v = pltpu.VMEM
    prep = [
        v((ch, vec_rows), f32),
        v((3 * CPAD, ch), bf16), v((ch, CPAD), bf16), v((hid, ch), bf16), v((ch, hid), bf16),
        v((ch, CPAD), bf16), v((ch, CPAD), bf16), v((ch, CPAD), bf16), v((CPAD, ch), bf16),
        v((ch, hid), bf16), v((hid, ch), bf16),
        v((ch, 9 * CPAD), bf16),
        v((TOK, LANE), f32),
        v((TOK, LANE), f32),
        v((hid, LANE), f32),
        v((10, ch, LANE), f32),
        v((2, CPAD, LANE), f32),
    ]
    wins = px // TOK
    tmp = [
        v((px, 9 * CPAD), bf16),
        v((CPAD, px), bf16), v((CPAD, px), bf16), v((CPAD, px), bf16), v((hid, px), bf16), v((CPAD, px), bf16),
        v((wins, CPAD, LANE), bf16),
        v((wins, 3 * TOK, LANE), f32),
        v((wins, 3 * TOK, LANE), bf16),
        v((2, px, CPAD), bf16),
        v((ch, px), f32),
        v((CPAD, px), bf16),
        v((CPAD, px), bf16),
        v((2, px, CPAD), bf16),
        v((ch, px), f32),
        v((ch, px), f32),
        v((hid, px), f32),
        v((CPAD, px), bf16),
        v((CPAD, px), bf16),
        v((CPAD, px), bf16),
        v((8, px), f32),
        v((ch, px), bf16),
        v((hid, px), bf16),
    ]
    return prep + tmp


def halo_kernel(halo_ref, ig_ref, ig_out, ig_s):
    _, ch, rows, image_side = ig_ref.shape
    ig_s[:, :image_side] = ig_ref[0].reshape(ch * rows, image_side)
    for r in range(SHIFT):
        row = halo_ref[0, :, r * image_side : (r + 1) * image_side]
        ig_s[pl.ds(r, ch, stride=rows), :image_side] = row.astype(f32)
    ig_out[0] = ig_s[:, :image_side].reshape(ch, rows, image_side)


def bits_of(size):
    return list(range(size.bit_length() - 1))


def exchange_plan(sizes):
    (dp_axis, dp_size), (head_axis, head_size) = sizes
    first = (dp_axis, 0)
    rest = [(dp_axis, b) for b in bits_of(dp_size)[1:]]
    last = [(head_axis, b) for b in bits_of(head_size)]
    half = len(rest) // 2
    return first, [rest + last, rest[half:] + rest[:half] + last]


def exchange_kernel(
    first, orders, head_size,
    g_in, c1_in, c2_in, x_in, ig_in, conv_in, vec_ref,
    sum_ref, out_ref, ig_out,
    g, work, given, low, short, given_short, c1, c2, c_halo, ig_mine, ig_given, x, conv, wc, cs, rows_s, out_s,
    send_sem, recv_sem, local_sem,
):
    count, ch, own_rows, image_side = x.shape
    rows = g.shape[0]
    mesh_id = pl.DeviceIdType.MESH
    here = lax.axis_index("head")
    upper = {"head": (here + 1) % head_size}
    lower = {"head": (here + head_size - 1) % head_size}

    def load(k, src, dst):
        copy = pltpu.make_async_copy(src, dst, local_sem.at[k])
        copy.start()
        return copy

    loads = [
        load(0, g_in, g),
        load(1, conv_in, conv),
        load(2, c1_in, c1),
        load(3, c2_in, c2),
        load(4, x_in, x),
        load(5, ig_in, ig_mine),
    ]

    def meet(stage):
        axis, b = stage
        me = lax.axis_index(axis)
        step = 2**b
        bit = (me // step) % 2
        return {axis: me + (1 - 2 * bit) * step}, bit

    barrier = pltpu.get_barrier_semaphore()
    friends = [meet(stage)[0] for stage in [first] + orders[0]] + [upper, lower]
    for other in friends:
        pl.semaphore_signal(barrier, inc=1, device_id=other, device_id_type=mesh_id)
    pl.semaphore_wait(barrier, len(friends))

    used = [0]

    def send(src, dst, other):
        k = used[0]
        used[0] += 1
        copy = pltpu.make_async_remote_copy(
            src_ref=src,
            dst_ref=dst,
            send_sem=send_sem.at[k],
            recv_sem=recv_sem.at[k],
            device_id=other,
            device_id_type=mesh_id,
        )
        copy.start()
        return copy

    def span(start, size):
        return pl.ds(pl.multiple_of(start, 16), size)

    col = lax.broadcasted_iota(jnp.int32, (1, image_side, ch), 1)
    top = jnp.where(here == 0, 0.0, 1.0).astype(f32)
    bottom = jnp.where(here == head_size - 1, 0.0, 1.0).astype(f32)

    def prepare():
        loads[1].wait()
        wc[...] = jnp.zeros_like(wc)
        cs[...] = jnp.zeros_like(cs)
        for tap in range(9):
            wc[tap * TAP : tap * TAP + ch, :] = conv[tap // 3, tap % 3].astype(bf16)

    def conv_rows(image, block):
        for k in range(WIN + 2):
            r = block * WIN + k - 1 - SHIFT
            if r < 0:
                row = c_halo[image, r + SHIFT + 1 : r + SHIFT + 2]
            elif r < c1.shape[1]:
                row = c1[image, r : r + 1]
            else:
                row = c2[image, r - c1.shape[1] : r - c1.shape[1] + 1]
            row = row.astype(f32)
            if block == 0 and k == 0:
                row = row * top
            if block == own_rows // WIN - 1 and k == WIN + 1:
                row = row * bottom
            left = jnp.where(col == 0, 0.0, roll_cols(row, -1))
            right = jnp.where(col == image_side - 1, 0.0, roll_cols(row, 1))
            at = slice(k * image_side, (k + 1) * image_side)
            cs[at, 0:ch] = left[0].astype(bf16)
            cs[at, TAP : TAP + ch] = row[0].astype(bf16)
            cs[at, 2 * TAP : 2 * TAP + ch] = right[0].astype(bf16)
        total = vec_ref[10:11, :]
        for i in range(3):
            at = slice(i * image_side, (i + WIN) * image_side)
            total = total + nn(cs[at, :], wc[i * 3 * TAP : (i + 1) * 3 * TAP, :])
        for k in range(WIN):
            rows_s[image, block * WIN + k] = jnp.transpose(total[k * image_side : (k + 1) * image_side])

    stores = []

    def finish(image):
        out_s[image] = (jnp.swapaxes(rows_s[image], 0, 1) + x[image].astype(f32)).astype(bf16)
        stores.append(load(6 + image, out_s.at[image], out_ref.at[image]))

    blocks = own_rows // WIN
    inner = [(n, b) for n in range(count) for b in range(1, blocks)]
    outer = [(n, 0) for n in range(count)]
    stage_count = 2 * (1 + len(orders[0]))
    jobs = [[] for _ in range(stage_count)]
    for k, job in enumerate(inner + outer):
        jobs[min(1 + k * (stage_count - 2) // len(inner + outer), stage_count - 2)].append(job)

    halos = []

    def work_on(stage):
        if stage == 0:
            prepare()
        if stage == 1:
            for k in (2, 4, 5):
                loads[k].wait()
        for image, block in jobs[stage]:
            if block == 0 and image == 0:
                halos[0].wait()
            conv_rows(image, block)
            if block == 0:
                finish(image)

    loads[0].wait()
    other, bit = meet(first)
    half = rows // 2
    copy = send(g.at[span((1 - bit) * half, half)], given.at[pl.ds(0, half)], other)
    loads[3].wait()
    halos.append(send(c2.at[:, WIN - SHIFT - 1 :], c_halo, upper))
    work_on(0)
    copy.wait()
    keep = bit * half
    work[span(keep, half), :] = g[span(keep, half), :] + given[:half, :]
    unit = 16 * 2 ** len(orders[0])
    parts = half // unit
    cut = (parts + 1) // 2 * unit
    begin = [keep, keep + cut]
    size = [cut, half - cut]
    taken = half
    link_stages = len([stage for stage in orders[0] if stage[0] == first[0]])
    trail = [[], []]
    for s in range(len(orders[0])):
        flying = []
        for p in range(2):
            if size[p] == 0:
                continue
            other, bit = meet(orders[p][s])
            size[p] //= 2
            trail[p].append(begin[p])
            give = begin[p] + (1 - bit) * size[p]
            begin[p] = begin[p] + bit * size[p]
            if s < link_stages:
                short[span(give, size[p]), :] = work[span(give, size[p]), :].astype(bf16)
                copy = send(short.at[span(give, size[p])], given_short.at[pl.ds(taken - half, size[p])], other)
            else:
                copy = send(work.at[span(give, size[p])], given.at[pl.ds(taken, size[p])], other)
            flying.append((p, taken, copy))
            taken += size[p]
        work_on(1 + s)
        for p, at, copy in flying:
            copy.wait()
            if s < link_stages:
                there = given_short[at - half : at - half + size[p], :].astype(f32)
            else:
                there = given[at : at + size[p], :]
            total = work[span(begin[p], size[p]), :] + there
            if s < len(orders[0]) - 1:
                work[span(begin[p], size[p]), :] = total
            else:
                low[span(begin[p], size[p]), :] = total.astype(bf16)

    for s in reversed(range(len(orders[0]))):
        flying = []
        for p in range(2):
            if size[p] == 0:
                continue
            if s == link_stages - 1 and p == 0:
                halos.append(send(ig_mine, ig_given, upper))
            other, _ = meet(orders[p][s])
            here_now = low.at[span(begin[p], size[p])]
            flying.append(send(here_now, here_now, other))
            begin[p] = trail[p][s]
            size[p] *= 2
        work_on(2 * len(orders[0]) - s)
        for copy in flying:
            copy.wait()
    other, _ = meet(first)
    here_now = low.at[span(keep, half)]
    copy = send(here_now, here_now, other)
    work_on(stage_count - 1)
    copy.wait()
    sum_ref[...] = low[...]
    halos[1].wait()
    stores.append(load(6 + count, ig_given, ig_out))
    for copy in stores:
        copy.wait()


def exchange(packed, c1, c2, images, ig_halo, conv_weight, vectors, sizes):
    first, orders = exchange_plan(sizes)
    rows = packed.shape[0]
    count, ch, own_rows, image_side = images.shape
    vmem = pl.BlockSpec(memory_space=pltpu.VMEM)
    hbm = pl.BlockSpec(memory_space=pl.ANY)
    v = pltpu.VMEM
    sends = 2 + 2 + 4 * len(orders[0])
    return pl.pallas_call(
        functools.partial(exchange_kernel, first, orders, sizes[1][1]),
        in_specs=[hbm] * 6 + [vmem],
        out_specs=[vmem, hbm, hbm],
        out_shape=[
            jax.ShapeDtypeStruct(packed.shape, bf16),
            jax.ShapeDtypeStruct(images.shape, bf16),
            jax.ShapeDtypeStruct(ig_halo.shape, bf16),
        ],
        scratch_shapes=[
            v(packed.shape, f32),
            v(packed.shape, f32),
            v(packed.shape, f32),
            v(packed.shape, bf16),
            v(packed.shape, bf16),
            v((rows // 2, LANE), bf16),
            v(c1.shape, bf16),
            v(c2.shape, bf16),
            v((count, SHIFT + 1, image_side, ch), bf16),
            v(ig_halo.shape, bf16),
            v(ig_halo.shape, bf16),
            v(images.shape, bf16),
            v(conv_weight.shape, f32),
            v((9 * TAP, ch), bf16),
            v(((WIN + 2) * image_side, 3 * TAP), bf16),
            v((count, own_rows, ch, image_side), f32),
            v(images.shape, bf16),
            pltpu.SemaphoreType.DMA((sends,)),
            pltpu.SemaphoreType.DMA((sends,)),
            pltpu.SemaphoreType.DMA((7 + count,)),
        ],
        compiler_params=pltpu.CompilerParams(
            collective_id=0, has_side_effects=True, vmem_limit_bytes=46 * 1024 * 1024
        ),
        name="sum_gradients",
    )(packed, c1, c2, images, ig_halo, conv_weight, vectors)


def adam_kernel(scal, g_ref, *refs):
    given, refs = refs[:21], refs[21:]
    norm_ref, psnr_ref, results, refs = refs[0], refs[1], refs[2:23], refs[23:]
    held, made, in_sem, out_sem = refs[:21], refs[21:42], refs[42], refs[43]
    order = [6, 1, 4, 5, 2, 0, 3]
    loads = {}
    for k in order:
        for part in range(3):
            n = 3 * k + part
            loads[n] = pltpu.make_async_copy(given[n], held[n], in_sem.at[n])
            loads[n].start()
    stores = []

    def arrived(k):
        for part in range(3):
            loads[3 * k + part].wait()
        return [held[3 * k + part] for part in range(3)]

    def leave(k):
        for part in range(3):
            n = 3 * k + part
            stores.append(pltpu.make_async_copy(made[n], results[n], out_sem.at[n]))
            stores[-1].start()

    weights = held[0::3]
    ch = weights[2].shape[0]
    up, count, vec_at, rel_at, used = pack_rows(ch)
    rest = ch - LANE

    def block(k):
        left = g_ref[k * up : (k + 1) * up, :].astype(f32)
        at = (count + k // 2) * up
        right = g_ref[at : at + up, :].astype(f32)
        if k % 2:
            right = pltpu.roll(right, TOK, 1)
        return jnp.concatenate([left, right[:, :rest]], axis=1)[:ch]

    vec_rows = g_ref[vec_at : vec_at + 32, :].astype(f32)
    vec = jnp.concatenate([vec_rows[:11], vec_rows[16:27, :rest]], axis=1)
    psnr = vec_rows[11:12] + vec_rows[12:13] + vec_rows[13:14]
    psnr_ref[...] = jnp.sum(psnr, axis=1, keepdims=True)

    span = 2 * WIN
    wide = span * span
    at = lax.broadcasted_iota(jnp.int32, (TOK, wide), 0)
    to = lax.broadcasted_iota(jnp.int32, (TOK, wide), 1)
    place = ((at >> 3) + (WIN - 1)) * span + (at & 7) + (WIN - 1)
    expand = (to == place).astype(f32).astype(bf16)
    pairs = g_ref[rel_at:used, :]
    rel_rows = []
    for p in range(3):
        for parity in range(2):
            part = pairs[p * TOK : (p + 1) * TOK, :].astype(f32)
            if parity:
                part = pltpu.roll(part, TOK, 1)
            spread = nn(part[:, :TOK].astype(bf16), expand)
            total = jnp.zeros((WIN, wide), f32)
            for row in range(WIN):
                piece = spread[row * WIN : (row + 1) * WIN]
                piece = pltpu.roll(piece, (wide - span * row) % wide, 1)
                total = total + piece
            line = total[0:1]
            for c in range(1, WIN):
                line = line + pltpu.roll(total, wide - c, 1)[c : c + 1]
            rel_rows.append(line)
    rel = jnp.concatenate(rel_rows, axis=0)
    rel = jnp.concatenate(
        [rel[:, k * span : k * span + span - 1] for k in range(span - 1)], axis=1
    )
    qkv = jnp.concatenate([block(9), block(10), block(11)], axis=1)
    fc1 = jnp.concatenate([block(13), block(14)], axis=1)
    fc2 = jnp.concatenate([block(15), block(16)], axis=1)
    small = [vec, qkv, block(12), rel, fc1, fc2]
    taps = [block(t) for t in range(9)]
    total = jnp.zeros((1, 1), f32)
    for g in small + taps:
        total = total + jnp.sum(jnp.sum(g * g, axis=0, keepdims=True), axis=1, keepdims=True)
    norm = jnp.sqrt(total)
    norm_ref[...] = norm
    clip = jnp.minimum(1.0, max_norm / (norm + 1e-06))
    fix_one, fix_two = scal[0], scal[1]

    def update(w, m1, m2, g, rate):
        g = g * clip
        m1 = beta_one * m1 + (1.0 - beta_one) * g
        m2 = beta_two * m2 + (1.0 - beta_two) * g * g
        step = (m1 / fix_one) / (jnp.sqrt(m2 / fix_two) + adam_eps)
        return w - rate * (step + decay_rate * w), m1, m2

    for k in order:
        w, m1, m2 = arrived(k)
        if k == 6:
            for t, g in enumerate(taps):
                at = (t // 3, t % 3)
                for ref, value in zip(made[18:21], update(w[at], m1[at], m2[at], g, learn_rate)):
                    ref[at] = value
        else:
            new = update(w[...], m1[...], m2[...], small[k], vector_rate if k == 0 else learn_rate)
            for ref, value in zip(made[3 * k : 3 * k + 3], new):
                ref[...] = value
        leave(k)
    for copy in stores:
        copy.wait()


def relative_onehot_keys_first():
    position = np.arange(TOK)
    pos_row, pos_col = position // WIN, position % WIN
    span = 2 * WIN - 1
    index = (pos_row[None, :] - pos_row[:, None] + WIN - 1) * span + (
        pos_col[None, :] - pos_col[:, None] + WIN - 1
    )
    return index.reshape(-1), span * span


def on_device(
    images, cotangent, valid_size,
    vectors, vectors_first, vectors_second,
    qkv_weight, qkv_first, qkv_second,
    proj_weight, proj_first, proj_second,
    rel_table, rel_first, rel_second,
    fc1_weight, fc1_first, fc1_second,
    fc2_weight, fc2_first, fc2_second,
    conv_weight, conv_first, conv_second,
    step, sr_crops, hr_crops, psnr_running,
):
    count, own_rows, image_side, ch = images.shape
    out_shape = (count, ch, own_rows, image_side)
    hid = fc1_weight.shape[1]
    px = image_side * WIN
    blocks = own_rows // WIN
    heads = lax.axis_size("head")
    place = lax.axis_index("head")
    to_lower = [((i + 1) % heads, i) for i in range(heads)]
    info = jnp.concatenate(
        [
            jnp.stack([place, (place == heads - 1).astype(jnp.int32)]).astype(jnp.int32),
            valid_size.astype(jnp.int32),
            ((lax.axis_index("dp") * heads + place) % LANE)[None].astype(jnp.int32),
        ]
    )
    images = images.transpose(0, 3, 1, 2)
    cotangent = cotangent.transpose(0, 3, 1, 2)
    top_rows = pl.BlockSpec((1, ch, WIN, image_side), lambda n: (n, 0, 0, 0))
    edge = pl.pallas_call(
        edge_kernel,
        grid=(count,),
        in_specs=[top_rows, top_rows],
        out_specs=pl.BlockSpec((1, ch, (2 * SHIFT + 1) * image_side), lambda n: (n, 0, 0)),
        out_shape=jax.ShapeDtypeStruct((count, ch, (2 * SHIFT + 1) * image_side), bf16),
        scratch_shapes=[pltpu.VMEM((ch * WIN, LANE), f32)] * 2,
        name="edge_rows",
    )(images, cotangent)
    halo = lax.ppermute(edge, "head", to_lower)

    index, span = relative_onehot_keys_first()
    onehot = (jnp.asarray(index)[:, None] == jnp.arange(span)[None, :]).astype(f32)
    bias = jnp.dot(onehot, rel_table, precision=highest)
    bias = bias.reshape(TOK, TOK, 3, 2).transpose(2, 0, 3, 1).reshape(3, TOK, LANE)

    wts = (vectors, qkv_weight, proj_weight, fc1_weight, fc2_weight.T, conv_weight, bias)
    wts_specs = [whole(w.shape) for w in wts]
    acc_dims = acc_shapes(ch, hid)
    acc_types = [jax.ShapeDtypeStruct(s, f32) for s in acc_dims]
    smem = pl.BlockSpec(memory_space=pltpu.SMEM)
    params = pltpu.CompilerParams(
        dimension_semantics=("arbitrary", "arbitrary"), vmem_limit_bytes=46 * 1024 * 1024
    )
    view = lambda rows, at, dims: pl.BlockSpec((1, ch, rows, image_side), lambda n, *_: (n, 0, at, 0))
    c_block = lambda size: pl.BlockSpec((1, size, image_side, ch), lambda n, *_: (n, 0, 0, 0))
    row_view = pltpu.VMEM((ch * own_rows, LANE), f32)
    c1, ig, *acc = pl.pallas_call(
        functools.partial(inner_kernel, image_side, own_rows),
        grid=(count, blocks - 1),
        in_specs=[smem, view(own_rows, 0, 2), view(own_rows, 0, 2), *wts_specs],
        out_specs=[
            pl.BlockSpec((1, WIN, image_side, ch), lambda n, r: (n, r, 0, 0)),
            view(own_rows, 0, 2),
            *[whole(s) for s in acc_dims],
        ],
        out_shape=[
            jax.ShapeDtypeStruct((count, own_rows - WIN, image_side, ch), bf16),
            jax.ShapeDtypeStruct(out_shape, f32),
            *acc_types,
        ],
        scratch_shapes=[row_view] * 3 + scratches(ch, hid, px, vectors.shape[0]),
        compiler_params=params,
        name="inner_windows",
    )(info, images, cotangent, *wts)
    device_count = lax.axis_size("dp") * heads
    unit = 16 * device_count
    rows = -(-pack_rows(ch)[-1] // unit) * unit
    c2, ig, ig_halo, packed = pl.pallas_call(
        functools.partial(last_kernel, image_side, own_rows),
        grid=(count,),
        in_specs=[
            smem,
            view(WIN, blocks - 1, 1),
            view(WIN, blocks - 1, 1),
            pl.BlockSpec((1, ch, halo.shape[2]), lambda n: (n, 0, 0)),
            view(WIN, blocks - 1, 1),
            *wts_specs,
            *[whole(s) for s in acc_dims],
            whole(sr_crops.shape),
            whole(hr_crops.shape),
        ],
        out_specs=[
            c_block(WIN),
            view(WIN, blocks - 1, 1),
            pl.BlockSpec((1, ch, SHIFT * image_side), lambda n: (n, 0, 0)),
            whole((rows, LANE)),
        ],
        out_shape=[
            jax.ShapeDtypeStruct((count, WIN, image_side, ch), bf16),
            jax.ShapeDtypeStruct(out_shape, f32),
            jax.ShapeDtypeStruct((count, ch, SHIFT * image_side), bf16),
            jax.ShapeDtypeStruct((rows, LANE), f32),
        ],
        input_output_aliases={4: 1},
        scratch_shapes=[pltpu.VMEM(s, f32) for s in acc_dims]
        + [pltpu.VMEM((ch * k, LANE), f32) for k in (WIN, WIN, WIN)]
        + scratches(ch, hid, px, vectors.shape[0]),
        compiler_params=pltpu.CompilerParams(
            dimension_semantics=("arbitrary",), vmem_limit_bytes=46 * 1024 * 1024
        ),
        name="last_windows",
    )(info, images, cotangent, halo, ig, *wts, *acc, sr_crops, hr_crops)

    summed, output, ig_halo = exchange(
        packed, c1, c2, images, ig_halo, conv_weight, vectors, (("dp", lax.axis_size("dp")), ("head", heads))
    )
    image_grad = pl.pallas_call(
        halo_kernel,
        grid=(count,),
        in_specs=[pl.BlockSpec((1, ch, SHIFT * image_side), lambda n: (n, 0, 0)), view(WIN, 0, 1)],
        out_specs=view(WIN, 0, 1),
        scratch_shapes=[pltpu.VMEM((ch * WIN, LANE), f32)],
        out_shape=jax.ShapeDtypeStruct(out_shape, f32),
        input_output_aliases={1: 0},
        name="halo_rows",
    )(ig_halo, ig)
    output, image_grad = output.transpose(0, 2, 3, 1), image_grad.transpose(0, 2, 3, 1)

    step_count = step[0].astype(f32)
    scal = jnp.stack([1.0 - beta_one**step_count, 1.0 - beta_two**step_count])
    weights = (vectors, qkv_weight, proj_weight, rel_table.T, fc1_weight, fc2_weight.T, conv_weight)
    firsts = (vectors_first, qkv_first, proj_first, rel_first.T, fc1_first, fc2_first.T, conv_first)
    seconds = (vectors_second, qkv_second, proj_second, rel_second.T, fc1_second, fc2_second.T, conv_second)
    vmem = pl.BlockSpec(memory_space=pltpu.VMEM)
    hbm = pl.BlockSpec(memory_space=pl.ANY)
    state = [array for group in zip(weights, firsts, seconds) for array in group]
    grad_norm, psnr, *updated = pl.pallas_call(
        adam_kernel,
        in_specs=[smem, vmem] + [hbm] * 21,
        out_specs=[vmem] * 2 + [hbm] * 21,
        out_shape=[jax.ShapeDtypeStruct((1, 1), f32)] * 2
        + [jax.ShapeDtypeStruct(array.shape, f32) for array in state],
        scratch_shapes=[pltpu.VMEM(array.shape, f32) for array in state * 2]
        + [pltpu.SemaphoreType.DMA((21,)), pltpu.SemaphoreType.DMA((21,))],
        compiler_params=pltpu.CompilerParams(vmem_limit_bytes=60 * 1024 * 1024),
        name="adam",
    )(scal, summed, *state)
    for k in (9, 10, 11, 15, 16, 17):
        updated[k] = updated[k].T
    psnr_total = psnr_running + psnr.reshape(1)
    return (output, image_grad, grad_norm.reshape(1), psnr_total, *updated)


def solution(mesh):
    pixels = P("dp", "head", None, None)
    crops = P(("dp", "head"), None, None, None)
    placed = (pixels, pixels, P("dp")) + (P(),) * 22 + (crops, crops, P())
    return jax.shard_map(
        on_device,
        mesh=mesh,
        in_specs=placed,
        out_specs=(pixels, pixels) + (P(),) * 23,
        check_vma=False,
    )
```
